32 devices in a mesh: dp: 4 (over z), fsdp: 8 (over y, x, core).
Axes of the slice: x: 2, y: 2, z: 4, core: 2. Of those that a mesh axis runs over, the one named last changes fastest.
Arguments:
- inputs: bfloat16 [32, 1024, 1024], P(('dp', 'fsdp')), may hold values from -6 to 6
- memory: bfloat16 [32, 512, 1024], P(('dp', 'fsdp')), may hold values from -6 to 6
- cotangent: bfloat16 [32, 1024, 1024], P(('dp', 'fsdp')), may hold values from -6 to 6
- target_lengths: int32 [32], P(('dp', 'fsdp')), may hold values from 1 to 1024, as said below
- memory_lengths: int32 [32], P(('dp', 'fsdp')), may hold values from 128 to 512, as said below
- norm_gains: bfloat16 [3, 1024], P(None, ('dp', 'fsdp')), may hold values from 0.5 to 1.5
- norm_biases: bfloat16 [3, 1024], P(None, ('dp', 'fsdp')), may hold values from -4 to 4
- self_qkv: bfloat16 [1024, 3072], P(('dp', 'fsdp')), may hold values from -0.1875 to 0.1875
- self_out: bfloat16 [1024, 1024], P(('dp', 'fsdp')), may hold values from -0.5 to 0.5
- cross_query: bfloat16 [1024, 1024], P(('dp', 'fsdp')), may hold values from -0.1875 to 0.1875
- cross_kv: bfloat16 [1024, 2048], P(('dp', 'fsdp')), may hold values from -0.1875 to 0.1875
- cross_out: bfloat16 [1024, 1024], P(('dp', 'fsdp')), may hold values from -0.5 to 0.5
- ffn_in: bfloat16 [1024, 4096], P(('dp', 'fsdp')), may hold values from -0.1875 to 0.1875
- ffn_out: bfloat16 [4096, 1024], P(('dp', 'fsdp')), may hold values from -0.09375 to 0.09375
- proj_biases: bfloat16 [7, 1024], P(None, ('dp', 'fsdp')), may hold values from -4 to 4
- ffn_in_bias: bfloat16 [4096], P(('dp', 'fsdp')), may hold values from -4 to 4
Outputs:
- layer_output: bfloat16 [32, 1024, 1024], P(('dp', 'fsdp'))
- input_grad: float32 [32, 1024, 1024], P(('dp', 'fsdp'))
- memory_grad: float32 [32, 512, 1024], P(('dp', 'fsdp'))
- norm_gains_grad: float32 [3, 1024], P(None, ('dp', 'fsdp'))
- norm_biases_grad: float32 [3, 1024], P(None, ('dp', 'fsdp'))
- self_qkv_grad: float32 [1024, 3072], P(('dp', 'fsdp'))
- self_out_grad: float32 [1024, 1024], P(('dp', 'fsdp'))
- cross_query_grad: float32 [1024, 1024], P(('dp', 'fsdp'))
- cross_kv_grad: float32 [1024, 2048], P(('dp', 'fsdp'))
- cross_out_grad: float32 [1024, 1024], P(('dp', 'fsdp'))
- ffn_in_grad: float32 [1024, 4096], P(('dp', 'fsdp'))
- ffn_out_grad: float32 [4096, 1024], P(('dp', 'fsdp'))
- proj_biases_grad: float32 [7, 1024], P(None, ('dp', 'fsdp'))
- ffn_in_bias_grad: float32 [4096], P(('dp', 'fsdp'))
The draws below stay inside these ranges and needn't reach their ends.
Inputs may be any that keep to these rules, and one draw needn't show every extreme that they name: `target_lengths`: at least one row has all 1024 positions live. `memory_lengths`: at least one row has all 512 memory positions live.
All inputs are finite; a program needn't handle non-finite values.
Results may differ from the reference program's by a relative error of at most 0.017.
Values may be sent and summed in bfloat16 or wider, within the bound.
No kernel may reach another device: no remote copies, remote signals or barrier semaphores. Data moves between devices by JAX's collectives and lax.ppermute only.
A program may use at most 448 MiB of HBM per device.

```python
import jax
import jax.numpy as jnp
from jax import lax

D = 1024
FF = 4096
HEAD = 64
SEQ = 1024
MEM = 512
ROWS = 32


def draw_target_lengths(key, part):
    key = jax.random.fold_in(key, 11)
    picker, longer, shorter, chosen = jax.random.split(key, 4)
    category = jax.random.randint(picker, (ROWS,), 0, 4)
    long_lengths = jax.random.randint(longer, (ROWS,), SEQ // 2, SEQ + 1)
    short_lengths = jax.random.randint(shorter, (ROWS,), 1, max(SEQ // 8, 2) + 1)
    lengths_drawn = jnp.where(category > 0, long_lengths, short_lengths)
    forced = jax.random.randint(chosen, (), 0, ROWS)
    return jnp.where(jnp.arange(ROWS) == forced, SEQ, lengths_drawn).astype(jnp.int32)


def draw_memory_lengths(key, part):
    key = jax.random.fold_in(key, 23)
    spread_key, chosen = jax.random.split(key, 2)
    lengths_drawn = jax.random.randint(spread_key, (ROWS,), MEM // 4, MEM + 1)
    forced = jax.random.randint(chosen, (), 0, ROWS)
    return jnp.where(jnp.arange(ROWS) == forced, MEM, lengths_drawn).astype(jnp.int32)


def level_of(rng, dims, cuts, least, high):
    def one(axis_at, shards_of):
        steps = jax.random.uniform(jax.random.fold_in(jax.random.fold_in(rng, 6), axis_at), (shards_of,), jnp.float32, least / len(cuts), high / len(cuts))
        return jnp.repeat(jnp.exp(steps), dims[axis_at] // shards_of).reshape((-1,) + (1,) * (len(dims) - axis_at - 1))

    loudness = one(*cuts[0])
    for cut in cuts[1:]:
        loudness = loudness * one(*cut)
    return loudness


def scatter_about(rng, shape, scale, most, pieces=(), held_as=jnp.bfloat16):
    drawn = scale * jax.random.normal(rng, shape, jnp.float32)
    if pieces:
        drawn = drawn * level_of(rng, shape, pieces, -0.22, 0.18)
    return jnp.clip(drawn, -most, most).astype(held_as)


def setup_inputs(seed: int = 0) -> dict:
    seeds = jax.random.split(jax.random.key(seed), 17)
    return {
        "inputs": scatter_about(seeds[0], (ROWS, SEQ, D), 1.0, 6.0, ((0, 32),)),
        "memory": scatter_about(seeds[1], (ROWS, MEM, D), 1.0, 6.0, ((0, 32),)),
        "cotangent": scatter_about(seeds[2], (ROWS, SEQ, D), 1.0, 6.0, ((0, 32),)),
        "target_lengths": draw_target_lengths(jax.random.fold_in(seeds[16], 71), 0),
        "memory_lengths": draw_memory_lengths(jax.random.fold_in(seeds[16], 71), 0),
        "norm_gains": jnp.clip(1.0 + 0.1 * jax.random.normal(seeds[5], (3, D), jnp.float32), 0.5, 1.5).astype(jnp.bfloat16),
        "norm_biases": scatter_about(seeds[6], (3, D), 0.3, 4.0, ((1, 32),)),
        "self_qkv": scatter_about(seeds[7], (D, 3 * D), D ** -0.5, 0.1875, ((0, 32),)),
        "self_out": scatter_about(seeds[8], (D, D), (D // 8) ** -0.5, 0.5, ((0, 32),)),
        "cross_query": scatter_about(seeds[9], (D, D), D ** -0.5, 0.1875, ((0, 32),)),
        "cross_kv": scatter_about(seeds[10], (D, 2 * D), D ** -0.5, 0.1875, ((0, 32),)),
        "cross_out": scatter_about(seeds[11], (D, D), (D // 8) ** -0.5, 0.5, ((0, 32),)),
        "ffn_in": scatter_about(seeds[12], (D, FF), D ** -0.5, 0.1875, ((0, 32),)),
        "ffn_out": scatter_about(seeds[13], (FF, D), FF ** -0.5, 0.09375, ((0, 32),)),
        "proj_biases": scatter_about(seeds[14], (7, D), 0.3, 4.0, ((1, 32),)),
        "ffn_in_bias": scatter_about(seeds[15], (FF,), 0.3, 4.0, ((0, 32),)),
    }


highest = lax.Precision.HIGHEST
eps_norm = 1e-05
masked_score = -1e+30

@jax.custom_vjp
def low(v):
    return lax.optimization_barrier(v.astype(jnp.bfloat16)).astype(jnp.float32)

@jax.custom_vjp
def low_back(v):
    return v

def low_keep(v):
    return (low(v), None)

def low_pass(kept, grad):
    return (grad,)

def back_keep(v):
    return (v, None)

def back_low(kept, grad):
    return (low(grad),)
low.defvjp(low_keep, low_pass)
low_back.defvjp(back_keep, back_low)

def matmul(left, right):
    return jnp.dot(left, right, preferred_element_type=jnp.float32, precision=highest)

def layer_norm(hidden, gain, shift):
    centred = hidden - lax.optimization_barrier(jnp.mean(hidden, axis=-1, keepdims=True))
    spread = lax.optimization_barrier(jnp.mean(centred * centred, axis=-1, keepdims=True))
    return centred * lax.rsqrt(spread + eps_norm) * gain + shift

def attention(queries, key_tokens, value_tokens, allowed_fn):
    length = queries.shape[0]
    block_rows = min(512, length)
    head_count = queries.shape[1] // HEAD
    key_heads = key_tokens.reshape(key_tokens.shape[0], head_count, HEAD)
    value_heads = value_tokens.reshape(value_tokens.shape[0], head_count, HEAD)

    def one_block(offset):
        query_heads = lax.dynamic_slice_in_dim(queries, offset, block_rows, 0).reshape(block_rows, head_count, HEAD)
        scores = jnp.einsum('qhd,khd->hqk', query_heads, key_heads, precision=highest) * HEAD ** (-0.5)
        scores = low_back(jnp.where(allowed_fn(offset, block_rows)[None], scores, masked_score))
        largest = lax.optimization_barrier(jnp.max(scores, axis=-1, keepdims=True))
        exponent = jnp.exp(scores - largest)
        probability = low(exponent / lax.optimization_barrier(jnp.sum(exponent, axis=-1, keepdims=True)))
        blended = jnp.einsum('hqk,khd->qhd', probability, value_heads, precision=highest)
        return blended.reshape(block_rows, head_count * HEAD)
    starts = (jnp.arange(length // block_rows) * block_rows).astype(jnp.int32)
    return lax.map(jax.checkpoint(one_block), starts).reshape(length, head_count * HEAD)

def decoder_row(hidden, memory_rows, target_length, memory_length, weights):
    gains, shifts, triple_weight, self_weight, query_weight, pair_weight, cross_weight, inner_weight, outer_weight, biases, inner_bias = weights
    sequence = hidden.shape[0]
    memory_size = memory_rows.shape[0]
    width = hidden.shape[1]
    positions = jnp.arange(sequence).astype(jnp.int32)
    memory_positions = jnp.arange(memory_size).astype(jnp.int32)

    def self_allowed(offset, block_rows):
        query_pos = offset + jnp.arange(block_rows).astype(jnp.int32)
        return (positions[None, :] <= query_pos[:, None]) & (positions[None, :] < target_length)

    def cross_allowed(offset, block_rows):
        return jnp.broadcast_to(memory_positions[None, :] < memory_length, (block_rows, memory_size))
    zero_bias = jnp.zeros_like(biases[0])
    normed = low(layer_norm(hidden, gains[0], shifts[0]))
    triple = low(low_back(matmul(normed, triple_weight) + jnp.concatenate([biases[0], zero_bias, biases[1]])))
    blended = low(low_back(attention(triple[:, :width], triple[:, width:2 * width], triple[:, 2 * width:], self_allowed)))
    hidden = hidden + low_back(matmul(blended, self_weight) + biases[2])
    normed = low(layer_norm(hidden, gains[1], shifts[1]))
    cross_queries = low(low_back(matmul(normed, query_weight) + biases[3]))
    paired = low(low_back(matmul(memory_rows, pair_weight) + jnp.concatenate([zero_bias, biases[4]])))
    blended = low(low_back(attention(cross_queries, paired[:, :width], paired[:, width:], cross_allowed)))
    hidden = hidden + low_back(matmul(blended, cross_weight) + biases[5])
    normed = low(layer_norm(hidden, gains[2], shifts[2]))
    inner = low_back(matmul(normed, inner_weight) + inner_bias)
    active = low(jax.nn.gelu(inner))
    return hidden + low_back(matmul(active, outer_weight) + biases[6])

def reference(inputs, memory, cotangent, target_lengths, memory_lengths, norm_gains, norm_biases, self_qkv, self_out, cross_query, cross_kv, cross_out, ffn_in, ffn_out, proj_biases, ffn_in_bias):
    weights = tuple((parameter.astype(jnp.float32) for parameter in (norm_gains, norm_biases, self_qkv, self_out, cross_query, cross_kv, cross_out, ffn_in, ffn_out, proj_biases, ffn_in_bias)))

    def forward(hidden_all, memory_all, weight_set):

        def advance(carry, sample):
            hidden, memory_rows, target_length, memory_length = sample
            return (carry, decoder_row(hidden, memory_rows, target_length, memory_length, weight_set))
        unused, outputs = lax.scan(advance, jnp.zeros((), jnp.float32), (hidden_all, memory_all, target_lengths, memory_lengths))
        return outputs
    outputs, pullback = jax.vjp(forward, inputs.astype(jnp.float32), memory.astype(jnp.float32), weights)
    input_grad, memory_grad, weight_grads = pullback(cotangent.astype(jnp.float32))
    gains_grad, shifts_grad, triple_grad, self_grad, query_grad, pair_grad, cross_grad, inner_grad, outer_grad, biases_grad, inner_bias_grad = weight_grads
    return (outputs.astype(jnp.bfloat16), input_grad, memory_grad, gains_grad, shifts_grad, triple_grad, self_grad, query_grad, pair_grad, cross_grad, inner_grad, outer_grad, biases_grad, inner_bias_grad)
```

```python
import functools

import jax
import jax.numpy as jnp
from jax import lax
from jax.experimental import pallas as pl
from jax.experimental.pallas import tpu as pltpu
from jax.sharding import PartitionSpec as P

f32 = jnp.float32
bf16 = jnp.bfloat16

HEAD = 64
PAIR = 2 * HEAD
BLOCK = 256
ROWS = 256
SMALL = 128
eps_norm = 1e-05
masked_score = -1e30
gelu_slope = 0.7978845608028654
gelu_cubic = 0.044715
MiB = 1 << 20


def nn(left, right):
    return jnp.dot(left, right, preferred_element_type=f32)


def nt(left, right):
    return lax.dot_general(left, right, (((1,), (1,)), ((), ())), preferred_element_type=f32)


def tn(left, right):
    return lax.dot_general(left, right, (((0,), (0,)), ((), ())), preferred_element_type=f32)


def normalise(hidden):
    centred = hidden - jnp.mean(hidden, axis=-1, keepdims=True)
    spread = lax.rsqrt(jnp.mean(centred * centred, axis=-1, keepdims=True) + eps_norm)
    return centred * spread, spread


def norm_back(hidden, incoming, gain):
    normed, spread = normalise(hidden)
    scaled = incoming * gain
    part = spread * (
        scaled
        - jnp.mean(scaled, axis=-1, keepdims=True)
        - normed * jnp.mean(scaled * normed, axis=-1, keepdims=True)
    )
    gain_grad = jnp.sum(incoming * normed, axis=0, keepdims=True)
    shift_grad = jnp.sum(incoming, axis=0, keepdims=True)
    return part, gain_grad, shift_grad


def column_sum(gradient):
    return jnp.sum(gradient.astype(f32), axis=0, keepdims=True)


def params():
    return pltpu.CompilerParams(vmem_limit_bytes=60 * MiB)


def after(waits, kernel, in_specs):
    count = len(waits)

    def waiting(*refs):
        kernel(*refs[count:])

    return waiting, [pl.BlockSpec(memory_space=pl.ANY)] * count + in_specs


def cost(flops, nbytes, transcendentals=0, high=64):
    return pl.CostEstimate(
        flops=high * flops, bytes_accessed=high * nbytes, transcendentals=high * transcendentals
    )


def held(shape, at=None):
    place = (0,) * len(shape) if at is None else at
    return pl.BlockSpec(shape, lambda j: place, pipeline_mode=pl.Buffered(1))


def by_rows(shape):
    return pl.BlockSpec(shape, lambda j: (j, 0))


def out(shape, dtype):
    return jax.ShapeDtypeStruct(shape, dtype)


GAIN, SHIFT, BIAS, HIDDEN_BIAS = 0, 3, 6, 13


def row_of(table_ref, at):
    return table_ref[at : at + 1, :]


def entry_kernel(x_ref, weight_ref, table_ref, normed_ref, triple_ref):
    width = x_ref.shape[1]
    normed, _ = normalise(x_ref[...].astype(f32))
    low = (normed * row_of(table_ref, GAIN) + row_of(table_ref, SHIFT)).astype(bf16)
    normed_ref[...] = low
    for part in range(3):
        span = slice(part * width, (part + 1) * width)
        made = nn(low, weight_ref[:, span])
        if part == 0:
            made = made + row_of(table_ref, BIAS)
        if part == 2:
            made = made + row_of(table_ref, BIAS + 1)
        triple_ref[:, span] = made.astype(bf16)


def entry(x, weights, table, waits=()):
    tokens, width = x.shape
    kernel, in_specs = after(
        waits, entry_kernel, [by_rows((ROWS, width)), held(weights.shape), held(table.shape)]
    )
    return pl.pallas_call(
        kernel,
        grid=(tokens // ROWS,),
        in_specs=in_specs,
        out_specs=[by_rows((ROWS, width)), by_rows((ROWS, 3 * width))],
        out_shape=[out((tokens, width), bf16), out((tokens, 3 * width), bf16)],
        compiler_params=params(),
        cost_estimate=cost(6 * tokens * width * width, 10 * tokens * width + 6 * width * width),
        name="norm_and_qkv",
    )(*waits, x, weights, table)


def middle_kernel(x_ref, mixed_ref, out_ref, query_ref, table_ref, hidden_ref, normed_ref, made_ref):
    hidden = x_ref[...].astype(f32) + nn(mixed_ref[...], out_ref[...]) + row_of(table_ref, BIAS + 2)
    hidden_ref[...] = hidden
    normed, _ = normalise(hidden)
    low = (normed * row_of(table_ref, GAIN + 1) + row_of(table_ref, SHIFT + 1)).astype(bf16)
    normed_ref[...] = low
    made_ref[...] = (nn(low, query_ref[...]) + row_of(table_ref, BIAS + 3)).astype(bf16)


def middle(x, mixed, weights, table):
    tokens, width = x.shape
    block = by_rows((ROWS, width))
    return pl.pallas_call(
        middle_kernel,
        grid=(tokens // ROWS,),
        in_specs=[
            block,
            block,
            held((width, width), (0, 0)),
            held((width, width), (0, 1)),
            held(table.shape),
        ],
        out_specs=[block, block, block],
        out_shape=[out((tokens, width), f32), out((tokens, width), bf16), out((tokens, width), bf16)],
        compiler_params=params(),
        cost_estimate=cost(4 * tokens * width * width, 12 * tokens * width + 4 * width * width),
        name="self_out_norm_query",
    )(x, mixed, weights, weights, table)


def memory_kernel(memory_ref, weight_ref, table_ref, pair_ref):
    width = memory_ref.shape[1]
    rows = memory_ref[...]
    pair_ref[:, :width] = nn(rows, weight_ref[:, :width]).astype(bf16)
    pair_ref[:, width:] = (nn(rows, weight_ref[:, width:]) + row_of(table_ref, BIAS + 4)).astype(bf16)


def memory_pair(memory, weights, table):
    tokens, width = memory.shape
    return pl.pallas_call(
        memory_kernel,
        grid=(tokens // ROWS,),
        in_specs=[by_rows((ROWS, width)), held((width, 2 * width), (0, 1)), held(table.shape)],
        out_specs=by_rows((ROWS, 2 * width)),
        out_shape=out((tokens, 2 * width), bf16),
        compiler_params=params(),
        cost_estimate=cost(4 * tokens * width * width, 6 * tokens * width + 4 * width * width),
        name="memory_keys_values",
    )(memory, weights, table)


def late_kernel(hidden_ref, mixed_ref, out_ref, table_ref, next_ref, normed_ref):
    hidden = hidden_ref[...] + nn(mixed_ref[...], out_ref[...]) + row_of(table_ref, BIAS + 5)
    next_ref[...] = hidden
    normed, _ = normalise(hidden)
    normed_ref[...] = (normed * row_of(table_ref, GAIN + 2) + row_of(table_ref, SHIFT + 2)).astype(bf16)


def late(hidden, mixed, weights, table):
    tokens, width = hidden.shape
    block = by_rows((ROWS, width))
    return pl.pallas_call(
        late_kernel,
        grid=(tokens // ROWS,),
        in_specs=[block, block, held((width, width), (0, 4)), held(table.shape)],
        out_specs=[block, block],
        out_shape=[out((tokens, width), f32), out((tokens, width), bf16)],
        compiler_params=params(),
        cost_estimate=cost(2 * tokens * width * width, 12 * tokens * width + 2 * width * width),
        name="cross_out_norm",
    )(hidden, mixed, weights, table)


def head_operands(lane, side, query, key, key_bias):
    own = (lane < HEAD) if side == 0 else (lane >= HEAD)
    spare = lane == (HEAD if side == 0 else 0)
    zero = jnp.zeros((), bf16)
    query_own = jnp.where(own, query, zero)
    key_own = jnp.where(own, key, zero)
    query_wide = jnp.where(spare, jnp.ones((), bf16), query_own)
    key_wide = jnp.where(spare, key_bias, key_own)
    return own, query_own, query_wide, key_own, key_wide


def pair_operands(length_ref, query_ref, key_ref):
    lane = lax.broadcasted_iota(jnp.int32, (1, PAIR), 1)
    key_pos = lax.broadcasted_iota(jnp.int32, (key_ref.shape[0], 1), 0)
    key_bias = jnp.where(key_pos < length_ref[0], 0.0, masked_score).astype(bf16)
    query = query_ref[...] * jnp.asarray(HEAD**-0.5, bf16)
    key = key_ref[...]
    return lane, [head_operands(lane, side, query, key, key_bias) for side in (0, 1)]


def scores_by_key(key_wide, query_block, keys, allowed):
    scores = nt(key_wide[:keys], query_block)
    if allowed is None:
        return scores
    last = jnp.where(allowed, scores[keys - BLOCK :], masked_score)
    return last if keys == BLOCK else jnp.concatenate([scores[: keys - BLOCK], last], axis=0)


def causal_block():
    key = lax.broadcasted_iota(jnp.int32, (BLOCK, BLOCK), 0)
    query = lax.broadcasted_iota(jnp.int32, (BLOCK, BLOCK), 1)
    return key <= query


def attend_kernel(causal, length_ref, query_ref, key_ref, value_ref, mixed_ref, stat_ref):
    rows, keys_all = query_ref.shape[0], key_ref.shape[0]
    lane, heads = pair_operands(length_ref, query_ref, key_ref)
    value = value_ref[...]
    allowed = causal_block() if causal else None
    first = lane < HEAD
    value_wide = [jnp.where(heads[side][0], value, jnp.ones((), bf16)) for side in (0, 1)]
    for at in range(0, rows, BLOCK):
        keys = at + BLOCK if causal else keys_all
        got, tops = [], []
        for side in (0, 1):
            _, _, query_wide, _, key_wide = heads[side]
            scores = scores_by_key(key_wide, query_wide[at : at + BLOCK], keys, allowed)
            top = jnp.max(scores, axis=0, keepdims=True)
            exponent = jnp.exp(scores - top)
            got.append(tn(exponent.astype(bf16), value_wide[side][:keys]))
            tops.append(top)
        total = jnp.where(first, got[1], got[0])
        mixed = jnp.where(first, got[0], got[1]) / pltpu.roll(total, HEAD, 1)
        mixed_ref[at : at + BLOCK, :] = mixed.astype(bf16)
        logs = jnp.log(total).T
        stat_ref[0, 0:1, at : at + BLOCK] = tops[0] + logs[HEAD : HEAD + 1]
        stat_ref[0, 1:2, at : at + BLOCK] = tops[1] + logs[0:1]


def pair_block(rows, column=0):
    return pl.BlockSpec((rows, PAIR), lambda j: (0, column + j))


def attend(lengths, query, key, value, causal):
    rows, keys, width = query[0].shape[0], key[0].shape[0], query[2]
    pairs = width // PAIR
    return pl.pallas_call(
        functools.partial(attend_kernel, causal),
        grid=(pairs,),
        in_specs=[
            pl.BlockSpec(memory_space=pltpu.SMEM),
            pair_block(rows, query[1]),
            pair_block(keys, key[1]),
            pair_block(keys, value[1]),
        ],
        out_specs=[pair_block(rows), pl.BlockSpec((1, 2, rows), lambda j: (j, 0, 0))],
        out_shape=[out((rows, width), bf16), out((pairs, 2, rows), f32)],
        compiler_params=params(),
        cost_estimate=cost(16 * rows * keys * width, 4 * (rows + keys) * width, 16 * rows * keys),
        name="attend_causal" if causal else "attend_memory",
    )(lengths, query[0], key[0], value[0])


def attend_back_kernel(
    causal,
    length_ref,
    query_ref,
    key_ref,
    value_ref,
    mixed_ref,
    grad_ref,
    stat_ref,
    query_grad_ref,
    key_grad_ref,
    value_grad_ref,
    sums_ref,
    key_sum,
    value_sum,
):
    rows, keys_all = query_ref.shape[0], key_ref.shape[0]
    scale = HEAD**-0.5
    lane, heads = pair_operands(length_ref, query_ref, key_ref)
    value = value_ref[...]
    grad = grad_ref[...]
    inner = (grad.astype(f32) * mixed_ref[...].astype(f32)).T
    allowed = causal_block() if causal else None
    zero = jnp.zeros((), bf16)
    value_own = [jnp.where(heads[side][0], value, zero) for side in (0, 1)]
    grad_own = [jnp.where(heads[side][0], grad, zero) for side in (0, 1)]
    inner_sum = [
        jnp.sum(inner[side * HEAD : (side + 1) * HEAD], axis=0, keepdims=True) for side in (0, 1)
    ]
    for at in range(rows - BLOCK, -1, -BLOCK):
        keys = at + BLOCK if causal else keys_all
        span = slice(at, at + BLOCK)
        sums = None
        for side in (0, 1):
            _, query_own, query_wide, key_own, key_wide = heads[side]
            scores = scores_by_key(key_wide, query_wide[span], keys, allowed)
            probs = jnp.exp(scores - stat_ref[0, side : side + 1, span])
            grad_probs = nt(value_own[side][:keys], grad[span])
            grad_scores = (probs * (grad_probs - inner_sum[side][:, span])).astype(bf16)
            parts = (
                tn(grad_scores, key_own[:keys]),
                nn(grad_scores, query_own[span]),
                nn(probs.astype(bf16), grad_own[side][span]),
            )
            sums = parts if sums is None else tuple(a + b for a, b in zip(sums, parts))
        query_low = (sums[0] * scale).astype(bf16)
        query_grad_ref[span, :] = query_low
        query_total = column_sum(query_low) + (0.0 if at == rows - BLOCK else query_total)
        if at == rows - BLOCK:
            key_sum[...] = sums[1]
            value_sum[...] = sums[2]
        else:
            key_sum[:keys] += sums[1]
            value_sum[:keys] += sums[2]
    key_grad_ref[...] = key_sum[...].astype(bf16)
    value_low = value_sum[...].astype(bf16)
    value_grad_ref[...] = value_low
    sums_ref[...] = jnp.zeros_like(sums_ref)
    sums_ref[0:1, :] = query_total
    sums_ref[1:2, :] = column_sum(value_low)


def attend_back(lengths, query, key, value, mixed, grad, stats, causal, waits=(), share=(0, 1)):
    rows, keys = query[0].shape[0], key[0].shape[0]
    pairs = query[2] // PAIR // share[1]
    first, width = share[0] * pairs, pairs * PAIR
    kernel, in_specs = after(
        waits,
        functools.partial(attend_back_kernel, causal),
        [
            pl.BlockSpec(memory_space=pltpu.SMEM),
            pair_block(rows, query[1] + first),
            pair_block(keys, key[1] + first),
            pair_block(keys, value[1] + first),
            pair_block(rows, first),
            pair_block(rows, first),
            pl.BlockSpec((1, 2, rows), lambda j: (first + j, 0, 0)),
        ],
    )
    return pl.pallas_call(
        kernel,
        grid=(pairs,),
        in_specs=in_specs,
        out_specs=[pair_block(rows), pair_block(keys), pair_block(keys), pair_block(8)],
        out_shape=[
            out((rows, width), bf16),
            out((keys, width), bf16),
            out((keys, width), bf16),
            out((8, width), f32),
        ],
        scratch_shapes=[pltpu.VMEM((keys, PAIR), f32), pltpu.VMEM((keys, PAIR), f32)],
        compiler_params=params(),
        cost_estimate=cost(24 * rows * keys * width, 8 * (rows + keys) * width, 16 * rows * keys),
        name="attend_causal_back" if causal else "attend_memory_back",
    )(*waits, lengths, query[0], key[0], value[0], mixed, grad, stats)


FEED_ROWS = 512


def feed_kernel(
    split, me_ref, normed_ref, branch_ref, weight_ref, table_ref, made_ref, back_ref, bias_ref, *refs
):
    turned, act, dact = refs[-3:]
    step = pl.program_id(0)
    tokens, width = normed_ref.shape

    @pl.when(step == 0)
    def _():
        made_ref[...] = jnp.zeros_like(made_ref)
        back_ref[...] = jnp.zeros_like(back_ref)
        turned[...] = normed_ref[...].T

    bias = table_ref[pl.ds(HIDDEN_BIAS + step, 1), :]
    bias_sum = jnp.zeros((1, width), f32)
    for at in range(0, tokens, FEED_ROWS):
        span = slice(at, at + FEED_ROWS)
        inner = nn(normed_ref[span, :], weight_ref[:, :width]) + bias
        grad_active = nt(branch_ref[span, :], weight_ref[:, width:])
        square = inner * inner
        bent = jnp.tanh(inner * (gelu_slope + (gelu_slope * gelu_cubic) * square))
        half = 0.5 + 0.5 * bent
        active = (inner * half).astype(bf16)
        slope = half + (0.5 * inner) * (1.0 - bent * bent) * (
            gelu_slope + (3.0 * gelu_slope * gelu_cubic) * square
        )
        grad_inner = (grad_active * slope).astype(bf16)
        act[span, :] = active
        dact[span, :] = grad_inner
        bias_sum += column_sum(grad_inner)
        made_ref[span, :] += nn(active, weight_ref[:, width:])
        back_ref[span, :] += nt(grad_inner, weight_ref[:, :width])
    bias_ref[0] = jnp.broadcast_to(bias_sum, bias_ref.shape[1:])
    for at in range(0, width, FEED_ROWS):
        span = slice(at, at + FEED_ROWS)
        inner_part = nn(turned[span, :], dact[...]).astype(bf16)
        outer_part = tn(act[:, span], branch_ref[...]).astype(bf16)
        for part, columns in ((inner_part, slice(0, width)), (outer_part, slice(width, 2 * width))):
            if split is None:
                refs[0][span, columns] = part
            else:
                dp_size, own = split
                spread(part, at // (2 * own), own, dp_size, me_ref, refs[0], refs[1], columns)


def feed(normed, branch, weights, table, split):
    tokens, width = normed.shape
    steps = weights.shape[1] // (2 * width)
    hidden = steps * width
    whole = pl.BlockSpec((tokens, width), lambda j: (0, 0))
    tile = pl.BlockSpec((width, 2 * width), lambda j: (0, j))
    if split[1:]:
        grad_specs = [pl.BlockSpec((width // 2, 2 * width), lambda j: (0, j))] * 2
        grad_shapes = [out((width // 2, 2 * hidden), bf16)] * 2
    else:
        grad_specs, grad_shapes = [tile], [out((width, 2 * hidden), bf16)]
    return pl.pallas_call(
        functools.partial(feed_kernel, split[1:] or None),
        grid=(steps,),
        in_specs=[
            pl.BlockSpec(memory_space=pltpu.SMEM),
            held((tokens, width)),
            held((tokens, width)),
            tile,
            held(table.shape),
        ],
        out_specs=[whole, whole, pl.BlockSpec((1, 8, width), lambda j: (j, 0, 0))] + grad_specs,
        out_shape=[
            out((tokens, width), f32),
            out((tokens, width), f32),
            out((steps, 8, width), f32),
        ]
        + grad_shapes,
        scratch_shapes=[
            pltpu.VMEM((width, tokens), bf16),
            pltpu.VMEM((tokens, width), bf16),
            pltpu.VMEM((tokens, width), bf16),
        ],
        compiler_params=params(),
        cost_estimate=cost(
            12 * tokens * width * hidden, 8 * width * hidden + 12 * tokens * width, tokens * hidden
        ),
        name="feed_forward_both_ways",
    )(split[0], normed, branch, weights, table)


def add_rows(ref, rows):
    @pl.when(pl.program_id(0) == 0)
    def _():
        ref[...] = jnp.zeros_like(ref)

    for at, row in rows:
        ref[at : at + 1, :] += row


def turn_kernel(
    hidden_ref, made_ref, back_ref, cotangent_ref, out_ref, table_ref,
    result_ref, grad_ref, branch_ref, mixed_grad_ref, sums_ref,
):
    hidden = hidden_ref[...]
    low_in = cotangent_ref[...]
    result_ref[...] = (hidden + made_ref[...] + row_of(table_ref, BIAS + 6)).astype(bf16)
    part, gain_grad, shift_grad = norm_back(hidden, back_ref[...], row_of(table_ref, GAIN + 2))
    grad = low_in.astype(f32) + part
    grad_ref[...] = grad
    low = grad.astype(bf16)
    branch_ref[...] = low
    mixed_grad_ref[...] = nt(low, out_ref[...]).astype(bf16)
    add_rows(
        sums_ref,
        ((0, gain_grad), (1, shift_grad), (2, column_sum(low_in)), (3, column_sum(low))),
    )


def turn(hidden, made, back, cotangent, weights, table):
    tokens, width = hidden.shape
    block = by_rows((ROWS, width))
    return pl.pallas_call(
        turn_kernel,
        grid=(tokens // ROWS,),
        in_specs=[block, block, block, block, held((width, width), (0, 4)), held(table.shape)],
        out_specs=[block, block, block, block, pl.BlockSpec((8, width), lambda j: (0, 0))],
        out_shape=[
            out((tokens, width), bf16),
            out((tokens, width), f32),
            out((tokens, width), bf16),
            out((tokens, width), bf16),
            out((8, width), f32),
        ],
        compiler_params=params(),
        cost_estimate=cost(2 * tokens * width * width, 24 * tokens * width + 2 * width * width),
        name="norm_back_cross_out_back",
    )(hidden, made, back, cotangent, weights, table)


def middle_back_kernel(
    hidden_ref, grad_ref, query_grad_ref, query_ref, out_ref, table_ref,
    next_ref, branch_ref, mixed_grad_ref, sums_ref,
):
    incoming = nt(query_grad_ref[...], query_ref[...])
    part, gain_grad, shift_grad = norm_back(hidden_ref[...], incoming, row_of(table_ref, GAIN + 1))
    grad = grad_ref[...] + part
    next_ref[...] = grad
    low = grad.astype(bf16)
    branch_ref[...] = low
    mixed_grad_ref[...] = nt(low, out_ref[...]).astype(bf16)
    add_rows(
        sums_ref,
        ((0, gain_grad), (1, shift_grad), (3, column_sum(low))),
    )


def middle_back(hidden, grad, query_grad, weights, table, waits=()):
    tokens, width = hidden.shape
    block = by_rows((ROWS, width))
    kernel, in_specs = after(
        waits,
        middle_back_kernel,
        [
            block,
            block,
            block,
            held((width, width), (0, 1)),
            held((width, width), (0, 0)),
            held(table.shape),
        ],
    )
    return pl.pallas_call(
        kernel,
        grid=(tokens // ROWS,),
        in_specs=in_specs,
        out_specs=[block, block, block, pl.BlockSpec((8, width), lambda j: (0, 0))],
        out_shape=[
            out((tokens, width), f32),
            out((tokens, width), bf16),
            out((tokens, width), bf16),
            out((8, width), f32),
        ],
        compiler_params=params(),
        cost_estimate=cost(4 * tokens * width * width, 20 * tokens * width + 4 * width * width),
        name="query_norm_back_self_out_back",
    )(*waits, hidden, grad, query_grad, weights, weights, table)


def entry_back_kernel(x_ref, grad_ref, weight_ref, table_ref, *refs):
    grads, (input_grad_ref, sums_ref) = refs[:-2], refs[-2:]
    incoming, at = 0.0, 0
    for ref in grads:
        columns = ref.shape[1]
        incoming += nt(ref[...], weight_ref[:, at : at + columns])
        at += columns
    part, gain_grad, shift_grad = norm_back(x_ref[...].astype(f32), incoming, row_of(table_ref, GAIN))
    input_grad_ref[...] = grad_ref[...] + part
    add_rows(sums_ref, ((0, gain_grad), (1, shift_grad)))


def entry_back(x, grad, grads, weights, table, waits=()):
    tokens, width = x.shape
    block = by_rows((ROWS, width))
    kernel, in_specs = after(
        waits,
        entry_back_kernel,
        [block, block, held(weights.shape), held(table.shape)]
        + [by_rows((ROWS, part.shape[1])) for part in grads],
    )
    return pl.pallas_call(
        kernel,
        grid=(tokens // ROWS,),
        in_specs=in_specs,
        out_specs=[block, pl.BlockSpec((8, width), lambda j: (0, 0))],
        out_shape=[out((tokens, width), f32), out((8, width), f32)],
        compiler_params=params(),
        cost_estimate=cost(6 * tokens * width * width, 16 * tokens * width + 6 * width * width),
        name="qkv_norm_back",
    )(*waits, x, grad, weights, table, *grads)


def memory_back_kernel(key_grad_ref, value_grad_ref, weight_ref, memory_grad_ref):
    width = key_grad_ref.shape[1]
    made = nt(key_grad_ref[...], weight_ref[:, :width])
    memory_grad_ref[...] = made + nt(value_grad_ref[...], weight_ref[:, width:])


def memory_back(key_grad, value_grad, weights, waits=()):
    tokens, width = key_grad.shape
    block = by_rows((ROWS, width))
    kernel, in_specs = after(
        waits, memory_back_kernel, [block, block, held((width, 2 * width), (0, 1))]
    )
    return pl.pallas_call(
        kernel,
        grid=(tokens // ROWS,),
        in_specs=in_specs,
        out_specs=block,
        out_shape=out((tokens, width), f32),
        compiler_params=params(),
        cost_estimate=cost(4 * tokens * width * width, 8 * tokens * width + 4 * width * width, 0, 64),
        name="memory_back",
    )(*waits, key_grad, value_grad, weights)


def weight_grads_kernel(picks, *refs):
    step = pl.program_id(0)
    grads_ref = refs[-1]
    half, wide = grads_ref.shape[0] // 2, grads_ref.shape[1]
    for at, (left, right, column) in enumerate(picks):

        @pl.when(step == at)
        def _(left=left, right=right, column=column):
            for low in (0, half):
                grads_ref[low : low + half, :] = tn(
                    refs[left][:, low : low + half], refs[right][:, column : column + wide]
                ).astype(bf16)


def spread(made, first_pair, own, dp_size, me_ref, keep_ref, send_ref, columns):
    mine = me_ref[0]
    upper = lax.rem(mine, 2) == 1
    planes = keep_ref.shape[0] // own // dp_size
    mine_plane = lax.rem(lax.shift_right_logical(mine, 1), planes)
    for piece in range(made.shape[0] // (2 * own)):
        pair = first_pair + piece
        away = lax.bitwise_xor(mine_plane, pair % planes)
        place = away * dp_size + pair // planes
        span = pl.ds(pl.multiple_of(place * own, own), own)
        one = made[2 * own * piece : 2 * own * piece + own]
        two = made[2 * own * piece + own : 2 * own * (piece + 1)]
        keep_ref[span, columns] = jnp.where(upper, two, one)
        send_ref[span, columns] = jnp.where(upper, one, two)


def small_grads_kernel(one_ref, two_ref, three_ref, cross_ref, self_ref, hidden_ref, rows_ref):
    rows_ref[...] = jnp.zeros_like(rows_ref)
    places = [(GAIN, one_ref, 0), (GAIN + 1, two_ref, 0), (GAIN + 2, three_ref, 0)]
    places += [(SHIFT, one_ref, 1), (SHIFT + 1, two_ref, 1), (SHIFT + 2, three_ref, 1)]
    places += [(BIAS, self_ref, 0), (BIAS + 1, self_ref, 1), (BIAS + 2, two_ref, 3), (BIAS + 3, cross_ref, 0)]
    places += [(BIAS + 4, cross_ref, 1), (BIAS + 5, three_ref, 3), (BIAS + 6, three_ref, 2)]
    for at, ref, row in places:
        rows_ref[at : at + 1, :] = ref[row : row + 1, :]
    for step in range(hidden_ref.shape[0]):
        rows_ref[HIDDEN_BIAS + step : HIDDEN_BIAS + step + 1, :] = hidden_ref[step, 0:1, :]


def small_grads(*sums):
    width = sums[0].shape[1]
    return pl.pallas_call(
        small_grads_kernel,
        out_shape=out((24, width), f32),
        compiler_params=params(),
        name="small_grads",
    )(*sums)


def split_grads_kernel(picks, dp_size, own, me_ref, *refs):
    step = pl.program_id(0)
    keep_ref, send_ref = refs[-2:]
    half, wide = keep_ref.shape
    for at, (left, right, column) in enumerate(picks):

        @pl.when(step == at)
        def _(left=left, right=right, column=column):
            for low in (0, half):
                made = tn(refs[left][:, low : low + half], refs[right][:, column : column + wide])
                first_pair = low // (2 * own)
                spread(made.astype(bf16), first_pair, own, dp_size, me_ref, keep_ref, send_ref, slice(0, wide))


def weight_grads(pairs, split=None, waits=(), wide=1024):
    arrays, picks = [], []
    for left, right in pairs:
        at = []
        for array in (left, right):
            known = [i for i, other in enumerate(arrays) if other is array]
            if not known:
                arrays.append(array)
            at.append(known[0] if known else len(arrays) - 1)
        picks += [(at[0], at[1], column) for column in range(0, right.shape[1], wide)]
    width = pairs[0][0].shape[1]
    columns = sum(right.shape[1] for _, right in pairs)
    flops = sum(2 * left.shape[0] * width * right.shape[1] for left, right in pairs)
    nbytes = 2 * sum(a.size for a in arrays) + 2 * width * columns
    if split is None:
        return pl.pallas_call(
            functools.partial(weight_grads_kernel, tuple(picks)),
            grid=(len(picks),),
            in_specs=[held(array.shape) for array in arrays],
            out_specs=pl.BlockSpec((width, wide), lambda j: (0, j)),
            out_shape=out((width, columns), bf16),
            compiler_params=params(),
            cost_estimate=cost(flops, nbytes),
            name="weight_grads",
        )(*arrays)
    mine, dp_size, own = split
    half = pl.BlockSpec((width // 2, wide), lambda j: (0, j))
    kernel, in_specs = after(
        waits,
        functools.partial(split_grads_kernel, tuple(picks), dp_size, own),
        [pl.BlockSpec(memory_space=pltpu.SMEM)] + [held(array.shape) for array in arrays],
    )
    return pl.pallas_call(
        kernel,
        grid=(len(picks),),
        in_specs=in_specs,
        out_specs=[half, half],
        out_shape=[out((width // 2, columns), bf16)] * 2,
        compiler_params=params(),
        cost_estimate=cost(flops, nbytes),
        name="weight_grads_by_distance",
    )(*waits, mine, *arrays)


def place_kernel(me_ref, near_ref, far_ref, whole_ref):
    own = near_ref.shape[1]
    upper = lax.rem(me_ref[0], 2) == 1
    near, far = near_ref[0], far_ref[0]
    whole_ref[:own, :] = jnp.where(upper, far, near)
    whole_ref[own:, :] = jnp.where(upper, near, far)


def place(mine, near, far, dp_size):
    pairs, own, columns = near.shape
    planes = pairs // dp_size

    def pair_at(j, me_ref):
        away = lax.rem(j, dp_size) * planes + lax.div(j, dp_size)
        return lax.bitwise_xor(lax.shift_right_logical(me_ref[0], 1), away), 0

    block = pl.BlockSpec((1, own, columns), lambda j, me_ref: (j, 0, 0))
    return pl.pallas_call(
        place_kernel,
        grid_spec=pltpu.PrefetchScalarGridSpec(
            num_scalar_prefetch=1,
            grid=(pairs,),
            in_specs=[block, block],
            out_specs=pl.BlockSpec((2 * own, columns), pair_at),
        ),
        out_shape=out((2 * pairs * own, columns), bf16),
        compiler_params=params(),
        cost_estimate=cost(0, 8 * pairs * own * columns),
        name="place_by_device",
    )(mine, near, far)


def feed_own_kernel(*refs):
    owned, (inner_ref, outer_ref) = refs[:-2], refs[-2:]
    own, width = owned[0].shape[0], outer_ref.shape[1]
    tiles = [
        (ref, at * width) for ref in owned for at in range(0, ref.shape[1] // width, 2)
    ]
    for step, (ref, at) in enumerate(tiles):
        outer_ref[step * own : (step + 1) * own, :] = ref[:, at + width : at + 2 * width].astype(f32)
    for device in range(width // own):
        pieces = [ref[:, at + device * own : at + (device + 1) * own].astype(f32) for ref, at in tiles]
        span = len(tiles) * own
        inner_ref[:, device * span : (device + 1) * span] = jnp.concatenate(pieces, axis=1)


def feed_own_grads(owned, width, waits=()):
    own = owned[0].shape[0]
    steps = sum(part.shape[1] for part in owned) // (2 * width)
    vmem = pl.BlockSpec(memory_space=pltpu.VMEM)
    kernel, in_specs = after(waits, feed_own_kernel, [vmem] * len(owned))
    return pl.pallas_call(
        kernel,
        in_specs=in_specs,
        out_shape=[out((own, steps * width), f32), out((steps * own, width), f32)],
        compiler_params=params(),
        name="feed_own_grads",
    )(*waits, *owned)


def cut_kernel(cuts, whole_ref, *outs):
    for ref, (low, high) in zip(outs, cuts):
        ref[...] = whole_ref[:, low:high].astype(f32)


def cut_columns(whole, ends, waits=()):
    cuts = tuple(zip(ends[:-1], ends[1:]))
    own = whole.shape[0]
    vmem = pl.BlockSpec(memory_space=pltpu.VMEM)
    kernel, in_specs = after(waits, functools.partial(cut_kernel, cuts), [vmem])
    return pl.pallas_call(
        kernel,
        in_specs=in_specs,
        out_shape=[out((own, high - low), f32) for low, high in cuts],
        compiler_params=params(),
        name="own_columns",
    )(*waits, whole)


def plane_pieces_kernel(count, ranges, keep_ref, got_ref, *outs):
    rows = keep_ref.shape[0] // count
    for at, (low, high) in enumerate(ranges):
        for k in range(count):
            span = slice(k * rows, (k + 1) * rows)
            made = keep_ref[span, low:high].astype(f32) + got_ref[span, low:high].astype(f32)
            outs[at * count + k][...] = made.astype(bf16)


def lanes_of(columns):
    return next(n for n in (2048, 1664, 1408, 1280, 1024, 128) if columns % n == 0)


def plane_pieces(keep, got, count, waits, ends):
    rows, columns = keep.shape
    ranges = tuple(zip(ends[:-1], ends[1:]))
    if len(ranges) == 1:
        lanes = lanes_of(columns)
        steps, shapes, ranges = columns // lanes, [(columns, lanes)], ((0, lanes),)
    else:
        lanes, steps, shapes = columns, 1, [(high - low, high - low) for low, high in ranges]
    block = pl.BlockSpec((rows, lanes), lambda j: (0, j))
    kernel, in_specs = after(
        waits, functools.partial(plane_pieces_kernel, count, ranges), [block, block]
    )
    return pl.pallas_call(
        kernel,
        grid=(steps,),
        in_specs=in_specs,
        out_specs=[
            pl.BlockSpec((rows // count, n), lambda j: (0, j)) for _, n in shapes for _ in range(count)
        ],
        out_shape=[out((rows // count, n), bf16) for n, _ in shapes for _ in range(count)],
        compiler_params=params(),
        cost_estimate=cost(0, 6 * rows * columns),
        name="plane_pieces",
    )(*waits, keep, got)


def plane_total_kernel(*refs):
    total = refs[0][...].astype(f32)
    for ref in refs[1:-1]:
        total = total + ref[...].astype(f32)
    refs[-1][...] = total.astype(bf16)


def plane_total(pieces, waits=(), weight=0):
    rows, columns = pieces[0].shape
    lanes = lanes_of(columns)
    block = pl.BlockSpec((rows, lanes), lambda j: (0, j))
    kernel, in_specs = after(waits, plane_total_kernel, [block] * len(pieces))
    return pl.pallas_call(
        kernel,
        grid=(columns // lanes,),
        in_specs=in_specs,
        out_specs=block,
        out_shape=out((rows, columns), bf16),
        compiler_params=params(),
        cost_estimate=cost(weight * rows * columns, 2 * (len(pieces) + 1) * rows * columns),
        name="plane_total",
    )(*waits, *pieces)


def prepare_kernel(
    qkv_ref, out_ref, query_ref, pair_ref, cross_ref, inner_ref, outer_ref, gains_ref, shifts_ref, biases_ref, hidden_ref,
    first_ref, second_ref, third_ref,
):
    own, width = out_ref.shape
    steps = inner_ref.shape[1] // width
    devices = width // own
    rows = [gains_ref[...].astype(f32), shifts_ref[...].astype(f32), biases_ref[...].astype(f32)]
    hidden = hidden_ref[...].astype(f32)
    rows += [hidden[:, step * own : (step + 1) * own] for step in range(steps)]
    rows += [jnp.zeros((SMALL - HIDDEN_BIAS - steps, own), f32)]
    first_ref[:, : 3 * width] = qkv_ref[...]
    first_ref[:, 3 * width :] = jnp.concatenate(rows, axis=0).T.astype(bf16)
    second_ref[:, :width] = out_ref[...]
    second_ref[:, width : 2 * width] = query_ref[...]
    second_ref[:, 2 * width : 4 * width] = pair_ref[...]
    second_ref[:, 4 * width :] = cross_ref[...]
    for step in range(steps):
        pieces = [
            inner_ref[:, (device * steps + step) * own : (device * steps + step + 1) * own].astype(f32)
            for device in range(devices)
        ]
        third_ref[:, 2 * step * width : (2 * step + 1) * width] = jnp.concatenate(pieces, axis=1).astype(bf16)
        third_ref[:, (2 * step + 1) * width : (2 * step + 2) * width] = outer_ref[step * own : (step + 1) * own, :]


def prepare(*shards):
    own, width = shards[1].shape
    steps = shards[5].shape[1] // width
    return pl.pallas_call(
        prepare_kernel,
        out_shape=[
            out((own, 3 * width + SMALL), bf16),
            out((own, 5 * width), bf16),
            out((own, 2 * steps * width), bf16),
        ],
        compiler_params=params(),
        name="shards_to_gather",
    )(*shards)


AXES = ("dp", "fsdp")


def gather(shard):
    return lax.all_gather(shard, AXES, axis=0, tiled=True)


def scatter_sum(whole):
    return lax.psum_scatter(whole, AXES, scatter_dimension=0, tiled=True)


def exchange(array, axis, size, distance):
    return lax.ppermute(array, axis, [(i, i ^ distance) for i in range(size)])


def small_sum(sums, own, dp_size, fsdp_size):
    kept = sums
    for axis, size in (("fsdp", fsdp_size), ("dp", dp_size)):
        distance = 1
        while distance < size:
            kept = kept + exchange(kept, axis, size, distance)
            distance *= 2
    start = (lax.axis_index("dp") * fsdp_size + lax.axis_index("fsdp")) * own
    return lax.dynamic_slice_in_dim(kept, start, own, axis=1)


def add_low(left, right):
    return (left.astype(f32) + right.astype(f32)).astype(bf16)


def scatter_plane(keep, got, fsdp_size, waits=(), cut=()):
    planes = fsdp_size // 2
    made = list(plane_pieces(keep, got, planes, waits, (0, *cut, keep.shape[1])))
    both = [made[at : at + planes] for at in range(0, len(made), planes)]
    return [
        (part[1:], part[:1] + [exchange(part[k], "fsdp", fsdp_size, 2 * k) for k in range(1, planes)])
        for part in both
    ]


def scatter_line(total):
    return lax.psum_scatter(total, "dp", scatter_dimension=0, tiled=True)


def local(
    inputs,
    memory,
    cotangent,
    target_lengths,
    memory_lengths,
    norm_gains,
    norm_biases,
    self_qkv,
    self_out,
    cross_query,
    cross_kv,
    cross_out,
    ffn_in,
    ffn_out,
    proj_biases,
    ffn_in_bias,
):
    width = inputs.shape[2]
    own = self_qkv.shape[0]
    devices = width // own
    steps = ffn_in.shape[1] // width
    dp_size, fsdp_size = lax.axis_size("dp"), lax.axis_size("fsdp")
    by_distance = own % 16 == 0
    mine = (lax.axis_index("dp") * fsdp_size + lax.axis_index("fsdp")).astype(jnp.int32).reshape(1)
    split = (mine, dp_size, own) if by_distance else (mine,)

    if by_distance:
        first_shard, second_shard, feed_shard = prepare(
            self_qkv, self_out, cross_query, cross_kv, cross_out, ffn_in, ffn_out,
            norm_gains, norm_biases, proj_biases, ffn_in_bias.reshape(1, -1),
        )
    else:
        small = jnp.concatenate(
            [norm_gains, norm_biases, proj_biases, ffn_in_bias.reshape(steps, own)], axis=0
        )
        small = jnp.pad(small, ((0, SMALL - small.shape[0]), (0, 0))).T
        first_shard = jnp.concatenate([self_qkv, small], axis=1)
        second_shard = jnp.concatenate([self_out, cross_query, cross_kv, cross_out], axis=1)
        inner_shard = ffn_in.reshape(own, devices, steps, own).transpose(0, 2, 1, 3).reshape(own, steps, width)
        outer_shard = ffn_out.reshape(steps, own, width).transpose(1, 0, 2)
        feed_shard = jnp.concatenate([inner_shard, outer_shard], axis=2).reshape(own, 2 * steps * width)

    first = gather(first_shard)
    third = gather(feed_shard)
    x = inputs[0]
    rows = memory[0]
    branch = cotangent[0]
    waits = ()
    if by_distance:
        line = jnp.stack(
            [second_shard] + [exchange(second_shard, "dp", dp_size, k) for k in range(1, dp_size)]
        )
        plane = [exchange(line, "fsdp", fsdp_size, 2 * k) for k in range(1, fsdp_size // 2)]
        waits = (line,)
    table = first[:, 3 * width :].astype(f32).T[:24]

    normed_one, triple = entry(x, first, table, waits)
    parts = [(triple, at * (width // PAIR), width) for at in range(3)]
    self_mixed, self_stats = attend(target_lengths, *parts, True)
    if by_distance:
        near = jnp.concatenate([line] + plane)
        second = place(mine, near, exchange(near, "fsdp", fsdp_size, 1), dp_size)
    else:
        second = gather(second_shard)
    pair = memory_pair(rows, second, table)
    hidden_one, normed_two, queries = middle(x, self_mixed, second, table)
    cross_parts = [(queries, 0, width), (pair, 0, width), (pair, width // PAIR, width)]
    cross_mixed, cross_stats = attend(memory_lengths, *cross_parts, False)
    hidden_two, normed_three = late(hidden_one, cross_mixed, second, table)
    made, back, hidden_bias_sums, *feed_grads = feed(normed_three, branch, third, table, split)
    result, grad_two, branch_two, mixed_grad, sums_three = turn(
        hidden_two, made, back, branch, second, table
    )
    waits = ()
    if by_distance:
        feed_got = exchange(feed_grads[1], "fsdp", fsdp_size, 1)
        [(feed_sent, feed_plane)] = scatter_plane(feed_grads[0], feed_got, fsdp_size, (result,))
        waits = tuple(feed_sent)
    else:
        feed_own = scatter_sum(feed_grads[0])
    query_grad, key_grad, value_grad, cross_sums = attend_back(
        memory_lengths, *cross_parts, cross_mixed, mixed_grad, cross_stats, False, waits
    )
    cross_pairs = [
        (cross_mixed, branch_two),
        (normed_two, query_grad),
        (rows, key_grad),
        (rows, value_grad),
    ]
    waits = ()
    if by_distance:
        cross_keep, cross_send = weight_grads(cross_pairs, split)
        cross_got = exchange(cross_send, "fsdp", fsdp_size, 1)
        waits = (cross_send,)
    grad_one, branch_one, mixed_grad, sums_two = middle_back(
        hidden_one, grad_two, query_grad, second, table, waits
    )
    if by_distance:
        [(cross_sent, cross_plane)] = scatter_plane(cross_keep, cross_got, fsdp_size, (grad_one,))
        waits = tuple(cross_sent)
    *self_grads, self_sums = attend_back(
        target_lengths, *parts, self_mixed, mixed_grad, self_stats, True, waits
    )
    self_pairs = [(self_mixed, branch_one)] + [(normed_one, part) for part in self_grads]
    waits = ()
    if by_distance:
        feed_total = plane_total(feed_plane, (self_sums,))
        feed_own = scatter_line(feed_total)
        self_keep, self_send = weight_grads(self_pairs, split, (feed_total,))
        self_got = exchange(self_send, "fsdp", fsdp_size, 1)
        cross_total = plane_total(cross_plane, (self_send,), 4096)
        cross_own = scatter_line(cross_total)
        [(self_sent, self_plane)] = scatter_plane(self_keep, self_got, fsdp_size, (cross_total,))
        waits = tuple(self_sent)
    input_grad, sums_one = entry_back(x, grad_one, self_grads, first, table, waits)
    sums = small_grads(sums_one, sums_two, sums_three, cross_sums, self_sums, hidden_bias_sums)
    if by_distance:
        memory_grad = memory_back(key_grad, value_grad, second, (input_grad,))
        inner_own, outer_own = feed_own_grads([feed_own], width, (memory_grad,))
        cross_out_own, query_own, pair_own = cut_columns(
            cross_own, (0, width, 2 * width, 4 * width), (inner_own,)
        )
        self_total = plane_total(self_plane, (cross_out_own,))
        self_own = scatter_line(self_total)
        self_out_own, triple_own = cut_columns(self_own, (0, width, 4 * width))
    else:
        memory_grad = memory_back(key_grad, value_grad, second)
        cross_own = scatter_sum(weight_grads(cross_pairs)).astype(f32)
        cross_out_own, query_own = cross_own[:, :width], cross_own[:, width : 2 * width]
        pair_own = cross_own[:, 2 * width :]
        self_own = scatter_sum(weight_grads(self_pairs)).astype(f32)
        self_out_own, triple_own = self_own[:, :width], self_own[:, width:]
        feed_own = feed_own.astype(f32).reshape(own, steps, 2, width)
        inner_own = feed_own[:, :, 0].reshape(own, steps, devices, own).transpose(0, 2, 1, 3)
        inner_own = inner_own.reshape(own, steps * width)
        outer_own = feed_own[:, :, 1].transpose(1, 0, 2).reshape(steps * own, width)
    small_own = small_sum(sums, own, dp_size, fsdp_size)
    return (
        result[None],
        input_grad[None],
        memory_grad[None],
        small_own[GAIN:SHIFT],
        small_own[SHIFT:BIAS],
        triple_own,
        self_out_own,
        query_own,
        pair_own,
        cross_out_own,
        inner_own,
        outer_own,
        small_own[BIAS:HIDDEN_BIAS],
        small_own[HIDDEN_BIAS : HIDDEN_BIAS + steps].reshape(steps * own),
    )


def solution(mesh):
    rows = P(AXES, None, None)
    lengths = P(AXES)
    split = P(AXES, None)
    features = P(None, AXES)
    return jax.shard_map(
        local,
        mesh=mesh,
        in_specs=(rows, rows, rows, lengths, lengths, features, features)
        + (split,) * 7
        + (features, lengths),
        out_specs=(rows, rows, rows, features, features) + (split,) * 7 + (features, lengths),
        check_vma=False,
    )
```

```python
import functools

import jax
import jax.numpy as jnp
from jax import lax
from jax.experimental import pallas as pl
from jax.experimental.pallas import tpu as pltpu
from jax.sharding import PartitionSpec as P

f32 = jnp.float32
bf16 = jnp.bfloat16

HEAD = 64
PAIR = 2 * HEAD
BLOCK = 256
ROWS = 256
SMALL = 128
eps_norm = 1e-05
masked_score = -1e30
gelu_slope = 0.7978845608028654
gelu_cubic = 0.044715
MiB = 1 << 20


def nn(left, right):
    return jnp.dot(left, right, preferred_element_type=f32)


def nt(left, right):
    return lax.dot_general(left, right, (((1,), (1,)), ((), ())), preferred_element_type=f32)


def tn(left, right):
    return lax.dot_general(left, right, (((0,), (0,)), ((), ())), preferred_element_type=f32)


def normalise(hidden):
    centred = hidden - jnp.mean(hidden, axis=-1, keepdims=True)
    spread = lax.rsqrt(jnp.mean(centred * centred, axis=-1, keepdims=True) + eps_norm)
    return centred * spread, spread


def norm_back(hidden, incoming, gain):
    normed, spread = normalise(hidden)
    scaled = incoming * gain
    part = spread * (
        scaled
        - jnp.mean(scaled, axis=-1, keepdims=True)
        - normed * jnp.mean(scaled * normed, axis=-1, keepdims=True)
    )
    gain_grad = jnp.sum(incoming * normed, axis=0, keepdims=True)
    shift_grad = jnp.sum(incoming, axis=0, keepdims=True)
    return part, gain_grad, shift_grad


def column_sum(gradient):
    return jnp.sum(gradient.astype(f32), axis=0, keepdims=True)


def params():
    return pltpu.CompilerParams(vmem_limit_bytes=60 * MiB)


def after(waits, kernel, in_specs):
    count = len(waits)

    def waiting(*refs):
        kernel(*refs[count:])

    return waiting, [pl.BlockSpec(memory_space=pl.ANY)] * count + in_specs


def cost(flops, nbytes, transcendentals=0, high=64):
    return pl.CostEstimate(
        flops=high * flops, bytes_accessed=high * nbytes, transcendentals=high * transcendentals
    )


def held(shape, at=None):
    place = (0,) * len(shape) if at is None else at
    return pl.BlockSpec(shape, lambda j: place, pipeline_mode=pl.Buffered(1))


def by_rows(shape):
    return pl.BlockSpec(shape, lambda j: (j, 0))


def out(shape, dtype):
    return jax.ShapeDtypeStruct(shape, dtype)


GAIN, SHIFT, BIAS, HIDDEN_BIAS = 0, 3, 6, 13


def row_of(table_ref, at):
    return table_ref[at : at + 1, :]


def entry_kernel(x_ref, weight_ref, table_ref, normed_ref, triple_ref):
    width = x_ref.shape[1]
    normed, _ = normalise(x_ref[...].astype(f32))
    low = (normed * row_of(table_ref, GAIN) + row_of(table_ref, SHIFT)).astype(bf16)
    normed_ref[...] = low
    for part in range(3):
        span = slice(part * width, (part + 1) * width)
        made = nn(low, weight_ref[:, span])
        if part == 0:
            made = made + row_of(table_ref, BIAS)
        if part == 2:
            made = made + row_of(table_ref, BIAS + 1)
        triple_ref[:, span] = made.astype(bf16)


def entry(x, weights, table, waits=()):
    tokens, width = x.shape
    kernel, in_specs = after(
        waits, entry_kernel, [by_rows((ROWS, width)), held(weights.shape), held(table.shape)]
    )
    return pl.pallas_call(
        kernel,
        grid=(tokens // ROWS,),
        in_specs=in_specs,
        out_specs=[by_rows((ROWS, width)), by_rows((ROWS, 3 * width))],
        out_shape=[out((tokens, width), bf16), out((tokens, 3 * width), bf16)],
        compiler_params=params(),
        cost_estimate=cost(6 * tokens * width * width, 10 * tokens * width + 6 * width * width, 0, 1),
        name="norm_and_qkv",
    )(*waits, x, weights, table)


def middle_kernel(x_ref, mixed_ref, out_ref, query_ref, table_ref, hidden_ref, normed_ref, made_ref):
    hidden = x_ref[...].astype(f32) + nn(mixed_ref[...], out_ref[...]) + row_of(table_ref, BIAS + 2)
    hidden_ref[...] = hidden
    normed, _ = normalise(hidden)
    low = (normed * row_of(table_ref, GAIN + 1) + row_of(table_ref, SHIFT + 1)).astype(bf16)
    normed_ref[...] = low
    made_ref[...] = (nn(low, query_ref[...]) + row_of(table_ref, BIAS + 3)).astype(bf16)


def middle(x, mixed, weights, table):
    tokens, width = x.shape
    block = by_rows((ROWS, width))
    return pl.pallas_call(
        middle_kernel,
        grid=(tokens // ROWS,),
        in_specs=[
            block,
            block,
            held((width, width), (0, 0)),
            held((width, width), (0, 1)),
            held(table.shape),
        ],
        out_specs=[block, block, block],
        out_shape=[out((tokens, width), f32), out((tokens, width), bf16), out((tokens, width), bf16)],
        compiler_params=params(),
        cost_estimate=cost(4 * tokens * width * width, 12 * tokens * width + 4 * width * width, 0, 1),
        name="self_out_norm_query",
    )(x, mixed, weights, weights, table)


def memory_kernel(memory_ref, weight_ref, table_ref, pair_ref):
    width = memory_ref.shape[1]
    rows = memory_ref[...]
    pair_ref[:, :width] = nn(rows, weight_ref[:, :width]).astype(bf16)
    pair_ref[:, width:] = (nn(rows, weight_ref[:, width:]) + row_of(table_ref, BIAS + 4)).astype(bf16)


def memory_pair(memory, weights, table):
    tokens, width = memory.shape
    return pl.pallas_call(
        memory_kernel,
        grid=(tokens // ROWS,),
        in_specs=[by_rows((ROWS, width)), held((width, 2 * width), (0, 1)), held(table.shape)],
        out_specs=by_rows((ROWS, 2 * width)),
        out_shape=out((tokens, 2 * width), bf16),
        compiler_params=params(),
        cost_estimate=cost(4 * tokens * width * width, 6 * tokens * width + 4 * width * width, 0, 1),
        name="memory_keys_values",
    )(memory, weights, table)


def late_kernel(hidden_ref, mixed_ref, out_ref, table_ref, next_ref, normed_ref):
    hidden = hidden_ref[...] + nn(mixed_ref[...], out_ref[...]) + row_of(table_ref, BIAS + 5)
    next_ref[...] = hidden
    normed, _ = normalise(hidden)
    normed_ref[...] = (normed * row_of(table_ref, GAIN + 2) + row_of(table_ref, SHIFT + 2)).astype(bf16)


def late(hidden, mixed, weights, table):
    tokens, width = hidden.shape
    block = by_rows((ROWS, width))
    return pl.pallas_call(
        late_kernel,
        grid=(tokens // ROWS,),
        in_specs=[block, block, held((width, width), (0, 4)), held(table.shape)],
        out_specs=[block, block],
        out_shape=[out((tokens, width), f32), out((tokens, width), bf16)],
        compiler_params=params(),
        cost_estimate=cost(2 * tokens * width * width, 12 * tokens * width + 2 * width * width, 0, 1),
        name="cross_out_norm",
    )(hidden, mixed, weights, table)


def head_operands(lane, side, query, key, key_bias):
    own = (lane < HEAD) if side == 0 else (lane >= HEAD)
    spare = lane == (HEAD if side == 0 else 0)
    zero = jnp.zeros((), bf16)
    query_own = jnp.where(own, query, zero)
    key_own = jnp.where(own, key, zero)
    query_wide = jnp.where(spare, jnp.ones((), bf16), query_own)
    key_wide = jnp.where(spare, key_bias, key_own)
    return own, query_own, query_wide, key_own, key_wide


def pair_operands(length_ref, query_ref, key_ref):
    lane = lax.broadcasted_iota(jnp.int32, (1, PAIR), 1)
    key_pos = lax.broadcasted_iota(jnp.int32, (key_ref.shape[0], 1), 0)
    key_bias = jnp.where(key_pos < length_ref[0], 0.0, masked_score).astype(bf16)
    query = query_ref[...] * jnp.asarray(HEAD**-0.5, bf16)
    key = key_ref[...]
    return lane, [head_operands(lane, side, query, key, key_bias) for side in (0, 1)]


def scores_by_key(key_wide, query_block, keys, allowed):
    scores = nt(key_wide[:keys], query_block)
    if allowed is None:
        return scores
    last = jnp.where(allowed, scores[keys - BLOCK :], masked_score)
    return last if keys == BLOCK else jnp.concatenate([scores[: keys - BLOCK], last], axis=0)


def causal_block():
    key = lax.broadcasted_iota(jnp.int32, (BLOCK, BLOCK), 0)
    query = lax.broadcasted_iota(jnp.int32, (BLOCK, BLOCK), 1)
    return key <= query


def attend_kernel(causal, length_ref, query_ref, key_ref, value_ref, mixed_ref, stat_ref):
    rows, keys_all = query_ref.shape[0], key_ref.shape[0]
    lane, heads = pair_operands(length_ref, query_ref, key_ref)
    value = value_ref[...]
    allowed = causal_block() if causal else None
    first = lane < HEAD
    value_wide = [jnp.where(heads[side][0], value, jnp.ones((), bf16)) for side in (0, 1)]
    for at in range(0, rows, BLOCK):
        keys = at + BLOCK if causal else keys_all
        got, tops = [], []
        for side in (0, 1):
            _, _, query_wide, _, key_wide = heads[side]
            scores = scores_by_key(key_wide, query_wide[at : at + BLOCK], keys, allowed)
            top = jnp.max(scores, axis=0, keepdims=True)
            exponent = jnp.exp(scores - top)
            got.append(tn(exponent.astype(bf16), value_wide[side][:keys]))
            tops.append(top)
        total = jnp.where(first, got[1], got[0])
        mixed = jnp.where(first, got[0], got[1]) / pltpu.roll(total, HEAD, 1)
        mixed_ref[at : at + BLOCK, :] = mixed.astype(bf16)
        logs = jnp.log(total).T
        stat_ref[0, 0:1, at : at + BLOCK] = tops[0] + logs[HEAD : HEAD + 1]
        stat_ref[0, 1:2, at : at + BLOCK] = tops[1] + logs[0:1]


def pair_block(rows, column=0):
    return pl.BlockSpec((rows, PAIR), lambda j: (0, column + j))


def attend(lengths, query, key, value, causal):
    rows, keys, width = query[0].shape[0], key[0].shape[0], query[2]
    pairs = width // PAIR
    return pl.pallas_call(
        functools.partial(attend_kernel, causal),
        grid=(pairs,),
        in_specs=[
            pl.BlockSpec(memory_space=pltpu.SMEM),
            pair_block(rows, query[1]),
            pair_block(keys, key[1]),
            pair_block(keys, value[1]),
        ],
        out_specs=[pair_block(rows), pl.BlockSpec((1, 2, rows), lambda j: (j, 0, 0))],
        out_shape=[out((rows, width), bf16), out((pairs, 2, rows), f32)],
        compiler_params=params(),
        cost_estimate=cost(16 * rows * keys * width, 4 * (rows + keys) * width, 16 * rows * keys, 1),
        name="attend_causal" if causal else "attend_memory",
    )(lengths, query[0], key[0], value[0])


def attend_back_kernel(
    causal,
    length_ref,
    query_ref,
    key_ref,
    value_ref,
    mixed_ref,
    grad_ref,
    stat_ref,
    query_grad_ref,
    key_grad_ref,
    value_grad_ref,
    sums_ref,
    key_sum,
    value_sum,
):
    rows, keys_all = query_ref.shape[0], key_ref.shape[0]
    scale = HEAD**-0.5
    lane, heads = pair_operands(length_ref, query_ref, key_ref)
    value = value_ref[...]
    grad = grad_ref[...]
    inner = (grad.astype(f32) * mixed_ref[...].astype(f32)).T
    allowed = causal_block() if causal else None
    zero = jnp.zeros((), bf16)
    value_own = [jnp.where(heads[side][0], value, zero) for side in (0, 1)]
    grad_own = [jnp.where(heads[side][0], grad, zero) for side in (0, 1)]
    inner_sum = [
        jnp.sum(inner[side * HEAD : (side + 1) * HEAD], axis=0, keepdims=True) for side in (0, 1)
    ]
    block = BLOCK if causal else rows
    for at in range(rows - block, -1, -block):
        keys = at + block if causal else keys_all
        span = slice(at, at + block)
        sums = None
        for side in (0, 1):
            _, query_own, query_wide, key_own, key_wide = heads[side]
            scores = scores_by_key(key_wide, query_wide[span], keys, allowed)
            probs = jnp.exp(scores - stat_ref[0, side : side + 1, span])
            grad_probs = nt(value_own[side][:keys], grad[span])
            grad_scores = (probs * (grad_probs - inner_sum[side][:, span])).astype(bf16)
            parts = (
                tn(grad_scores, key_own[:keys]),
                nn(grad_scores, query_own[span]),
                nn(probs.astype(bf16), grad_own[side][span]),
            )
            sums = parts if sums is None else tuple(a + b for a, b in zip(sums, parts))
        query_low = (sums[0] * scale).astype(bf16)
        query_grad_ref[span, :] = query_low
        query_total = column_sum(query_low) + (0.0 if at == rows - block else query_total)
        if at == rows - block:
            key_sum[...] = sums[1]
            value_sum[...] = sums[2]
        else:
            key_sum[:keys] += sums[1]
            value_sum[:keys] += sums[2]
    key_grad_ref[...] = key_sum[...].astype(bf16)
    value_low = value_sum[...].astype(bf16)
    value_grad_ref[...] = value_low
    sums_ref[...] = jnp.zeros_like(sums_ref)
    sums_ref[0:1, :] = query_total
    sums_ref[1:2, :] = column_sum(value_low)


def attend_back(lengths, query, key, value, mixed, grad, stats, causal, waits=(), share=(0, 1)):
    rows, keys = query[0].shape[0], key[0].shape[0]
    pairs = query[2] // PAIR // share[1]
    first, width = share[0] * pairs, pairs * PAIR
    kernel, in_specs = after(
        waits,
        functools.partial(attend_back_kernel, causal),
        [
            pl.BlockSpec(memory_space=pltpu.SMEM),
            pair_block(rows, query[1] + first),
            pair_block(keys, key[1] + first),
            pair_block(keys, value[1] + first),
            pair_block(rows, first),
            pair_block(rows, first),
            pl.BlockSpec((1, 2, rows), lambda j: (first + j, 0, 0)),
        ],
    )
    return pl.pallas_call(
        kernel,
        grid=(pairs,),
        in_specs=in_specs,
        out_specs=[pair_block(rows), pair_block(keys), pair_block(keys), pair_block(8)],
        out_shape=[
            out((rows, width), bf16),
            out((keys, width), bf16),
            out((keys, width), bf16),
            out((8, width), f32),
        ],
        scratch_shapes=[pltpu.VMEM((keys, PAIR), f32), pltpu.VMEM((keys, PAIR), f32)],
        compiler_params=params(),
        cost_estimate=cost(24 * rows * keys * width, 8 * (rows + keys) * width, 16 * rows * keys),
        name="attend_causal_back" if causal else "attend_memory_back",
    )(*waits, lengths, query[0], key[0], value[0], mixed, grad, stats)


FEED_ROWS = 512


def feed_kernel(
    split, me_ref, normed_ref, branch_ref, weight_ref, table_ref, made_ref, back_ref, bias_ref, *refs
):
    turned, act, dact = refs[-3:]
    step = pl.program_id(0)
    tokens, width = normed_ref.shape

    @pl.when(step == 0)
    def _():
        made_ref[...] = jnp.zeros_like(made_ref)
        back_ref[...] = jnp.zeros_like(back_ref)
        turned[...] = normed_ref[...].T

    bias = table_ref[pl.ds(HIDDEN_BIAS + step, 1), :]
    bias_sum = jnp.zeros((1, width), f32)
    for at in range(0, tokens, FEED_ROWS):
        span = slice(at, at + FEED_ROWS)
        inner = nn(normed_ref[span, :], weight_ref[:, :width]) + bias
        grad_active = nt(branch_ref[span, :], weight_ref[:, width:])
        square = inner * inner
        bent = jnp.tanh(inner * (gelu_slope + (gelu_slope * gelu_cubic) * square))
        half = 0.5 + 0.5 * bent
        active = (inner * half).astype(bf16)
        slope = half + (0.5 * inner) * (1.0 - bent * bent) * (
            gelu_slope + (3.0 * gelu_slope * gelu_cubic) * square
        )
        grad_inner = (grad_active * slope).astype(bf16)
        act[span, :] = active
        dact[span, :] = grad_inner
        bias_sum += column_sum(grad_inner)
        made_ref[span, :] += nn(active, weight_ref[:, width:])
        back_ref[span, :] += nt(grad_inner, weight_ref[:, :width])
    bias_ref[0] = jnp.broadcast_to(bias_sum, bias_ref.shape[1:])
    for at in range(0, width, FEED_ROWS):
        span = slice(at, at + FEED_ROWS)
        inner_part = nn(turned[span, :], dact[...]).astype(bf16)
        outer_part = tn(act[:, span], branch_ref[...]).astype(bf16)
        for part, columns in ((inner_part, slice(0, width)), (outer_part, slice(width, 2 * width))):
            if split is None:
                refs[0][span, columns] = part
            else:
                dp_size, own = split
                spread(part, at // (2 * own), own, dp_size, me_ref, refs[0], refs[1], columns)


def feed(normed, branch, weights, table, split):
    tokens, width = normed.shape
    steps = weights.shape[1] // (2 * width)
    hidden = steps * width
    whole = pl.BlockSpec((tokens, width), lambda j: (0, 0))
    tile = pl.BlockSpec((width, 2 * width), lambda j: (0, j))
    if split[1:]:
        grad_specs = [pl.BlockSpec((width // 2, 2 * width), lambda j: (0, j))] * 2
        grad_shapes = [out((width // 2, 2 * hidden), bf16)] * 2
    else:
        grad_specs, grad_shapes = [tile], [out((width, 2 * hidden), bf16)]
    return pl.pallas_call(
        functools.partial(feed_kernel, split[1:] or None),
        grid=(steps,),
        in_specs=[
            pl.BlockSpec(memory_space=pltpu.SMEM),
            held((tokens, width)),
            held((tokens, width)),
            tile,
            held(table.shape),
        ],
        out_specs=[whole, whole, pl.BlockSpec((1, 8, width), lambda j: (j, 0, 0))] + grad_specs,
        out_shape=[
            out((tokens, width), f32),
            out((tokens, width), f32),
            out((steps, 8, width), f32),
        ]
        + grad_shapes,
        scratch_shapes=[
            pltpu.VMEM((width, tokens), bf16),
            pltpu.VMEM((tokens, width), bf16),
            pltpu.VMEM((tokens, width), bf16),
        ],
        compiler_params=params(),
        cost_estimate=cost(
            12 * tokens * width * hidden, 8 * width * hidden + 12 * tokens * width, tokens * hidden
        ),
        name="feed_forward_both_ways",
    )(split[0], normed, branch, weights, table)


def add_rows(ref, rows):
    @pl.when(pl.program_id(0) == 0)
    def _():
        ref[...] = jnp.zeros_like(ref)

    for at, row in rows:
        ref[at : at + 1, :] += row


def turn_kernel(
    hidden_ref, back_ref, cotangent_ref, out_ref, table_ref, grad_ref, branch_ref, mixed_grad_ref, sums_ref
):
    low_in = cotangent_ref[...]
    part, gain_grad, shift_grad = norm_back(hidden_ref[...], back_ref[...], row_of(table_ref, GAIN + 2))
    grad = low_in.astype(f32) + part
    grad_ref[...] = grad
    low = grad.astype(bf16)
    branch_ref[...] = low
    mixed_grad_ref[...] = nt(low, out_ref[...]).astype(bf16)
    add_rows(
        sums_ref,
        ((0, gain_grad), (1, shift_grad), (2, column_sum(low_in)), (3, column_sum(low))),
    )


def turn(hidden, back, cotangent, weights, table):
    tokens, width = hidden.shape
    block = by_rows((ROWS, width))
    return pl.pallas_call(
        turn_kernel,
        grid=(tokens // ROWS,),
        in_specs=[block, block, block, held((width, width), (0, 4)), held(table.shape)],
        out_specs=[block, block, block, pl.BlockSpec((8, width), lambda j: (0, 0))],
        out_shape=[
            out((tokens, width), f32),
            out((tokens, width), bf16),
            out((tokens, width), bf16),
            out((8, width), f32),
        ],
        compiler_params=params(),
        cost_estimate=cost(2 * tokens * width * width, 18 * tokens * width + 2 * width * width),
        name="norm_back_cross_out_back",
    )(hidden, back, cotangent, weights, table)


def result_kernel(hidden_ref, made_ref, table_ref, result_ref):
    result_ref[...] = (hidden_ref[...] + made_ref[...] + row_of(table_ref, BIAS + 6)).astype(bf16)


def layer_result(hidden, made, table, waits=()):
    tokens, width = hidden.shape
    block = by_rows((ROWS, width))
    kernel, in_specs = after(waits, result_kernel, [block, block, held(table.shape)])
    return pl.pallas_call(
        kernel,
        grid=(tokens // ROWS,),
        in_specs=in_specs,
        out_specs=block,
        out_shape=out((tokens, width), bf16),
        compiler_params=params(),
        cost_estimate=cost(0, 10 * tokens * width),
        name="layer_result",
    )(*waits, hidden, made, table)


def middle_back_kernel(
    hidden_ref, grad_ref, query_grad_ref, query_ref, out_ref, table_ref,
    next_ref, branch_ref, mixed_grad_ref, sums_ref,
):
    incoming = nt(query_grad_ref[...], query_ref[...])
    part, gain_grad, shift_grad = norm_back(hidden_ref[...], incoming, row_of(table_ref, GAIN + 1))
    grad = grad_ref[...] + part
    next_ref[...] = grad
    low = grad.astype(bf16)
    branch_ref[...] = low
    mixed_grad_ref[...] = nt(low, out_ref[...]).astype(bf16)
    add_rows(
        sums_ref,
        ((0, gain_grad), (1, shift_grad), (3, column_sum(low))),
    )


def middle_back(hidden, grad, query_grad, weights, table, waits=()):
    tokens, width = hidden.shape
    block = by_rows((ROWS, width))
    kernel, in_specs = after(
        waits,
        middle_back_kernel,
        [
            block,
            block,
            block,
            held((width, width), (0, 1)),
            held((width, width), (0, 0)),
            held(table.shape),
        ],
    )
    return pl.pallas_call(
        kernel,
        grid=(tokens // ROWS,),
        in_specs=in_specs,
        out_specs=[block, block, block, pl.BlockSpec((8, width), lambda j: (0, 0))],
        out_shape=[
            out((tokens, width), f32),
            out((tokens, width), bf16),
            out((tokens, width), bf16),
            out((8, width), f32),
        ],
        compiler_params=params(),
        cost_estimate=cost(4 * tokens * width * width, 20 * tokens * width + 4 * width * width),
        name="query_norm_back_self_out_back",
    )(*waits, hidden, grad, query_grad, weights, weights, table)


def entry_back_kernel(x_ref, grad_ref, weight_ref, table_ref, *refs):
    grads, (input_grad_ref, sums_ref) = refs[:-2], refs[-2:]
    incoming, at = 0.0, 0
    for ref in grads:
        columns = ref.shape[1]
        incoming += nt(ref[...], weight_ref[:, at : at + columns])
        at += columns
    part, gain_grad, shift_grad = norm_back(x_ref[...].astype(f32), incoming, row_of(table_ref, GAIN))
    input_grad_ref[...] = grad_ref[...] + part
    add_rows(sums_ref, ((0, gain_grad), (1, shift_grad)))


def entry_back(x, grad, grads, weights, table, waits=()):
    tokens, width = x.shape
    block = by_rows((ROWS, width))
    kernel, in_specs = after(
        waits,
        entry_back_kernel,
        [block, block, held(weights.shape), held(table.shape)]
        + [by_rows((ROWS, part.shape[1])) for part in grads],
    )
    return pl.pallas_call(
        kernel,
        grid=(tokens // ROWS,),
        in_specs=in_specs,
        out_specs=[block, pl.BlockSpec((8, width), lambda j: (0, 0))],
        out_shape=[out((tokens, width), f32), out((8, width), f32)],
        compiler_params=params(),
        cost_estimate=cost(6 * tokens * width * width, 16 * tokens * width + 6 * width * width),
        name="qkv_norm_back",
    )(*waits, x, grad, weights, table, *grads)


def memory_back_kernel(key_grad_ref, value_grad_ref, weight_ref, memory_grad_ref):
    width = key_grad_ref.shape[1]
    made = nt(key_grad_ref[...], weight_ref[:, :width])
    memory_grad_ref[...] = made + nt(value_grad_ref[...], weight_ref[:, width:])


def memory_back(key_grad, value_grad, weights, waits=()):
    tokens, width = key_grad.shape
    block = by_rows((ROWS, width))
    kernel, in_specs = after(
        waits, memory_back_kernel, [block, block, held((width, 2 * width), (0, 1))]
    )
    return pl.pallas_call(
        kernel,
        grid=(tokens // ROWS,),
        in_specs=in_specs,
        out_specs=block,
        out_shape=out((tokens, width), f32),
        compiler_params=params(),
        cost_estimate=cost(4 * tokens * width * width, 8 * tokens * width + 4 * width * width, 0, 64),
        name="memory_back",
    )(*waits, key_grad, value_grad, weights)


def weight_grads_kernel(picks, *refs):
    step = pl.program_id(0)
    grads_ref = refs[-1]
    half, wide = grads_ref.shape[0] // 2, grads_ref.shape[1]
    for at, (left, right, column) in enumerate(picks):

        @pl.when(step == at)
        def _(left=left, right=right, column=column):
            for low in (0, half):
                grads_ref[low : low + half, :] = tn(
                    refs[left][:, low : low + half], refs[right][:, column : column + wide]
                ).astype(bf16)


def spread(made, first_pair, own, dp_size, me_ref, keep_ref, send_ref, columns):
    mine = me_ref[0]
    upper = lax.rem(mine, 2) == 1
    planes = keep_ref.shape[0] // own // dp_size
    mine_plane = lax.rem(lax.shift_right_logical(mine, 1), planes)
    for piece in range(made.shape[0] // (2 * own)):
        pair = first_pair + piece
        away = lax.bitwise_xor(mine_plane, pair % planes)
        place = away * dp_size + pair // planes
        span = pl.ds(pl.multiple_of(place * own, own), own)
        one = made[2 * own * piece : 2 * own * piece + own]
        two = made[2 * own * piece + own : 2 * own * (piece + 1)]
        keep_ref[span, columns] = jnp.where(upper, two, one)
        send_ref[span, columns] = jnp.where(upper, one, two)


def small_grads_kernel(one_ref, two_ref, three_ref, cross_ref, self_ref, hidden_ref, rows_ref):
    rows_ref[...] = jnp.zeros_like(rows_ref)
    places = [(GAIN, one_ref, 0), (GAIN + 1, two_ref, 0), (GAIN + 2, three_ref, 0)]
    places += [(SHIFT, one_ref, 1), (SHIFT + 1, two_ref, 1), (SHIFT + 2, three_ref, 1)]
    places += [(BIAS, self_ref, 0), (BIAS + 1, self_ref, 1), (BIAS + 2, two_ref, 3), (BIAS + 3, cross_ref, 0)]
    places += [(BIAS + 4, cross_ref, 1), (BIAS + 5, three_ref, 3), (BIAS + 6, three_ref, 2)]
    for at, ref, row in places:
        rows_ref[at : at + 1, :] = ref[row : row + 1, :]
    for step in range(hidden_ref.shape[0]):
        rows_ref[HIDDEN_BIAS + step : HIDDEN_BIAS + step + 1, :] = hidden_ref[step, 0:1, :]


def small_grads(*sums):
    width = sums[0].shape[1]
    return pl.pallas_call(
        small_grads_kernel,
        out_shape=out((24, width), f32),
        compiler_params=params(),
        name="small_grads",
    )(*sums)


def split_grads_kernel(picks, dp_size, own, count, me_ref, *refs):
    step = pl.program_id(0)
    keep_ref, send_ref = refs[count : count + 2]
    held_refs, sems = refs[count + 2 : -1], refs[-1]
    half, wide = keep_ref.shape
    copies = [pltpu.make_async_copy(refs[i], held_refs[i], sems.at[i]) for i in range(count)]

    @pl.when(step == 0)
    def _():
        for copy in copies:
            copy.start()

    known = set()
    for at, (left, right, column) in enumerate(picks):
        fresh = sorted({left, right} - known)
        known.update(fresh)

        @pl.when(step == at)
        def _(left=left, right=right, column=column, fresh=fresh):
            for i in fresh:
                copies[i].wait()
            for low in (0, half):
                made = tn(held_refs[left][:, low : low + half], held_refs[right][:, column : column + wide])
                first_pair = low // (2 * own)
                spread(made.astype(bf16), first_pair, own, dp_size, me_ref, keep_ref, send_ref, slice(0, wide))


def weight_grads(pairs, split=None, waits=(), wide=1024):
    arrays, picks = [], []
    for left, right in pairs:
        at = []
        for array in (left, right):
            known = [i for i, other in enumerate(arrays) if other is array]
            if not known:
                arrays.append(array)
            at.append(known[0] if known else len(arrays) - 1)
        picks += [(at[0], at[1], column) for column in range(0, right.shape[1], wide)]
    width = pairs[0][0].shape[1]
    columns = sum(right.shape[1] for _, right in pairs)
    flops = sum(2 * left.shape[0] * width * right.shape[1] for left, right in pairs)
    nbytes = 2 * sum(a.size for a in arrays) + 2 * width * columns
    if split is None:
        return pl.pallas_call(
            functools.partial(weight_grads_kernel, tuple(picks)),
            grid=(len(picks),),
            in_specs=[held(array.shape) for array in arrays],
            out_specs=pl.BlockSpec((width, wide), lambda j: (0, j)),
            out_shape=out((width, columns), bf16),
            compiler_params=params(),
            cost_estimate=cost(flops, nbytes),
            name="weight_grads",
        )(*arrays)
    mine, dp_size, own = split
    half = pl.BlockSpec((width // 2, wide), lambda j: (0, j))
    kernel, in_specs = after(
        waits,
        functools.partial(split_grads_kernel, tuple(picks), dp_size, own, len(arrays)),
        [pl.BlockSpec(memory_space=pltpu.SMEM)] + [pl.BlockSpec(memory_space=pl.ANY)] * len(arrays),
    )
    return pl.pallas_call(
        kernel,
        grid=(len(picks),),
        in_specs=in_specs,
        out_specs=[half, half],
        out_shape=[out((width // 2, columns), bf16)] * 2,
        scratch_shapes=[pltpu.VMEM(array.shape, bf16) for array in arrays]
        + [pltpu.SemaphoreType.DMA((len(arrays),))],
        compiler_params=params(),
        cost_estimate=cost(flops, nbytes),
        name="weight_grads_by_distance",
    )(*waits, mine, *arrays)


def near_kernel(*refs):
    whole_ref = refs[-1]
    rows = refs[0].shape[0]
    for at, ref in enumerate(refs[:-1]):
        whole_ref[at * rows : (at + 1) * rows] = ref[...]


def near_rows(pieces, waits=()):
    rows, own, columns = pieces[0].shape
    lanes = 1024
    block = pl.BlockSpec((rows, own, lanes), lambda j: (0, 0, j))
    kernel, in_specs = after(waits, near_kernel, [block] * len(pieces))
    return pl.pallas_call(
        kernel,
        grid=(columns // lanes,),
        in_specs=in_specs,
        out_specs=pl.BlockSpec((len(pieces) * rows, own, lanes), lambda j: (0, 0, j)),
        out_shape=out((len(pieces) * rows, own, columns), bf16),
        compiler_params=params(),
        cost_estimate=cost(0, 4 * len(pieces) * rows * own * columns),
        name="near_rows",
    )(*waits, *pieces)


def place_kernel(dp_size, me_ref, near_ref, far_ref, whole_ref):
    pairs, own = near_ref.shape[:2]
    planes = pairs // dp_size
    mine = me_ref[0]
    side = lax.rem(mine, 2)
    mine_pair = lax.shift_right_logical(mine, 1)
    for at in range(pairs):
        pair = lax.bitwise_xor(mine_pair, at % dp_size * planes + at // dp_size)
        for ref, core in ((near_ref, side), (far_ref, 1 - side)):
            rows = pl.ds(pl.multiple_of((2 * pair + core) * own, own), own)
            whole_ref[rows, :] = ref[at]


def place(mine, near, far, dp_size):
    pairs, own, columns = near.shape
    lanes = 1024
    block = pl.BlockSpec((pairs, own, lanes), lambda j: (0, 0, j))
    return pl.pallas_call(
        functools.partial(place_kernel, dp_size),
        grid=(columns // lanes,),
        in_specs=[pl.BlockSpec(memory_space=pltpu.SMEM), block, block],
        out_specs=pl.BlockSpec((2 * pairs * own, lanes), lambda j: (0, j)),
        out_shape=out((2 * pairs * own, columns), bf16),
        compiler_params=params(),
        cost_estimate=cost(0, 8 * pairs * own * columns),
        name="place_by_device",
    )(mine, near, far)


def feed_own_kernel(*refs):
    owned, (inner_ref, outer_ref) = refs[:-2], refs[-2:]
    own, width = owned[0].shape[0], outer_ref.shape[1]
    tiles = [
        (ref, at * width) for ref in owned for at in range(0, ref.shape[1] // width, 2)
    ]
    for step, (ref, at) in enumerate(tiles):
        outer_ref[step * own : (step + 1) * own, :] = ref[:, at + width : at + 2 * width].astype(f32)
    for device in range(width // own):
        pieces = [ref[:, at + device * own : at + (device + 1) * own].astype(f32) for ref, at in tiles]
        span = len(tiles) * own
        inner_ref[:, device * span : (device + 1) * span] = jnp.concatenate(pieces, axis=1)


def feed_own_grads(owned, width, waits=()):
    own = owned[0].shape[0]
    steps = sum(part.shape[1] for part in owned) // (2 * width)
    vmem = pl.BlockSpec(memory_space=pltpu.VMEM)
    kernel, in_specs = after(waits, feed_own_kernel, [vmem] * len(owned))
    return pl.pallas_call(
        kernel,
        in_specs=in_specs,
        out_shape=[out((own, steps * width), f32), out((steps * own, width), f32)],
        compiler_params=params(),
        name="feed_own_grads",
    )(*waits, *owned)


def cut_kernel(cuts, whole_ref, *outs):
    for ref, (low, high) in zip(outs, cuts):
        ref[...] = whole_ref[:, low:high].astype(f32)


def cut_columns(whole, ends, waits=()):
    cuts = tuple(zip(ends[:-1], ends[1:]))
    own = whole.shape[0]
    vmem = pl.BlockSpec(memory_space=pltpu.VMEM)
    kernel, in_specs = after(waits, functools.partial(cut_kernel, cuts), [vmem])
    return pl.pallas_call(
        kernel,
        in_specs=in_specs,
        out_shape=[out((own, high - low), f32) for low, high in cuts],
        compiler_params=params(),
        name="own_columns",
    )(*waits, whole)


def plane_pieces_kernel(count, ranges, keep_ref, got_ref, *outs):
    rows = keep_ref.shape[0] // count
    for at, (low, high) in enumerate(ranges):
        for k in range(count):
            span = slice(k * rows, (k + 1) * rows)
            made = keep_ref[span, low:high].astype(f32) + got_ref[span, low:high].astype(f32)
            outs[at * count + k][...] = made.astype(bf16)


def lanes_of(columns):
    return next(n for n in (2048, 1664, 1408, 1280, 1024, 128) if columns % n == 0)


def plane_pieces(keep, got, count, waits, ends):
    rows, columns = keep.shape
    ranges = tuple(zip(ends[:-1], ends[1:]))
    if len(ranges) == 1:
        lanes = lanes_of(columns)
        steps, shapes, ranges = columns // lanes, [(columns, lanes)], ((0, lanes),)
    else:
        lanes, steps, shapes = columns, 1, [(high - low, high - low) for low, high in ranges]
    block = pl.BlockSpec((rows, lanes), lambda j: (0, j))
    kernel, in_specs = after(
        waits, functools.partial(plane_pieces_kernel, count, ranges), [block, block]
    )
    return pl.pallas_call(
        kernel,
        grid=(steps,),
        in_specs=in_specs,
        out_specs=[
            pl.BlockSpec((rows // count, n), lambda j: (0, j)) for _, n in shapes for _ in range(count)
        ],
        out_shape=[out((rows // count, n), bf16) for n, _ in shapes for _ in range(count)],
        compiler_params=params(),
        cost_estimate=cost(0, 6 * rows * columns),
        name="plane_pieces",
    )(*waits, keep, got)


def plane_total_kernel(*refs):
    total = refs[0][...].astype(f32)
    for ref in refs[1:-1]:
        total = total + ref[...].astype(f32)
    refs[-1][...] = total.astype(bf16)


def plane_total(pieces, waits=(), weight=0):
    rows, columns = pieces[0].shape
    lanes = lanes_of(columns)
    block = pl.BlockSpec((rows, lanes), lambda j: (0, j))
    kernel, in_specs = after(waits, plane_total_kernel, [block] * len(pieces))
    return pl.pallas_call(
        kernel,
        grid=(columns // lanes,),
        in_specs=in_specs,
        out_specs=block,
        out_shape=out((rows, columns), bf16),
        compiler_params=params(),
        cost_estimate=cost(weight * rows * columns, 2 * (len(pieces) + 1) * rows * columns),
        name="plane_total",
    )(*waits, *pieces)


def prepare_kernel(
    qkv_ref, out_ref, query_ref, pair_ref, cross_ref, inner_ref, outer_ref, gains_ref, shifts_ref, biases_ref, hidden_ref,
    first_ref, second_ref, third_ref,
):
    own, width = out_ref.shape
    steps = inner_ref.shape[1] // width
    devices = width // own
    rows = [gains_ref[...].astype(f32), shifts_ref[...].astype(f32), biases_ref[...].astype(f32)]
    hidden = hidden_ref[...].astype(f32)
    rows += [hidden[:, step * own : (step + 1) * own] for step in range(steps)]
    rows += [jnp.zeros((SMALL - HIDDEN_BIAS - steps, own), f32)]
    first_ref[:, : 3 * width] = qkv_ref[...]
    first_ref[:, 3 * width :] = jnp.concatenate(rows, axis=0).T.astype(bf16)
    second_ref[:, :width] = out_ref[...]
    second_ref[:, width : 2 * width] = query_ref[...]
    second_ref[:, 2 * width : 4 * width] = pair_ref[...]
    second_ref[:, 4 * width :] = cross_ref[...]
    for step in range(steps):
        pieces = [
            inner_ref[:, (device * steps + step) * own : (device * steps + step + 1) * own].astype(f32)
            for device in range(devices)
        ]
        third_ref[:, 2 * step * width : (2 * step + 1) * width] = jnp.concatenate(pieces, axis=1).astype(bf16)
        third_ref[:, (2 * step + 1) * width : (2 * step + 2) * width] = outer_ref[step * own : (step + 1) * own, :]


def prepare(*shards):
    own, width = shards[1].shape
    steps = shards[5].shape[1] // width
    return pl.pallas_call(
        prepare_kernel,
        out_shape=[
            out((own, 3 * width + SMALL), bf16),
            out((own, 5 * width), bf16),
            out((own, 2 * steps * width), bf16),
        ],
        compiler_params=params(),
        name="shards_to_gather",
    )(*shards)


AXES = ("dp", "fsdp")


def gather(shard):
    return lax.all_gather(shard, AXES, axis=0, tiled=True)


def scatter_sum(whole):
    return lax.psum_scatter(whole, AXES, scatter_dimension=0, tiled=True)


def exchange(array, axis, size, distance):
    return lax.ppermute(array, axis, [(i, i ^ distance) for i in range(size)])


def small_sum(sums, own, dp_size, fsdp_size):
    kept = sums
    for axis, size in (("fsdp", fsdp_size), ("dp", dp_size)):
        distance = 1
        while distance < size:
            kept = kept + exchange(kept, axis, size, distance)
            distance *= 2
    start = (lax.axis_index("dp") * fsdp_size + lax.axis_index("fsdp")) * own
    return lax.dynamic_slice_in_dim(kept, start, own, axis=1)


def add_low(left, right):
    return (left.astype(f32) + right.astype(f32)).astype(bf16)


def scatter_plane(keep, got, fsdp_size, waits=(), cut=()):
    planes = fsdp_size // 2
    made = list(plane_pieces(keep, got, planes, waits, (0, *cut, keep.shape[1])))
    both = [made[at : at + planes] for at in range(0, len(made), planes)]
    return [
        (part[1:], part[:1] + [exchange(part[k], "fsdp", fsdp_size, 2 * k) for k in range(1, planes)])
        for part in both
    ]


def scatter_line(total):
    return lax.psum_scatter(total, "dp", scatter_dimension=0, tiled=True)


def local(
    inputs,
    memory,
    cotangent,
    target_lengths,
    memory_lengths,
    norm_gains,
    norm_biases,
    self_qkv,
    self_out,
    cross_query,
    cross_kv,
    cross_out,
    ffn_in,
    ffn_out,
    proj_biases,
    ffn_in_bias,
):
    width = inputs.shape[2]
    own = self_qkv.shape[0]
    devices = width // own
    steps = ffn_in.shape[1] // width
    dp_size, fsdp_size = lax.axis_size("dp"), lax.axis_size("fsdp")
    by_distance = own % 16 == 0
    mine = (lax.axis_index("dp") * fsdp_size + lax.axis_index("fsdp")).astype(jnp.int32).reshape(1)
    split = (mine, dp_size, own) if by_distance else (mine,)

    if by_distance:
        first_shard, second_shard, feed_shard = prepare(
            self_qkv, self_out, cross_query, cross_kv, cross_out, ffn_in, ffn_out,
            norm_gains, norm_biases, proj_biases, ffn_in_bias.reshape(1, -1),
        )
    else:
        small = jnp.concatenate(
            [norm_gains, norm_biases, proj_biases, ffn_in_bias.reshape(steps, own)], axis=0
        )
        small = jnp.pad(small, ((0, SMALL - small.shape[0]), (0, 0))).T
        first_shard = jnp.concatenate([self_qkv, small], axis=1)
        second_shard = jnp.concatenate([self_out, cross_query, cross_kv, cross_out], axis=1)
        inner_shard = ffn_in.reshape(own, devices, steps, own).transpose(0, 2, 1, 3).reshape(own, steps, width)
        outer_shard = ffn_out.reshape(steps, own, width).transpose(1, 0, 2)
        feed_shard = jnp.concatenate([inner_shard, outer_shard], axis=2).reshape(own, 2 * steps * width)

    first = gather(first_shard)
    third = gather(feed_shard)
    x = inputs[0]
    rows = memory[0]
    branch = cotangent[0]
    waits = ()
    if by_distance:
        line = jnp.stack(
            [second_shard] + [exchange(second_shard, "dp", dp_size, k) for k in range(1, dp_size)]
        )
        plane = [exchange(line, "fsdp", fsdp_size, 2 * k) for k in range(1, fsdp_size // 2)]
        waits = (line,)
    table = first[:, 3 * width :].astype(f32).T[:24]

    normed_one, triple = entry(x, first, table, waits)
    parts = [(triple, at * (width // PAIR), width) for at in range(3)]
    self_mixed, self_stats = attend(target_lengths, *parts, True)
    if by_distance:
        near = near_rows([line] + plane, (triple,))
        second = place(mine, near, exchange(near, "fsdp", fsdp_size, 1), dp_size)
    else:
        second = gather(second_shard)
    pair = memory_pair(rows, second, table)
    hidden_one, normed_two, queries = middle(x, self_mixed, second, table)
    cross_parts = [(queries, 0, width), (pair, 0, width), (pair, width // PAIR, width)]
    cross_mixed, cross_stats = attend(memory_lengths, *cross_parts, False)
    hidden_two, normed_three = late(hidden_one, cross_mixed, second, table)
    made, back, hidden_bias_sums, *feed_grads = feed(normed_three, branch, third, table, split)
    grad_two, branch_two, mixed_grad, sums_three = turn(hidden_two, back, branch, second, table)
    waits = ()
    if by_distance:
        feed_got = exchange(feed_grads[1], "fsdp", fsdp_size, 1)
        [(feed_sent, feed_plane)] = scatter_plane(feed_grads[0], feed_got, fsdp_size, (sums_three,))
        waits = tuple(feed_sent)
    else:
        feed_own = scatter_sum(feed_grads[0])
    query_grad, key_grad, value_grad, cross_sums = attend_back(
        memory_lengths, *cross_parts, cross_mixed, mixed_grad, cross_stats, False, waits
    )
    cross_pairs = [
        (cross_mixed, branch_two),
        (normed_two, query_grad),
        (rows, key_grad),
        (rows, value_grad),
    ]
    waits = ()
    if by_distance:
        cross_keep, cross_send = weight_grads(cross_pairs, split)
        cross_got = exchange(cross_send, "fsdp", fsdp_size, 1)
        waits = (cross_send,)
    grad_one, branch_one, mixed_grad, sums_two = middle_back(
        hidden_one, grad_two, query_grad, second, table, waits
    )
    if by_distance:
        [(cross_sent, cross_plane)] = scatter_plane(cross_keep, cross_got, fsdp_size, (grad_one,))
        waits = tuple(cross_sent)
    *self_grads, self_sums = attend_back(
        target_lengths, *parts, self_mixed, mixed_grad, self_stats, True, waits
    )
    self_pairs = [(self_mixed, branch_one)] + [(normed_one, part) for part in self_grads]
    waits = ()
    if by_distance:
        feed_total = plane_total(feed_plane, (self_sums,))
        feed_own = scatter_line(feed_total)
        self_keep, self_send = weight_grads(self_pairs, split, (feed_total,))
        self_got = exchange(self_send, "fsdp", fsdp_size, 1)
        memory_grad = memory_back(key_grad, value_grad, second, (self_send,))
        [(self_sent, self_plane)] = scatter_plane(self_keep, self_got, fsdp_size, (memory_grad,))
        cross_total = plane_total(cross_plane, (self_sent[0],))
        cross_own = scatter_line(cross_total)
        waits = (*self_sent, cross_total)
    input_grad, sums_one = entry_back(x, grad_one, self_grads, first, table, waits)
    sums = small_grads(sums_one, sums_two, sums_three, cross_sums, self_sums, hidden_bias_sums)
    if by_distance:
        result = layer_result(hidden_two, made, table, (input_grad,))
        inner_own, outer_own = feed_own_grads([feed_own], width, (result,))
        cross_out_own, query_own, pair_own = cut_columns(
            cross_own, (0, width, 2 * width, 4 * width), (inner_own,)
        )
        self_total = plane_total(self_plane, (cross_out_own,))
        self_own = scatter_line(self_total)
        self_out_own, triple_own = cut_columns(self_own, (0, width, 4 * width))
    else:
        result = layer_result(hidden_two, made, table)
        memory_grad = memory_back(key_grad, value_grad, second)
        cross_own = scatter_sum(weight_grads(cross_pairs)).astype(f32)
        cross_out_own, query_own = cross_own[:, :width], cross_own[:, width : 2 * width]
        pair_own = cross_own[:, 2 * width :]
        self_own = scatter_sum(weight_grads(self_pairs)).astype(f32)
        self_out_own, triple_own = self_own[:, :width], self_own[:, width:]
        feed_own = feed_own.astype(f32).reshape(own, steps, 2, width)
        inner_own = feed_own[:, :, 0].reshape(own, steps, devices, own).transpose(0, 2, 1, 3)
        inner_own = inner_own.reshape(own, steps * width)
        outer_own = feed_own[:, :, 1].transpose(1, 0, 2).reshape(steps * own, width)
    small_own = small_sum(sums, own, dp_size, fsdp_size)
    return (
        result[None],
        input_grad[None],
        memory_grad[None],
        small_own[GAIN:SHIFT],
        small_own[SHIFT:BIAS],
        triple_own,
        self_out_own,
        query_own,
        pair_own,
        cross_out_own,
        inner_own,
        outer_own,
        small_own[BIAS:HIDDEN_BIAS],
        small_own[HIDDEN_BIAS : HIDDEN_BIAS + steps].reshape(steps * own),
    )


def solution(mesh):
    rows = P(AXES, None, None)
    lengths = P(AXES)
    split = P(AXES, None)
    features = P(None, AXES)
    return jax.shard_map(
        local,
        mesh=mesh,
        in_specs=(rows, rows, rows, lengths, lengths, features, features)
        + (split,) * 7
        + (features, lengths),
        out_specs=(rows, rows, rows, features, features) + (split,) * 7 + (features, lengths),
        check_vma=False,
    )
```

```python
import functools

import jax
import jax.numpy as jnp
from jax import lax
from jax.experimental import pallas as pl
from jax.experimental.pallas import tpu as pltpu
from jax.sharding import PartitionSpec as P

f32 = jnp.float32
bf16 = jnp.bfloat16

HEAD = 64
PAIR = 2 * HEAD
BLOCK = 256
ROWS = 256
SMALL = 128
eps_norm = 1e-05
masked_score = -1e30
gelu_slope = 0.7978845608028654
gelu_cubic = 0.044715
MiB = 1 << 20


def nn(left, right):
    return jnp.dot(left, right, preferred_element_type=f32)


def nt(left, right):
    return lax.dot_general(left, right, (((1,), (1,)), ((), ())), preferred_element_type=f32)


def tn(left, right):
    return lax.dot_general(left, right, (((0,), (0,)), ((), ())), preferred_element_type=f32)


def normalise(hidden):
    centred = hidden - jnp.mean(hidden, axis=-1, keepdims=True)
    spread = lax.rsqrt(jnp.mean(centred * centred, axis=-1, keepdims=True) + eps_norm)
    return centred * spread, spread


def norm_back(hidden, incoming, gain):
    normed, spread = normalise(hidden)
    scaled = incoming * gain
    part = spread * (
        scaled
        - jnp.mean(scaled, axis=-1, keepdims=True)
        - normed * jnp.mean(scaled * normed, axis=-1, keepdims=True)
    )
    gain_grad = jnp.sum(incoming * normed, axis=0, keepdims=True)
    shift_grad = jnp.sum(incoming, axis=0, keepdims=True)
    return part, gain_grad, shift_grad


def column_sum(gradient):
    return jnp.sum(gradient.astype(f32), axis=0, keepdims=True)


def params():
    return pltpu.CompilerParams(vmem_limit_bytes=60 * MiB)


def after(waits, kernel, in_specs):
    count = len(waits)

    def waiting(*refs):
        kernel(*refs[count:])

    return waiting, [pl.BlockSpec(memory_space=pl.ANY)] * count + in_specs


def cost(flops, nbytes, transcendentals=0, high=64):
    return pl.CostEstimate(
        flops=high * flops, bytes_accessed=high * nbytes, transcendentals=high * transcendentals
    )


def held(shape, at=None):
    place = (0,) * len(shape) if at is None else at
    return pl.BlockSpec(shape, lambda j: place, pipeline_mode=pl.Buffered(1))


def by_rows(shape):
    return pl.BlockSpec(shape, lambda j: (j, 0))


def out(shape, dtype):
    return jax.ShapeDtypeStruct(shape, dtype)


GAIN, SHIFT, BIAS, HIDDEN_BIAS = 0, 3, 6, 13


def row_of(table_ref, at):
    return table_ref[at : at + 1, :]


def entry_kernel(x_ref, weight_ref, table_ref, normed_ref, triple_ref):
    width = x_ref.shape[1]
    normed, _ = normalise(x_ref[...].astype(f32))
    low = (normed * row_of(table_ref, GAIN) + row_of(table_ref, SHIFT)).astype(bf16)
    normed_ref[...] = low
    for part in range(3):
        span = slice(part * width, (part + 1) * width)
        made = nn(low, weight_ref[:, span])
        if part == 0:
            made = made + row_of(table_ref, BIAS)
        if part == 2:
            made = made + row_of(table_ref, BIAS + 1)
        triple_ref[:, span] = made.astype(bf16)


def entry(x, weights, table, waits=()):
    tokens, width = x.shape
    kernel, in_specs = after(
        waits, entry_kernel, [by_rows((ROWS, width)), held(weights.shape), held(table.shape)]
    )
    return pl.pallas_call(
        kernel,
        grid=(tokens // ROWS,),
        in_specs=in_specs,
        out_specs=[by_rows((ROWS, width)), by_rows((ROWS, 3 * width))],
        out_shape=[out((tokens, width), bf16), out((tokens, 3 * width), bf16)],
        compiler_params=params(),
        cost_estimate=cost(6 * tokens * width * width, 10 * tokens * width + 6 * width * width, 0, 1),
        name="norm_and_qkv",
    )(*waits, x, weights, table)


def middle_kernel(x_ref, mixed_ref, out_ref, query_ref, table_ref, hidden_ref, normed_ref, made_ref):
    hidden = x_ref[...].astype(f32) + nn(mixed_ref[...], out_ref[...]) + row_of(table_ref, BIAS + 2)
    hidden_ref[...] = hidden
    normed, _ = normalise(hidden)
    low = (normed * row_of(table_ref, GAIN + 1) + row_of(table_ref, SHIFT + 1)).astype(bf16)
    normed_ref[...] = low
    made_ref[...] = (nn(low, query_ref[...]) + row_of(table_ref, BIAS + 3)).astype(bf16)


def middle(x, mixed, weights, table):
    tokens, width = x.shape
    block = by_rows((ROWS, width))
    return pl.pallas_call(
        middle_kernel,
        grid=(tokens // ROWS,),
        in_specs=[
            block,
            block,
            held((width, width), (0, 0)),
            held((width, width), (0, 1)),
            held(table.shape),
        ],
        out_specs=[block, block, block],
        out_shape=[out((tokens, width), f32), out((tokens, width), bf16), out((tokens, width), bf16)],
        compiler_params=params(),
        cost_estimate=cost(4 * tokens * width * width, 12 * tokens * width + 4 * width * width, 0, 1),
        name="self_out_norm_query",
    )(x, mixed, weights, weights, table)


def memory_kernel(memory_ref, weight_ref, table_ref, pair_ref):
    width = memory_ref.shape[1]
    rows = memory_ref[...]
    pair_ref[:, :width] = nn(rows, weight_ref[:, :width]).astype(bf16)
    pair_ref[:, width:] = (nn(rows, weight_ref[:, width:]) + row_of(table_ref, BIAS + 4)).astype(bf16)


def memory_pair(memory, weights, table):
    tokens, width = memory.shape
    return pl.pallas_call(
        memory_kernel,
        grid=(tokens // ROWS,),
        in_specs=[by_rows((ROWS, width)), held((width, 2 * width), (0, 1)), held(table.shape)],
        out_specs=by_rows((ROWS, 2 * width)),
        out_shape=out((tokens, 2 * width), bf16),
        compiler_params=params(),
        cost_estimate=cost(4 * tokens * width * width, 6 * tokens * width + 4 * width * width, 0, 1),
        name="memory_keys_values",
    )(memory, weights, table)


def late_kernel(hidden_ref, mixed_ref, out_ref, table_ref, next_ref, normed_ref):
    hidden = hidden_ref[...] + nn(mixed_ref[...], out_ref[...]) + row_of(table_ref, BIAS + 5)
    next_ref[...] = hidden
    normed, _ = normalise(hidden)
    normed_ref[...] = (normed * row_of(table_ref, GAIN + 2) + row_of(table_ref, SHIFT + 2)).astype(bf16)


def late(hidden, mixed, weights, table):
    tokens, width = hidden.shape
    block = by_rows((ROWS, width))
    return pl.pallas_call(
        late_kernel,
        grid=(tokens // ROWS,),
        in_specs=[block, block, held((width, width), (0, 4)), held(table.shape)],
        out_specs=[block, block],
        out_shape=[out((tokens, width), f32), out((tokens, width), bf16)],
        compiler_params=params(),
        cost_estimate=cost(2 * tokens * width * width, 12 * tokens * width + 2 * width * width, 0, 1),
        name="cross_out_norm",
    )(hidden, mixed, weights, table)


def head_operands(lane, side, query, key, key_bias):
    own = (lane < HEAD) if side == 0 else (lane >= HEAD)
    spare = lane == (HEAD if side == 0 else 0)
    zero = jnp.zeros((), bf16)
    query_own = jnp.where(own, query, zero)
    key_own = jnp.where(own, key, zero)
    query_wide = jnp.where(spare, jnp.ones((), bf16), query_own)
    key_wide = jnp.where(spare, key_bias, key_own)
    return own, query_own, query_wide, key_own, key_wide


def pair_operands(length_ref, query_ref, key_ref):
    lane = lax.broadcasted_iota(jnp.int32, (1, PAIR), 1)
    key_pos = lax.broadcasted_iota(jnp.int32, (key_ref.shape[0], 1), 0)
    key_bias = jnp.where(key_pos < length_ref[0], 0.0, masked_score).astype(bf16)
    query = query_ref[...] * jnp.asarray(HEAD**-0.5, bf16)
    key = key_ref[...]
    return lane, [head_operands(lane, side, query, key, key_bias) for side in (0, 1)]


def scores_by_key(key_wide, query_block, keys, allowed):
    scores = nt(key_wide[:keys], query_block)
    if allowed is None:
        return scores
    last = jnp.where(allowed, scores[keys - BLOCK :], masked_score)
    return last if keys == BLOCK else jnp.concatenate([scores[: keys - BLOCK], last], axis=0)


def causal_block():
    key = lax.broadcasted_iota(jnp.int32, (BLOCK, BLOCK), 0)
    query = lax.broadcasted_iota(jnp.int32, (BLOCK, BLOCK), 1)
    return key <= query


def attend_kernel(causal, length_ref, query_ref, key_ref, value_ref, mixed_ref, stat_ref):
    rows, keys_all = query_ref.shape[0], key_ref.shape[0]
    lane, heads = pair_operands(length_ref, query_ref, key_ref)
    value = value_ref[...]
    allowed = causal_block() if causal else None
    first = lane < HEAD
    value_wide = [jnp.where(heads[side][0], value, jnp.ones((), bf16)) for side in (0, 1)]
    for at in range(0, rows, BLOCK):
        keys = at + BLOCK if causal else keys_all
        got, tops = [], []
        for side in (0, 1):
            _, _, query_wide, _, key_wide = heads[side]
            scores = scores_by_key(key_wide, query_wide[at : at + BLOCK], keys, allowed)
            top = jnp.max(scores, axis=0, keepdims=True)
            exponent = jnp.exp(scores - top)
            got.append(tn(exponent.astype(bf16), value_wide[side][:keys]))
            tops.append(top)
        total = jnp.where(first, got[1], got[0])
        mixed = jnp.where(first, got[0], got[1]) / pltpu.roll(total, HEAD, 1)
        mixed_ref[at : at + BLOCK, :] = mixed.astype(bf16)
        logs = jnp.log(total).T
        stat_ref[0, 0:1, at : at + BLOCK] = tops[0] + logs[HEAD : HEAD + 1]
        stat_ref[0, 1:2, at : at + BLOCK] = tops[1] + logs[0:1]


def pair_block(rows, column=0):
    return pl.BlockSpec((rows, PAIR), lambda j: (0, column + j))


def attend(lengths, query, key, value, causal):
    rows, keys, width = query[0].shape[0], key[0].shape[0], query[2]
    pairs = width // PAIR
    return pl.pallas_call(
        functools.partial(attend_kernel, causal),
        grid=(pairs,),
        in_specs=[
            pl.BlockSpec(memory_space=pltpu.SMEM),
            pair_block(rows, query[1]),
            pair_block(keys, key[1]),
            pair_block(keys, value[1]),
        ],
        out_specs=[pair_block(rows), pl.BlockSpec((1, 2, rows), lambda j: (j, 0, 0))],
        out_shape=[out((rows, width), bf16), out((pairs, 2, rows), f32)],
        compiler_params=params(),
        cost_estimate=cost(16 * rows * keys * width, 4 * (rows + keys) * width, 16 * rows * keys, 1),
        name="attend_causal" if causal else "attend_memory",
    )(lengths, query[0], key[0], value[0])


def attend_back_kernel(
    causal,
    length_ref,
    query_ref,
    key_ref,
    value_ref,
    mixed_ref,
    grad_ref,
    stat_ref,
    query_grad_ref,
    key_grad_ref,
    value_grad_ref,
    sums_ref,
    key_sum,
    value_sum,
):
    rows, keys_all = query_ref.shape[0], key_ref.shape[0]
    scale = HEAD**-0.5
    lane, heads = pair_operands(length_ref, query_ref, key_ref)
    value = value_ref[...]
    grad = grad_ref[...]
    inner = (grad.astype(f32) * mixed_ref[...].astype(f32)).T
    allowed = causal_block() if causal else None
    zero = jnp.zeros((), bf16)
    value_own = [jnp.where(heads[side][0], value, zero) for side in (0, 1)]
    grad_own = [jnp.where(heads[side][0], grad, zero) for side in (0, 1)]
    inner_sum = [
        jnp.sum(inner[side * HEAD : (side + 1) * HEAD], axis=0, keepdims=True) for side in (0, 1)
    ]
    block = BLOCK if causal else rows
    for at in range(rows - block, -1, -block):
        keys = at + block if causal else keys_all
        span = slice(at, at + block)
        sums = None
        for side in (0, 1):
            _, query_own, query_wide, key_own, key_wide = heads[side]
            scores = scores_by_key(key_wide, query_wide[span], keys, allowed)
            probs = jnp.exp(scores - stat_ref[0, side : side + 1, span])
            grad_probs = nt(value_own[side][:keys], grad[span])
            grad_scores = (probs * (grad_probs - inner_sum[side][:, span])).astype(bf16)
            parts = (
                tn(grad_scores, key_own[:keys]),
                nn(grad_scores, query_own[span]),
                nn(probs.astype(bf16), grad_own[side][span]),
            )
            sums = parts if sums is None else tuple(a + b for a, b in zip(sums, parts))
        query_low = (sums[0] * scale).astype(bf16)
        query_grad_ref[span, :] = query_low
        query_total = column_sum(query_low) + (0.0 if at == rows - block else query_total)
        if at == rows - block:
            key_sum[...] = sums[1]
            value_sum[...] = sums[2]
        else:
            key_sum[:keys] += sums[1]
            value_sum[:keys] += sums[2]
    key_grad_ref[...] = key_sum[...].astype(bf16)
    value_low = value_sum[...].astype(bf16)
    value_grad_ref[...] = value_low
    sums_ref[...] = jnp.zeros_like(sums_ref)
    sums_ref[0:1, :] = query_total
    sums_ref[1:2, :] = column_sum(value_low)


def attend_back(lengths, query, key, value, mixed, grad, stats, causal, waits=(), share=(0, 1)):
    rows, keys = query[0].shape[0], key[0].shape[0]
    pairs = query[2] // PAIR // share[1]
    first, width = share[0] * pairs, pairs * PAIR
    kernel, in_specs = after(
        waits,
        functools.partial(attend_back_kernel, causal),
        [
            pl.BlockSpec(memory_space=pltpu.SMEM),
            pair_block(rows, query[1] + first),
            pair_block(keys, key[1] + first),
            pair_block(keys, value[1] + first),
            pair_block(rows, first),
            pair_block(rows, first),
            pl.BlockSpec((1, 2, rows), lambda j: (first + j, 0, 0)),
        ],
    )
    return pl.pallas_call(
        kernel,
        grid=(pairs,),
        in_specs=in_specs,
        out_specs=[pair_block(rows), pair_block(keys), pair_block(keys), pair_block(8)],
        out_shape=[
            out((rows, width), bf16),
            out((keys, width), bf16),
            out((keys, width), bf16),
            out((8, width), f32),
        ],
        scratch_shapes=[pltpu.VMEM((keys, PAIR), f32), pltpu.VMEM((keys, PAIR), f32)],
        compiler_params=params(),
        cost_estimate=cost(24 * rows * keys * width, 8 * (rows + keys) * width, 16 * rows * keys),
        name="attend_causal_back" if causal else "attend_memory_back",
    )(*waits, lengths, query[0], key[0], value[0], mixed, grad, stats)


FEED_ROWS = 512


def feed_kernel(
    split, me_ref, normed_ref, branch_ref, weight_ref, table_ref, made_ref, back_ref, bias_ref, *refs
):
    turned, act, dact = refs[-3:]
    step = pl.program_id(0)
    tokens, width = normed_ref.shape

    @pl.when(step == 0)
    def _():
        made_ref[...] = jnp.zeros_like(made_ref)
        back_ref[...] = jnp.zeros_like(back_ref)
        turned[...] = normed_ref[...].T

    bias = table_ref[pl.ds(HIDDEN_BIAS + step, 1), :]
    bias_sum = jnp.zeros((1, width), f32)
    for at in range(0, tokens, FEED_ROWS):
        span = slice(at, at + FEED_ROWS)
        inner = nn(normed_ref[span, :], weight_ref[:, :width]) + bias
        grad_active = nt(branch_ref[span, :], weight_ref[:, width:])
        square = inner * inner
        bent = jnp.tanh(inner * (gelu_slope + (gelu_slope * gelu_cubic) * square))
        half = 0.5 + 0.5 * bent
        active = (inner * half).astype(bf16)
        slope = half + (0.5 * inner) * (1.0 - bent * bent) * (
            gelu_slope + (3.0 * gelu_slope * gelu_cubic) * square
        )
        grad_inner = (grad_active * slope).astype(bf16)
        act[span, :] = active
        dact[span, :] = grad_inner
        bias_sum += column_sum(grad_inner)
        made_ref[span, :] += nn(active, weight_ref[:, width:])
        back_ref[span, :] += nt(grad_inner, weight_ref[:, :width])
    bias_ref[0] = jnp.broadcast_to(bias_sum, bias_ref.shape[1:])
    for at in range(0, width, FEED_ROWS):
        span = slice(at, at + FEED_ROWS)
        inner_part = nn(turned[span, :], dact[...]).astype(bf16)
        outer_part = tn(act[:, span], branch_ref[...]).astype(bf16)
        for part, columns in ((inner_part, slice(0, width)), (outer_part, slice(width, 2 * width))):
            if split is None:
                refs[0][span, columns] = part
            else:
                dp_size, own = split
                spread(part, at // (2 * own), own, dp_size, me_ref, refs[0], refs[1], columns)


def feed(normed, branch, weights, table, split):
    tokens, width = normed.shape
    steps = weights.shape[1] // (2 * width)
    hidden = steps * width
    whole = pl.BlockSpec((tokens, width), lambda j: (0, 0))
    tile = pl.BlockSpec((width, 2 * width), lambda j: (0, j))
    if split[1:]:
        grad_specs = [pl.BlockSpec((width // 2, 2 * width), lambda j: (0, j))] * 2
        grad_shapes = [out((width // 2, 2 * hidden), bf16)] * 2
    else:
        grad_specs, grad_shapes = [tile], [out((width, 2 * hidden), bf16)]
    return pl.pallas_call(
        functools.partial(feed_kernel, split[1:] or None),
        grid=(steps,),
        in_specs=[
            pl.BlockSpec(memory_space=pltpu.SMEM),
            held((tokens, width)),
            held((tokens, width)),
            tile,
            held(table.shape),
        ],
        out_specs=[whole, whole, pl.BlockSpec((1, 8, width), lambda j: (j, 0, 0))] + grad_specs,
        out_shape=[
            out((tokens, width), f32),
            out((tokens, width), f32),
            out((steps, 8, width), f32),
        ]
        + grad_shapes,
        scratch_shapes=[
            pltpu.VMEM((width, tokens), bf16),
            pltpu.VMEM((tokens, width), bf16),
            pltpu.VMEM((tokens, width), bf16),
        ],
        compiler_params=params(),
        cost_estimate=cost(
            12 * tokens * width * hidden, 8 * width * hidden + 12 * tokens * width, tokens * hidden
        ),
        name="feed_forward_both_ways",
    )(split[0], normed, branch, weights, table)


def add_rows(ref, rows):
    @pl.when(pl.program_id(0) == 0)
    def _():
        ref[...] = jnp.zeros_like(ref)

    for at, row in rows:
        ref[at : at + 1, :] += row


def turn_kernel(
    hidden_ref, back_ref, cotangent_ref, out_ref, table_ref, grad_ref, branch_ref, mixed_grad_ref, sums_ref
):
    low_in = cotangent_ref[...]
    part, gain_grad, shift_grad = norm_back(hidden_ref[...], back_ref[...], row_of(table_ref, GAIN + 2))
    grad = low_in.astype(f32) + part
    grad_ref[...] = grad
    low = grad.astype(bf16)
    branch_ref[...] = low
    mixed_grad_ref[...] = nt(low, out_ref[...]).astype(bf16)
    add_rows(
        sums_ref,
        ((0, gain_grad), (1, shift_grad), (2, column_sum(low_in)), (3, column_sum(low))),
    )


def turn(hidden, back, cotangent, weights, table):
    tokens, width = hidden.shape
    block = by_rows((ROWS, width))
    return pl.pallas_call(
        turn_kernel,
        grid=(tokens // ROWS,),
        in_specs=[block, block, block, held((width, width), (0, 4)), held(table.shape)],
        out_specs=[block, block, block, pl.BlockSpec((8, width), lambda j: (0, 0))],
        out_shape=[
            out((tokens, width), f32),
            out((tokens, width), bf16),
            out((tokens, width), bf16),
            out((8, width), f32),
        ],
        compiler_params=params(),
        cost_estimate=cost(2 * tokens * width * width, 18 * tokens * width + 2 * width * width),
        name="norm_back_cross_out_back",
    )(hidden, back, cotangent, weights, table)


def result_kernel(hidden_ref, made_ref, table_ref, result_ref):
    result_ref[...] = (hidden_ref[...] + made_ref[...] + row_of(table_ref, BIAS + 6)).astype(bf16)


def layer_result(hidden, made, table, waits=()):
    tokens, width = hidden.shape
    block = by_rows((ROWS, width))
    kernel, in_specs = after(waits, result_kernel, [block, block, held(table.shape)])
    return pl.pallas_call(
        kernel,
        grid=(tokens // ROWS,),
        in_specs=in_specs,
        out_specs=block,
        out_shape=out((tokens, width), bf16),
        compiler_params=params(),
        cost_estimate=cost(0, 10 * tokens * width),
        name="layer_result",
    )(*waits, hidden, made, table)


def middle_back_kernel(
    hidden_ref, grad_ref, query_grad_ref, query_ref, out_ref, table_ref,
    next_ref, branch_ref, mixed_grad_ref, sums_ref,
):
    incoming = nt(query_grad_ref[...], query_ref[...])
    part, gain_grad, shift_grad = norm_back(hidden_ref[...], incoming, row_of(table_ref, GAIN + 1))
    grad = grad_ref[...] + part
    next_ref[...] = grad
    low = grad.astype(bf16)
    branch_ref[...] = low
    mixed_grad_ref[...] = nt(low, out_ref[...]).astype(bf16)
    add_rows(
        sums_ref,
        ((0, gain_grad), (1, shift_grad), (3, column_sum(low))),
    )


def middle_back(hidden, grad, query_grad, weights, table, waits=()):
    tokens, width = hidden.shape
    block = by_rows((ROWS, width))
    kernel, in_specs = after(
        waits,
        middle_back_kernel,
        [
            block,
            block,
            block,
            held((width, width), (0, 1)),
            held((width, width), (0, 0)),
            held(table.shape),
        ],
    )
    return pl.pallas_call(
        kernel,
        grid=(tokens // ROWS,),
        in_specs=in_specs,
        out_specs=[block, block, block, pl.BlockSpec((8, width), lambda j: (0, 0))],
        out_shape=[
            out((tokens, width), f32),
            out((tokens, width), bf16),
            out((tokens, width), bf16),
            out((8, width), f32),
        ],
        compiler_params=params(),
        cost_estimate=cost(4 * tokens * width * width, 20 * tokens * width + 4 * width * width),
        name="query_norm_back_self_out_back",
    )(*waits, hidden, grad, query_grad, weights, weights, table)


def entry_back_kernel(x_ref, grad_ref, weight_ref, table_ref, *refs):
    grads, (input_grad_ref, sums_ref) = refs[:-2], refs[-2:]
    incoming, at = 0.0, 0
    for ref in grads:
        columns = ref.shape[1]
        incoming += nt(ref[...], weight_ref[:, at : at + columns])
        at += columns
    part, gain_grad, shift_grad = norm_back(x_ref[...].astype(f32), incoming, row_of(table_ref, GAIN))
    input_grad_ref[...] = grad_ref[...] + part
    add_rows(sums_ref, ((0, gain_grad), (1, shift_grad)))


def entry_back(x, grad, grads, weights, table, waits=()):
    tokens, width = x.shape
    block = by_rows((ROWS, width))
    kernel, in_specs = after(
        waits,
        entry_back_kernel,
        [block, block, held(weights.shape), held(table.shape)]
        + [by_rows((ROWS, part.shape[1])) for part in grads],
    )
    return pl.pallas_call(
        kernel,
        grid=(tokens // ROWS,),
        in_specs=in_specs,
        out_specs=[block, pl.BlockSpec((8, width), lambda j: (0, 0))],
        out_shape=[out((tokens, width), f32), out((8, width), f32)],
        compiler_params=params(),
        cost_estimate=cost(6 * tokens * width * width, 16 * tokens * width + 6 * width * width),
        name="qkv_norm_back",
    )(*waits, x, grad, weights, table, *grads)


def memory_back_kernel(key_grad_ref, value_grad_ref, weight_ref, memory_grad_ref):
    width = key_grad_ref.shape[1]
    made = nt(key_grad_ref[...], weight_ref[:, :width])
    memory_grad_ref[...] = made + nt(value_grad_ref[...], weight_ref[:, width:])


def memory_back(key_grad, value_grad, weights, waits=()):
    tokens, width = key_grad.shape
    block = by_rows((ROWS, width))
    kernel, in_specs = after(
        waits, memory_back_kernel, [block, block, held((width, 2 * width), (0, 1))]
    )
    return pl.pallas_call(
        kernel,
        grid=(tokens // ROWS,),
        in_specs=in_specs,
        out_specs=block,
        out_shape=out((tokens, width), f32),
        compiler_params=params(),
        cost_estimate=cost(4 * tokens * width * width, 8 * tokens * width + 4 * width * width, 0, 64),
        name="memory_back",
    )(*waits, key_grad, value_grad, weights)


def weight_grads_kernel(picks, *refs):
    step = pl.program_id(0)
    grads_ref = refs[-1]
    half, wide = grads_ref.shape[0] // 2, grads_ref.shape[1]
    for at, (left, right, column) in enumerate(picks):

        @pl.when(step == at)
        def _(left=left, right=right, column=column):
            for low in (0, half):
                grads_ref[low : low + half, :] = tn(
                    refs[left][:, low : low + half], refs[right][:, column : column + wide]
                ).astype(bf16)


def spread(made, first_pair, own, dp_size, me_ref, keep_ref, send_ref, columns):
    mine = me_ref[0]
    upper = lax.rem(mine, 2) == 1
    planes = keep_ref.shape[0] // own // dp_size
    mine_plane = lax.rem(lax.shift_right_logical(mine, 1), planes)
    for piece in range(made.shape[0] // (2 * own)):
        pair = first_pair + piece
        away = lax.bitwise_xor(mine_plane, pair % planes)
        place = away * dp_size + pair // planes
        span = pl.ds(pl.multiple_of(place * own, own), own)
        one = made[2 * own * piece : 2 * own * piece + own]
        two = made[2 * own * piece + own : 2 * own * (piece + 1)]
        keep_ref[span, columns] = jnp.where(upper, two, one)
        send_ref[span, columns] = jnp.where(upper, one, two)


def small_grads_kernel(one_ref, two_ref, three_ref, cross_ref, self_ref, hidden_ref, rows_ref):
    rows_ref[...] = jnp.zeros_like(rows_ref)
    places = [(GAIN, one_ref, 0), (GAIN + 1, two_ref, 0), (GAIN + 2, three_ref, 0)]
    places += [(SHIFT, one_ref, 1), (SHIFT + 1, two_ref, 1), (SHIFT + 2, three_ref, 1)]
    places += [(BIAS, self_ref, 0), (BIAS + 1, self_ref, 1), (BIAS + 2, two_ref, 3), (BIAS + 3, cross_ref, 0)]
    places += [(BIAS + 4, cross_ref, 1), (BIAS + 5, three_ref, 3), (BIAS + 6, three_ref, 2)]
    for at, ref, row in places:
        rows_ref[at : at + 1, :] = ref[row : row + 1, :]
    for step in range(hidden_ref.shape[0]):
        rows_ref[HIDDEN_BIAS + step : HIDDEN_BIAS + step + 1, :] = hidden_ref[step, 0:1, :]


def small_grads(*sums):
    width = sums[0].shape[1]
    return pl.pallas_call(
        small_grads_kernel,
        out_shape=out((24, width), f32),
        compiler_params=params(),
        name="small_grads",
    )(*sums)


def split_grads_kernel(picks, dp_size, own, count, me_ref, *refs):
    step = pl.program_id(0)
    keep_ref, send_ref = refs[count : count + 2]
    held_refs, sems = refs[count + 2 : -1], refs[-1]
    half, wide = keep_ref.shape
    copies = [pltpu.make_async_copy(refs[i], held_refs[i], sems.at[i]) for i in range(count)]

    @pl.when(step == 0)
    def _():
        for copy in copies:
            copy.start()

    known = set()
    for at, (left, right, column) in enumerate(picks):
        fresh = sorted({left, right} - known)
        known.update(fresh)

        @pl.when(step == at)
        def _(left=left, right=right, column=column, fresh=fresh):
            for i in fresh:
                copies[i].wait()
            for low in (0, half):
                made = tn(held_refs[left][:, low : low + half], held_refs[right][:, column : column + wide])
                first_pair = low // (2 * own)
                spread(made.astype(bf16), first_pair, own, dp_size, me_ref, keep_ref, send_ref, slice(0, wide))


def weight_grads(pairs, split=None, waits=(), wide=1024):
    arrays, picks = [], []
    for left, right in pairs:
        at = []
        for array in (left, right):
            known = [i for i, other in enumerate(arrays) if other is array]
            if not known:
                arrays.append(array)
            at.append(known[0] if known else len(arrays) - 1)
        picks += [(at[0], at[1], column) for column in range(0, right.shape[1], wide)]
    width = pairs[0][0].shape[1]
    columns = sum(right.shape[1] for _, right in pairs)
    flops = sum(2 * left.shape[0] * width * right.shape[1] for left, right in pairs)
    nbytes = 2 * sum(a.size for a in arrays) + 2 * width * columns
    if split is None:
        return pl.pallas_call(
            functools.partial(weight_grads_kernel, tuple(picks)),
            grid=(len(picks),),
            in_specs=[held(array.shape) for array in arrays],
            out_specs=pl.BlockSpec((width, wide), lambda j: (0, j)),
            out_shape=out((width, columns), bf16),
            compiler_params=params(),
            cost_estimate=cost(flops, nbytes),
            name="weight_grads",
        )(*arrays)
    mine, dp_size, own = split
    half = pl.BlockSpec((width // 2, wide), lambda j: (0, j))
    kernel, in_specs = after(
        waits,
        functools.partial(split_grads_kernel, tuple(picks), dp_size, own, len(arrays)),
        [pl.BlockSpec(memory_space=pltpu.SMEM)] + [pl.BlockSpec(memory_space=pl.ANY)] * len(arrays),
    )
    return pl.pallas_call(
        kernel,
        grid=(len(picks),),
        in_specs=in_specs,
        out_specs=[half, half],
        out_shape=[out((width // 2, columns), bf16)] * 2,
        scratch_shapes=[pltpu.VMEM(array.shape, bf16) for array in arrays]
        + [pltpu.SemaphoreType.DMA((len(arrays),))],
        compiler_params=params(),
        cost_estimate=cost(flops, nbytes),
        name="weight_grads_by_distance",
    )(*waits, mine, *arrays)


def near_kernel(steps, first_x_ref, first_x_got_ref, first_y_ref, first_y_got_ref, whole_ref):
    step = pl.program_id(0)
    rows = first_x_ref.shape[0] // 2

    def put(place, ref, at):
        whole_ref[place * rows : (place + 1) * rows] = ref[at * rows : (at + 1) * rows]

    @pl.when(step < steps)
    def _():
        for place, ref, at in ((0, first_x_ref, 0), (1, first_x_ref, 1), (2, first_x_got_ref, 0), (3, first_x_got_ref, 1)):
            put(place, ref, at)

    @pl.when(step >= steps)
    def _():
        for place, ref, at in ((0, first_y_ref, 0), (2, first_y_ref, 1), (1, first_y_got_ref, 0), (3, first_y_got_ref, 1)):
            put(place, ref, at)


def near_rows(first_x, first_x_got, first_y, first_y_got, waits=()):
    rows, own, columns = first_x.shape
    lanes = 512
    steps = columns // lanes
    low = pl.BlockSpec((rows, own, lanes), lambda j: (0, 0, jnp.minimum(j, steps - 1)))
    high = pl.BlockSpec((rows, own, lanes), lambda j: (0, 0, jnp.maximum(j - steps, 0)))
    kernel, in_specs = after(waits, functools.partial(near_kernel, steps), [low, low, high, high])
    return pl.pallas_call(
        kernel,
        grid=(2 * steps,),
        in_specs=in_specs,
        out_specs=pl.BlockSpec((2 * rows, own, lanes), lambda j: (0, 0, j)),
        out_shape=out((2 * rows, own, 2 * columns), bf16),
        compiler_params=params(),
        cost_estimate=cost(0, 8 * rows * own * columns),
        name="near_rows",
    )(*waits, first_x, first_x_got, first_y, first_y_got)


def place_kernel(dp_size, me_ref, near_ref, far_ref, whole_ref):
    pairs, own = near_ref.shape[:2]
    planes = pairs // dp_size
    mine = me_ref[0]
    side = lax.rem(mine, 2)
    mine_pair = lax.shift_right_logical(mine, 1)
    for at in range(pairs):
        pair = lax.bitwise_xor(mine_pair, at % dp_size * planes + at // dp_size)
        for ref, core in ((near_ref, side), (far_ref, 1 - side)):
            rows = pl.ds(pl.multiple_of((2 * pair + core) * own, own), own)
            whole_ref[rows, :] = ref[at]


def place(mine, near, far, dp_size):
    pairs, own, columns = near.shape
    lanes = 1024
    block = pl.BlockSpec((pairs, own, lanes), lambda j: (0, 0, j))
    return pl.pallas_call(
        functools.partial(place_kernel, dp_size),
        grid=(columns // lanes,),
        in_specs=[pl.BlockSpec(memory_space=pltpu.SMEM), block, block],
        out_specs=pl.BlockSpec((2 * pairs * own, lanes), lambda j: (0, j)),
        out_shape=out((2 * pairs * own, columns), bf16),
        compiler_params=params(),
        cost_estimate=cost(0, 8 * pairs * own * columns),
        name="place_by_device",
    )(mine, near, far)


def feed_own_kernel(*refs):
    owned, (inner_ref, outer_ref) = refs[:-2], refs[-2:]
    own, width = owned[0].shape[0], outer_ref.shape[1]
    tiles = [
        (ref, at * width) for ref in owned for at in range(0, ref.shape[1] // width, 2)
    ]
    for step, (ref, at) in enumerate(tiles):
        outer_ref[step * own : (step + 1) * own, :] = ref[:, at + width : at + 2 * width].astype(f32)
    for device in range(width // own):
        pieces = [ref[:, at + device * own : at + (device + 1) * own].astype(f32) for ref, at in tiles]
        span = len(tiles) * own
        inner_ref[:, device * span : (device + 1) * span] = jnp.concatenate(pieces, axis=1)


def feed_own_grads(owned, width, waits=()):
    own = owned[0].shape[0]
    steps = sum(part.shape[1] for part in owned) // (2 * width)
    vmem = pl.BlockSpec(memory_space=pltpu.VMEM)
    kernel, in_specs = after(waits, feed_own_kernel, [vmem] * len(owned))
    return pl.pallas_call(
        kernel,
        in_specs=in_specs,
        out_shape=[out((own, steps * width), f32), out((steps * own, width), f32)],
        compiler_params=params(),
        name="feed_own_grads",
    )(*waits, *owned)


def cut_kernel(cuts, whole_ref, *outs):
    for ref, (low, high) in zip(outs, cuts):
        ref[...] = whole_ref[:, low:high].astype(f32)


def cut_columns(whole, ends, waits=()):
    cuts = tuple(zip(ends[:-1], ends[1:]))
    own = whole.shape[0]
    vmem = pl.BlockSpec(memory_space=pltpu.VMEM)
    kernel, in_specs = after(waits, functools.partial(cut_kernel, cuts), [vmem])
    return pl.pallas_call(
        kernel,
        in_specs=in_specs,
        out_shape=[out((own, high - low), f32) for low, high in cuts],
        compiler_params=params(),
        name="own_columns",
    )(*waits, whole)


def plane_pieces_kernel(count, ranges, keep_ref, got_ref, *outs):
    rows = keep_ref.shape[0] // count
    for at, (low, high) in enumerate(ranges):
        for k in range(count):
            span = slice(k * rows, (k + 1) * rows)
            made = keep_ref[span, low:high].astype(f32) + got_ref[span, low:high].astype(f32)
            outs[at * count + k][...] = made.astype(bf16)


def lanes_of(columns):
    return next(n for n in (2048, 1664, 1408, 1280, 1024, 128) if columns % n == 0)


def plane_pieces(keep, got, count, waits, ends):
    rows, columns = keep.shape
    ranges = tuple(zip(ends[:-1], ends[1:]))
    if len(ranges) == 1:
        lanes = lanes_of(columns)
        steps, shapes, ranges = columns // lanes, [(columns, lanes)], ((0, lanes),)
    else:
        lanes, steps, shapes = columns, 1, [(high - low, high - low) for low, high in ranges]
    block = pl.BlockSpec((rows, lanes), lambda j: (0, j))
    kernel, in_specs = after(
        waits, functools.partial(plane_pieces_kernel, count, ranges), [block, block]
    )
    return pl.pallas_call(
        kernel,
        grid=(steps,),
        in_specs=in_specs,
        out_specs=[
            pl.BlockSpec((rows // count, n), lambda j: (0, j)) for _, n in shapes for _ in range(count)
        ],
        out_shape=[out((rows // count, n), bf16) for n, _ in shapes for _ in range(count)],
        compiler_params=params(),
        cost_estimate=cost(0, 6 * rows * columns),
        name="plane_pieces",
    )(*waits, keep, got)


def plane_total_kernel(*refs):
    total = refs[0][...].astype(f32)
    for ref in refs[1:-1]:
        total = total + ref[...].astype(f32)
    refs[-1][...] = total.astype(bf16)


def plane_total(pieces, waits=(), weight=0):
    rows, columns = pieces[0].shape
    lanes = lanes_of(columns)
    block = pl.BlockSpec((rows, lanes), lambda j: (0, j))
    kernel, in_specs = after(waits, plane_total_kernel, [block] * len(pieces))
    return pl.pallas_call(
        kernel,
        grid=(columns // lanes,),
        in_specs=in_specs,
        out_specs=block,
        out_shape=out((rows, columns), bf16),
        compiler_params=params(),
        cost_estimate=cost(weight * rows * columns, 2 * (len(pieces) + 1) * rows * columns),
        name="plane_total",
    )(*waits, *pieces)


def prepare_kernel(
    qkv_ref, out_ref, query_ref, pair_ref, cross_ref, inner_ref, outer_ref, gains_ref, shifts_ref, biases_ref, hidden_ref,
    first_ref, second_ref, third_ref,
):
    own, width = out_ref.shape
    steps = inner_ref.shape[1] // width
    devices = width // own
    rows = [gains_ref[...].astype(f32), shifts_ref[...].astype(f32), biases_ref[...].astype(f32)]
    hidden = hidden_ref[...].astype(f32)
    rows += [hidden[:, step * own : (step + 1) * own] for step in range(steps)]
    rows += [jnp.zeros((SMALL - HIDDEN_BIAS - steps, own), f32)]
    first_ref[:, : 3 * width] = qkv_ref[...]
    first_ref[:, 3 * width :] = jnp.concatenate(rows, axis=0).T.astype(bf16)
    second_ref[:, :width] = out_ref[...]
    second_ref[:, width : 2 * width] = query_ref[...]
    second_ref[:, 2 * width : 4 * width] = pair_ref[...]
    second_ref[:, 4 * width :] = cross_ref[...]
    for step in range(steps):
        pieces = [
            inner_ref[:, (device * steps + step) * own : (device * steps + step + 1) * own].astype(f32)
            for device in range(devices)
        ]
        third_ref[:, 2 * step * width : (2 * step + 1) * width] = jnp.concatenate(pieces, axis=1).astype(bf16)
        third_ref[:, (2 * step + 1) * width : (2 * step + 2) * width] = outer_ref[step * own : (step + 1) * own, :]


def prepare(*shards):
    own, width = shards[1].shape
    steps = shards[5].shape[1] // width
    return pl.pallas_call(
        prepare_kernel,
        out_shape=[
            out((own, 3 * width + SMALL), bf16),
            out((own, 5 * width), bf16),
            out((own, 2 * steps * width), bf16),
        ],
        compiler_params=params(),
        name="shards_to_gather",
    )(*shards)


AXES = ("dp", "fsdp")


def gather(shard):
    return lax.all_gather(shard, AXES, axis=0, tiled=True)


def scatter_sum(whole):
    return lax.psum_scatter(whole, AXES, scatter_dimension=0, tiled=True)


def exchange(array, axis, size, distance):
    return lax.ppermute(array, axis, [(i, i ^ distance) for i in range(size)])


def sum_along(sums, axis, size):
    distance = 1
    while distance < size:
        sums = sums + exchange(sums, axis, size, distance)
        distance *= 2
    return sums


def small_sum(sums, own, dp_size, fsdp_size):
    kept = sum_along(sums, "fsdp", fsdp_size)
    start = (lax.axis_index("dp") * fsdp_size + lax.axis_index("fsdp")) * own
    return lax.dynamic_slice_in_dim(kept, start, own, axis=1)


def add_low(left, right):
    return (left.astype(f32) + right.astype(f32)).astype(bf16)


def scatter_plane(keep, got, fsdp_size, waits=(), cut=()):
    planes = fsdp_size // 2
    made = list(plane_pieces(keep, got, planes, waits, (0, *cut, keep.shape[1])))
    both = [made[at : at + planes] for at in range(0, len(made), planes)]
    return [
        (part[1:], part[:1] + [exchange(part[k], "fsdp", fsdp_size, 2 * k) for k in range(1, planes)])
        for part in both
    ]


def scatter_line(total):
    return lax.psum_scatter(total, "dp", scatter_dimension=0, tiled=True)


def local(
    inputs,
    memory,
    cotangent,
    target_lengths,
    memory_lengths,
    norm_gains,
    norm_biases,
    self_qkv,
    self_out,
    cross_query,
    cross_kv,
    cross_out,
    ffn_in,
    ffn_out,
    proj_biases,
    ffn_in_bias,
):
    width = inputs.shape[2]
    own = self_qkv.shape[0]
    devices = width // own
    steps = ffn_in.shape[1] // width
    dp_size, fsdp_size = lax.axis_size("dp"), lax.axis_size("fsdp")
    by_distance = own % 16 == 0 and fsdp_size == 8
    mine = (lax.axis_index("dp") * fsdp_size + lax.axis_index("fsdp")).astype(jnp.int32).reshape(1)
    split = (mine, dp_size, own) if by_distance else (mine,)

    if by_distance:
        first_shard, second_shard, feed_shard = prepare(
            self_qkv, self_out, cross_query, cross_kv, cross_out, ffn_in, ffn_out,
            norm_gains, norm_biases, proj_biases, ffn_in_bias.reshape(1, -1),
        )
    else:
        small = jnp.concatenate(
            [norm_gains, norm_biases, proj_biases, ffn_in_bias.reshape(steps, own)], axis=0
        )
        small = jnp.pad(small, ((0, SMALL - small.shape[0]), (0, 0))).T
        first_shard = jnp.concatenate([self_qkv, small], axis=1)
        second_shard = jnp.concatenate([self_out, cross_query, cross_kv, cross_out], axis=1)
        inner_shard = ffn_in.reshape(own, devices, steps, own).transpose(0, 2, 1, 3).reshape(own, steps, width)
        outer_shard = ffn_out.reshape(steps, own, width).transpose(1, 0, 2)
        feed_shard = jnp.concatenate([inner_shard, outer_shard], axis=2).reshape(own, 2 * steps * width)

    first = gather(first_shard)
    third = gather(feed_shard)
    x = inputs[0]
    rows = memory[0]
    branch = cotangent[0]
    waits = ()
    if by_distance:
        line = jnp.stack(
            [second_shard] + [exchange(second_shard, "dp", dp_size, k) for k in range(1, dp_size)]
        )
        side = line.shape[2] // 2
        first_x, first_y = line[:, :, :side], line[:, :, side:]
        first_x = jnp.concatenate([first_x, exchange(first_x, "fsdp", fsdp_size, 2)])
        first_y = jnp.concatenate([first_y, exchange(first_y, "fsdp", fsdp_size, 4)])
        first_x_got = exchange(first_x, "fsdp", fsdp_size, 4)
        first_y_got = exchange(first_y, "fsdp", fsdp_size, 2)
        waits = (first_x, first_y)
    table = first[:, 3 * width :].astype(f32).T[:24]

    normed_one, triple = entry(x, first, table, waits)
    parts = [(triple, at * (width // PAIR), width) for at in range(3)]
    self_mixed, self_stats = attend(target_lengths, *parts, True)
    if by_distance:
        near = near_rows(first_x, first_x_got, first_y, first_y_got, (triple,))
        second = place(mine, near, exchange(near, "fsdp", fsdp_size, 1), dp_size)
    else:
        second = gather(second_shard)
    pair = memory_pair(rows, second, table)
    hidden_one, normed_two, queries = middle(x, self_mixed, second, table)
    cross_parts = [(queries, 0, width), (pair, 0, width), (pair, width // PAIR, width)]
    cross_mixed, cross_stats = attend(memory_lengths, *cross_parts, False)
    hidden_two, normed_three = late(hidden_one, cross_mixed, second, table)
    made, back, hidden_bias_sums, *feed_grads = feed(normed_three, branch, third, table, split)
    grad_two, branch_two, mixed_grad, sums_three = turn(hidden_two, back, branch, second, table)
    waits = ()
    if by_distance:
        feed_got = exchange(feed_grads[1], "fsdp", fsdp_size, 1)
        [(feed_sent, feed_plane)] = scatter_plane(feed_grads[0], feed_got, fsdp_size, (sums_three,))
        waits = tuple(feed_sent)
    else:
        feed_own = scatter_sum(feed_grads[0])
    query_grad, key_grad, value_grad, cross_sums = attend_back(
        memory_lengths, *cross_parts, cross_mixed, mixed_grad, cross_stats, False, waits
    )
    cross_pairs = [
        (cross_mixed, branch_two),
        (normed_two, query_grad),
        (rows, key_grad),
        (rows, value_grad),
    ]
    waits = ()
    if by_distance:
        cross_keep, cross_send = weight_grads(cross_pairs, split)
        cross_got = exchange(cross_send, "fsdp", fsdp_size, 1)
        waits = (cross_send,)
    grad_one, branch_one, mixed_grad, sums_two = middle_back(
        hidden_one, grad_two, query_grad, second, table, waits
    )
    if by_distance:
        [(cross_sent, cross_plane)] = scatter_plane(cross_keep, cross_got, fsdp_size, (grad_one,))
        waits = tuple(cross_sent)
    *self_grads, self_sums = attend_back(
        target_lengths, *parts, self_mixed, mixed_grad, self_stats, True, waits
    )
    self_pairs = [(self_mixed, branch_one)] + [(normed_one, part) for part in self_grads]
    waits = ()
    if by_distance:
        feed_total = plane_total(feed_plane, (self_sums,))
        feed_own = scatter_line(feed_total)
        self_keep, self_send = weight_grads(self_pairs, split, (feed_total,))
        self_got = exchange(self_send, "fsdp", fsdp_size, 1)
        memory_grad = memory_back(key_grad, value_grad, second, (self_send,))
        [(self_sent, self_plane)] = scatter_plane(self_keep, self_got, fsdp_size, (memory_grad,))
        cross_total = plane_total(cross_plane, (self_sent[0],))
        cross_own = scatter_line(cross_total)
        waits = (*self_sent, cross_total)
    input_grad, sums_one = entry_back(x, grad_one, self_grads, first, table, waits)
    sums = small_grads(sums_one, sums_two, sums_three, cross_sums, self_sums, hidden_bias_sums)
    sums = sum_along(sums, "dp", dp_size)
    if by_distance:
        result = layer_result(hidden_two, made, table, (input_grad,))
        inner_own, outer_own = feed_own_grads([feed_own], width, (result,))
        cross_out_own, query_own, pair_own = cut_columns(
            cross_own, (0, width, 2 * width, 4 * width), (inner_own,)
        )
        self_total = plane_total(self_plane, (cross_out_own, sums))
        self_own = scatter_line(self_total)
        self_out_own, triple_own = cut_columns(self_own, (0, width, 4 * width))
    else:
        result = layer_result(hidden_two, made, table)
        memory_grad = memory_back(key_grad, value_grad, second)
        cross_own = scatter_sum(weight_grads(cross_pairs)).astype(f32)
        cross_out_own, query_own = cross_own[:, :width], cross_own[:, width : 2 * width]
        pair_own = cross_own[:, 2 * width :]
        self_own = scatter_sum(weight_grads(self_pairs)).astype(f32)
        self_out_own, triple_own = self_own[:, :width], self_own[:, width:]
        feed_own = feed_own.astype(f32).reshape(own, steps, 2, width)
        inner_own = feed_own[:, :, 0].reshape(own, steps, devices, own).transpose(0, 2, 1, 3)
        inner_own = inner_own.reshape(own, steps * width)
        outer_own = feed_own[:, :, 1].transpose(1, 0, 2).reshape(steps * own, width)
    small_own = small_sum(sums, own, dp_size, fsdp_size)
    return (
        result[None],
        input_grad[None],
        memory_grad[None],
        small_own[GAIN:SHIFT],
        small_own[SHIFT:BIAS],
        triple_own,
        self_out_own,
        query_own,
        pair_own,
        cross_out_own,
        inner_own,
        outer_own,
        small_own[BIAS:HIDDEN_BIAS],
        small_own[HIDDEN_BIAS : HIDDEN_BIAS + steps].reshape(steps * own),
    )


def solution(mesh):
    rows = P(AXES, None, None)
    lengths = P(AXES)
    split = P(AXES, None)
    features = P(None, AXES)
    return jax.shard_map(
        local,
        mesh=mesh,
        in_specs=(rows, rows, rows, lengths, lengths, features, features)
        + (split,) * 7
        + (features, lengths),
        out_specs=(rows, rows, rows, features, features) + (split,) * 7 + (features, lengths),
        check_vma=False,
    )
```

```python
import functools

import jax
import jax.numpy as jnp
from jax import lax
from jax.experimental import pallas as pl
from jax.experimental.pallas import tpu as pltpu
from jax.sharding import PartitionSpec as P

f32 = jnp.float32
bf16 = jnp.bfloat16

HEAD = 64
PAIR = 2 * HEAD
BLOCK = 256
ROWS = 256
SMALL = 128
eps_norm = 1e-05
masked_score = -1e30
gelu_slope = 0.7978845608028654
gelu_cubic = 0.044715
MiB = 1 << 20


def nn(left, right):
    return jnp.dot(left, right, preferred_element_type=f32)


def nt(left, right):
    return lax.dot_general(left, right, (((1,), (1,)), ((), ())), preferred_element_type=f32)


def tn(left, right):
    return lax.dot_general(left, right, (((0,), (0,)), ((), ())), preferred_element_type=f32)


def normalise(hidden):
    centred = hidden - jnp.mean(hidden, axis=-1, keepdims=True)
    spread = lax.rsqrt(jnp.mean(centred * centred, axis=-1, keepdims=True) + eps_norm)
    return centred * spread, spread


def norm_back(hidden, incoming, gain):
    normed, spread = normalise(hidden)
    scaled = incoming * gain
    part = spread * (
        scaled
        - jnp.mean(scaled, axis=-1, keepdims=True)
        - normed * jnp.mean(scaled * normed, axis=-1, keepdims=True)
    )
    gain_grad = jnp.sum(incoming * normed, axis=0, keepdims=True)
    shift_grad = jnp.sum(incoming, axis=0, keepdims=True)
    return part, gain_grad, shift_grad


def column_sum(gradient):
    return jnp.sum(gradient.astype(f32), axis=0, keepdims=True)


def params():
    return pltpu.CompilerParams(vmem_limit_bytes=60 * MiB)


def after(waits, kernel, in_specs):
    count = len(waits)

    def waiting(*refs):
        kernel(*refs[count:])

    return waiting, [pl.BlockSpec(memory_space=pl.ANY)] * count + in_specs


def cost(flops, nbytes, transcendentals=0, high=64):
    return pl.CostEstimate(
        flops=high * flops, bytes_accessed=high * nbytes, transcendentals=high * transcendentals
    )


def held(shape, at=None):
    place = (0,) * len(shape) if at is None else at
    return pl.BlockSpec(shape, lambda j: place, pipeline_mode=pl.Buffered(1))


def by_rows(shape):
    return pl.BlockSpec(shape, lambda j: (j, 0))


def out(shape, dtype):
    return jax.ShapeDtypeStruct(shape, dtype)


GAIN, SHIFT, BIAS, HIDDEN_BIAS = 0, 3, 6, 13


def row_of(table_ref, at):
    return table_ref[at : at + 1, :]


def entry_kernel(x_ref, weight_ref, table_ref, normed_ref, triple_ref):
    width = x_ref.shape[1]
    normed, _ = normalise(x_ref[...].astype(f32))
    low = (normed * row_of(table_ref, GAIN) + row_of(table_ref, SHIFT)).astype(bf16)
    normed_ref[...] = low
    for part in range(3):
        span = slice(part * width, (part + 1) * width)
        made = nn(low, weight_ref[:, span])
        if part == 0:
            made = made + row_of(table_ref, BIAS)
        if part == 2:
            made = made + row_of(table_ref, BIAS + 1)
        triple_ref[:, span] = made.astype(bf16)


def entry(x, weights, table, waits=()):
    tokens, width = x.shape
    kernel, in_specs = after(
        waits, entry_kernel, [by_rows((ROWS, width)), held(weights.shape), held(table.shape)]
    )
    return pl.pallas_call(
        kernel,
        grid=(tokens // ROWS,),
        in_specs=in_specs,
        out_specs=[by_rows((ROWS, width)), by_rows((ROWS, 3 * width))],
        out_shape=[out((tokens, width), bf16), out((tokens, 3 * width), bf16)],
        compiler_params=params(),
        cost_estimate=cost(6 * tokens * width * width, 10 * tokens * width + 6 * width * width, 0, 1),
        name="norm_and_qkv",
    )(*waits, x, weights, table)


def middle_kernel(x_ref, mixed_ref, out_ref, query_ref, table_ref, hidden_ref, normed_ref, made_ref):
    hidden = x_ref[...].astype(f32) + nn(mixed_ref[...], out_ref[...]) + row_of(table_ref, BIAS + 2)
    hidden_ref[...] = hidden
    normed, _ = normalise(hidden)
    low = (normed * row_of(table_ref, GAIN + 1) + row_of(table_ref, SHIFT + 1)).astype(bf16)
    normed_ref[...] = low
    made_ref[...] = (nn(low, query_ref[...]) + row_of(table_ref, BIAS + 3)).astype(bf16)


def middle(x, mixed, weights, table):
    tokens, width = x.shape
    block = by_rows((ROWS, width))
    return pl.pallas_call(
        middle_kernel,
        grid=(tokens // ROWS,),
        in_specs=[
            block,
            block,
            held((width, width), (0, 0)),
            held((width, width), (0, 1)),
            held(table.shape),
        ],
        out_specs=[block, block, block],
        out_shape=[out((tokens, width), f32), out((tokens, width), bf16), out((tokens, width), bf16)],
        compiler_params=params(),
        cost_estimate=cost(4 * tokens * width * width, 12 * tokens * width + 4 * width * width, 0, 1),
        name="self_out_norm_query",
    )(x, mixed, weights, weights, table)


def memory_kernel(memory_ref, weight_ref, table_ref, pair_ref):
    width = memory_ref.shape[1]
    rows = memory_ref[...]
    pair_ref[:, :width] = nn(rows, weight_ref[:, :width]).astype(bf16)
    pair_ref[:, width:] = (nn(rows, weight_ref[:, width:]) + row_of(table_ref, BIAS + 4)).astype(bf16)


def memory_pair(memory, weights, table):
    tokens, width = memory.shape
    return pl.pallas_call(
        memory_kernel,
        grid=(tokens // ROWS,),
        in_specs=[by_rows((ROWS, width)), held((width, 2 * width), (0, 1)), held(table.shape)],
        out_specs=by_rows((ROWS, 2 * width)),
        out_shape=out((tokens, 2 * width), bf16),
        compiler_params=params(),
        cost_estimate=cost(4 * tokens * width * width, 6 * tokens * width + 4 * width * width, 0, 1),
        name="memory_keys_values",
    )(memory, weights, table)


def late_kernel(hidden_ref, mixed_ref, out_ref, table_ref, next_ref, normed_ref):
    hidden = hidden_ref[...] + nn(mixed_ref[...], out_ref[...]) + row_of(table_ref, BIAS + 5)
    next_ref[...] = hidden
    normed, _ = normalise(hidden)
    normed_ref[...] = (normed * row_of(table_ref, GAIN + 2) + row_of(table_ref, SHIFT + 2)).astype(bf16)


def late(hidden, mixed, weights, table):
    tokens, width = hidden.shape
    block = by_rows((ROWS, width))
    return pl.pallas_call(
        late_kernel,
        grid=(tokens // ROWS,),
        in_specs=[block, block, held((width, width), (0, 4)), held(table.shape)],
        out_specs=[block, block],
        out_shape=[out((tokens, width), f32), out((tokens, width), bf16)],
        compiler_params=params(),
        cost_estimate=cost(2 * tokens * width * width, 12 * tokens * width + 2 * width * width, 0, 1),
        name="cross_out_norm",
    )(hidden, mixed, weights, table)


def head_operands(lane, side, query, key, key_bias):
    own = (lane < HEAD) if side == 0 else (lane >= HEAD)
    spare = lane == (HEAD if side == 0 else 0)
    zero = jnp.zeros((), bf16)
    query_own = jnp.where(own, query, zero)
    key_own = jnp.where(own, key, zero)
    query_wide = jnp.where(spare, jnp.ones((), bf16), query_own)
    key_wide = jnp.where(spare, key_bias, key_own)
    return own, query_own, query_wide, key_own, key_wide


def pair_operands(length_ref, query_ref, key_ref):
    lane = lax.broadcasted_iota(jnp.int32, (1, PAIR), 1)
    key_pos = lax.broadcasted_iota(jnp.int32, (key_ref.shape[0], 1), 0)
    key_bias = jnp.where(key_pos < length_ref[0], 0.0, masked_score).astype(bf16)
    query = query_ref[...] * jnp.asarray(HEAD**-0.5, bf16)
    key = key_ref[...]
    return lane, [head_operands(lane, side, query, key, key_bias) for side in (0, 1)]


def scores_by_key(key_wide, query_block, keys, allowed):
    scores = nt(key_wide[:keys], query_block)
    if allowed is None:
        return scores
    last = jnp.where(allowed, scores[keys - BLOCK :], masked_score)
    return last if keys == BLOCK else jnp.concatenate([scores[: keys - BLOCK], last], axis=0)


def causal_block():
    key = lax.broadcasted_iota(jnp.int32, (BLOCK, BLOCK), 0)
    query = lax.broadcasted_iota(jnp.int32, (BLOCK, BLOCK), 1)
    return key <= query


def attend_kernel(causal, length_ref, query_ref, key_ref, value_ref, mixed_ref, stat_ref):
    rows, keys_all = query_ref.shape[0], key_ref.shape[0]
    lane, heads = pair_operands(length_ref, query_ref, key_ref)
    value = value_ref[...]
    allowed = causal_block() if causal else None
    first = lane < HEAD
    value_wide = [jnp.where(heads[side][0], value, jnp.ones((), bf16)) for side in (0, 1)]
    for at in range(0, rows, BLOCK):
        keys = at + BLOCK if causal else keys_all
        got, tops = [], []
        for side in (0, 1):
            _, _, query_wide, _, key_wide = heads[side]
            scores = scores_by_key(key_wide, query_wide[at : at + BLOCK], keys, allowed)
            top = jnp.max(scores, axis=0, keepdims=True)
            exponent = jnp.exp(scores - top)
            got.append(tn(exponent.astype(bf16), value_wide[side][:keys]))
            tops.append(top)
        total = jnp.where(first, got[1], got[0])
        mixed = jnp.where(first, got[0], got[1]) / pltpu.roll(total, HEAD, 1)
        mixed_ref[at : at + BLOCK, :] = mixed.astype(bf16)
        logs = jnp.log(total).T
        stat_ref[0, 0:1, at : at + BLOCK] = tops[0] + logs[HEAD : HEAD + 1]
        stat_ref[0, 1:2, at : at + BLOCK] = tops[1] + logs[0:1]


def pair_block(rows, column=0):
    return pl.BlockSpec((rows, PAIR), lambda j: (0, column + j))


def attend(lengths, query, key, value, causal):
    rows, keys, width = query[0].shape[0], key[0].shape[0], query[2]
    pairs = width // PAIR
    return pl.pallas_call(
        functools.partial(attend_kernel, causal),
        grid=(pairs,),
        in_specs=[
            pl.BlockSpec(memory_space=pltpu.SMEM),
            pair_block(rows, query[1]),
            pair_block(keys, key[1]),
            pair_block(keys, value[1]),
        ],
        out_specs=[pair_block(rows), pl.BlockSpec((1, 2, rows), lambda j: (j, 0, 0))],
        out_shape=[out((rows, width), bf16), out((pairs, 2, rows), f32)],
        compiler_params=params(),
        cost_estimate=cost(16 * rows * keys * width, 4 * (rows + keys) * width, 16 * rows * keys, 1),
        name="attend_causal" if causal else "attend_memory",
    )(lengths, query[0], key[0], value[0])


def attend_back_kernel(
    causal,
    length_ref,
    query_ref,
    key_ref,
    value_ref,
    mixed_ref,
    grad_ref,
    stat_ref,
    query_grad_ref,
    key_grad_ref,
    value_grad_ref,
    sums_ref,
    key_sum,
    value_sum,
):
    rows, keys_all = query_ref.shape[0], key_ref.shape[0]
    scale = HEAD**-0.5
    lane, heads = pair_operands(length_ref, query_ref, key_ref)
    value = value_ref[...]
    grad = grad_ref[...]
    inner = (grad.astype(f32) * mixed_ref[...].astype(f32)).T
    allowed = causal_block() if causal else None
    zero = jnp.zeros((), bf16)
    value_own = [jnp.where(heads[side][0], value, zero) for side in (0, 1)]
    grad_own = [jnp.where(heads[side][0], grad, zero) for side in (0, 1)]
    inner_sum = [
        jnp.sum(inner[side * HEAD : (side + 1) * HEAD], axis=0, keepdims=True) for side in (0, 1)
    ]
    block = BLOCK if causal else rows
    for at in range(rows - block, -1, -block):
        keys = at + block if causal else keys_all
        span = slice(at, at + block)
        sums = None
        for side in (0, 1):
            _, query_own, query_wide, key_own, key_wide = heads[side]
            scores = scores_by_key(key_wide, query_wide[span], keys, allowed)
            probs = jnp.exp(scores - stat_ref[0, side : side + 1, span])
            grad_probs = nt(value_own[side][:keys], grad[span])
            grad_scores = (probs * (grad_probs - inner_sum[side][:, span])).astype(bf16)
            parts = (
                tn(grad_scores, key_own[:keys]),
                nn(grad_scores, query_own[span]),
                nn(probs.astype(bf16), grad_own[side][span]),
            )
            sums = parts if sums is None else tuple(a + b for a, b in zip(sums, parts))
        query_low = (sums[0] * scale).astype(bf16)
        query_grad_ref[span, :] = query_low
        query_total = column_sum(query_low) + (0.0 if at == rows - block else query_total)
        if at == rows - block:
            key_sum[...] = sums[1]
            value_sum[...] = sums[2]
        else:
            key_sum[:keys] += sums[1]
            value_sum[:keys] += sums[2]
    key_grad_ref[...] = key_sum[...].astype(bf16)
    value_low = value_sum[...].astype(bf16)
    value_grad_ref[...] = value_low
    sums_ref[...] = jnp.zeros_like(sums_ref)
    sums_ref[0:1, :] = query_total
    sums_ref[1:2, :] = column_sum(value_low)


def attend_back(lengths, query, key, value, mixed, grad, stats, causal, waits=(), share=(0, 1)):
    rows, keys = query[0].shape[0], key[0].shape[0]
    pairs = query[2] // PAIR // share[1]
    first, width = share[0] * pairs, pairs * PAIR
    kernel, in_specs = after(
        waits,
        functools.partial(attend_back_kernel, causal),
        [
            pl.BlockSpec(memory_space=pltpu.SMEM),
            pair_block(rows, query[1] + first),
            pair_block(keys, key[1] + first),
            pair_block(keys, value[1] + first),
            pair_block(rows, first),
            pair_block(rows, first),
            pl.BlockSpec((1, 2, rows), lambda j: (first + j, 0, 0)),
        ],
    )
    return pl.pallas_call(
        kernel,
        grid=(pairs,),
        in_specs=in_specs,
        out_specs=[pair_block(rows), pair_block(keys), pair_block(keys), pair_block(8)],
        out_shape=[
            out((rows, width), bf16),
            out((keys, width), bf16),
            out((keys, width), bf16),
            out((8, width), f32),
        ],
        scratch_shapes=[pltpu.VMEM((keys, PAIR), f32), pltpu.VMEM((keys, PAIR), f32)],
        compiler_params=params(),
        cost_estimate=cost(24 * rows * keys * width, 8 * (rows + keys) * width, 16 * rows * keys),
        name="attend_causal_back" if causal else "attend_memory_back",
    )(*waits, lengths, query[0], key[0], value[0], mixed, grad, stats)


FEED_ROWS = 512


def feed_kernel(
    split, me_ref, normed_ref, branch_ref, weight_ref, table_ref, made_ref, back_ref, bias_ref, *refs
):
    turned, act, dact = refs[-3:]
    step = pl.program_id(0)
    tokens, width = normed_ref.shape

    @pl.when(step == 0)
    def _():
        made_ref[...] = jnp.zeros_like(made_ref)
        back_ref[...] = jnp.zeros_like(back_ref)
        turned[...] = normed_ref[...].T

    bias = table_ref[pl.ds(HIDDEN_BIAS + step, 1), :]
    bias_sum = jnp.zeros((1, width), f32)
    for at in range(0, tokens, FEED_ROWS):
        span = slice(at, at + FEED_ROWS)
        inner = nn(normed_ref[span, :], weight_ref[:, :width]) + bias
        grad_active = nt(branch_ref[span, :], weight_ref[:, width:])
        square = inner * inner
        bent = jnp.tanh(inner * (gelu_slope + (gelu_slope * gelu_cubic) * square))
        half = 0.5 + 0.5 * bent
        active = (inner * half).astype(bf16)
        slope = half + (0.5 * inner) * (1.0 - bent * bent) * (
            gelu_slope + (3.0 * gelu_slope * gelu_cubic) * square
        )
        grad_inner = (grad_active * slope).astype(bf16)
        act[span, :] = active
        dact[span, :] = grad_inner
        bias_sum += column_sum(grad_inner)
        made_ref[span, :] += nn(active, weight_ref[:, width:])
        back_ref[span, :] += nt(grad_inner, weight_ref[:, :width])
    bias_ref[0] = jnp.broadcast_to(bias_sum, bias_ref.shape[1:])
    for at in range(0, width, FEED_ROWS):
        span = slice(at, at + FEED_ROWS)
        inner_part = nn(turned[span, :], dact[...]).astype(bf16)
        outer_part = tn(act[:, span], branch_ref[...]).astype(bf16)
        for part, columns in ((inner_part, slice(0, width)), (outer_part, slice(width, 2 * width))):
            if split is None:
                refs[0][span, columns] = part
            else:
                dp_size, own = split
                spread(part, at // (2 * own), own, dp_size, me_ref, refs[0], refs[1], columns)


def feed(normed, branch, weights, table, split):
    tokens, width = normed.shape
    steps = weights.shape[1] // (2 * width)
    hidden = steps * width
    whole = pl.BlockSpec((tokens, width), lambda j: (0, 0))
    tile = pl.BlockSpec((width, 2 * width), lambda j: (0, j))
    if split[1:]:
        grad_specs = [pl.BlockSpec((width // 2, 2 * width), lambda j: (0, j))] * 2
        grad_shapes = [out((width // 2, 2 * hidden), bf16)] * 2
    else:
        grad_specs, grad_shapes = [tile], [out((width, 2 * hidden), bf16)]
    return pl.pallas_call(
        functools.partial(feed_kernel, split[1:] or None),
        grid=(steps,),
        in_specs=[
            pl.BlockSpec(memory_space=pltpu.SMEM),
            held((tokens, width)),
            held((tokens, width)),
            tile,
            held(table.shape),
        ],
        out_specs=[whole, whole, pl.BlockSpec((1, 8, width), lambda j: (j, 0, 0))] + grad_specs,
        out_shape=[
            out((tokens, width), f32),
            out((tokens, width), f32),
            out((steps, 8, width), f32),
        ]
        + grad_shapes,
        scratch_shapes=[
            pltpu.VMEM((width, tokens), bf16),
            pltpu.VMEM((tokens, width), bf16),
            pltpu.VMEM((tokens, width), bf16),
        ],
        compiler_params=params(),
        cost_estimate=cost(
            12 * tokens * width * hidden, 8 * width * hidden + 12 * tokens * width, tokens * hidden
        ),
        name="feed_forward_both_ways",
    )(split[0], normed, branch, weights, table)


def add_rows(ref, rows):
    @pl.when(pl.program_id(0) == 0)
    def _():
        ref[...] = jnp.zeros_like(ref)

    for at, row in rows:
        ref[at : at + 1, :] += row


def turn_kernel(
    hidden_ref, back_ref, cotangent_ref, out_ref, table_ref, grad_ref, branch_ref, mixed_grad_ref, sums_ref
):
    low_in = cotangent_ref[...]
    part, gain_grad, shift_grad = norm_back(hidden_ref[...], back_ref[...], row_of(table_ref, GAIN + 2))
    grad = low_in.astype(f32) + part
    grad_ref[...] = grad
    low = grad.astype(bf16)
    branch_ref[...] = low
    mixed_grad_ref[...] = nt(low, out_ref[...]).astype(bf16)
    add_rows(
        sums_ref,
        ((0, gain_grad), (1, shift_grad), (2, column_sum(low_in)), (3, column_sum(low))),
    )


def turn(hidden, back, cotangent, weights, table):
    tokens, width = hidden.shape
    block = by_rows((ROWS, width))
    return pl.pallas_call(
        turn_kernel,
        grid=(tokens // ROWS,),
        in_specs=[block, block, block, held((width, width), (0, 4)), held(table.shape)],
        out_specs=[block, block, block, pl.BlockSpec((8, width), lambda j: (0, 0))],
        out_shape=[
            out((tokens, width), f32),
            out((tokens, width), bf16),
            out((tokens, width), bf16),
            out((8, width), f32),
        ],
        compiler_params=params(),
        cost_estimate=cost(2 * tokens * width * width, 18 * tokens * width + 2 * width * width),
        name="norm_back_cross_out_back",
    )(hidden, back, cotangent, weights, table)


def result_kernel(hidden_ref, made_ref, table_ref, result_ref):
    result_ref[...] = (hidden_ref[...] + made_ref[...] + row_of(table_ref, BIAS + 6)).astype(bf16)


def layer_result(hidden, made, table, waits=()):
    tokens, width = hidden.shape
    block = by_rows((ROWS, width))
    kernel, in_specs = after(waits, result_kernel, [block, block, held(table.shape)])
    return pl.pallas_call(
        kernel,
        grid=(tokens // ROWS,),
        in_specs=in_specs,
        out_specs=block,
        out_shape=out((tokens, width), bf16),
        compiler_params=params(),
        cost_estimate=cost(0, 10 * tokens * width),
        name="layer_result",
    )(*waits, hidden, made, table)


def middle_back_kernel(
    hidden_ref, grad_ref, query_grad_ref, query_ref, out_ref, table_ref,
    next_ref, branch_ref, mixed_grad_ref, sums_ref,
):
    incoming = nt(query_grad_ref[...], query_ref[...])
    part, gain_grad, shift_grad = norm_back(hidden_ref[...], incoming, row_of(table_ref, GAIN + 1))
    grad = grad_ref[...] + part
    next_ref[...] = grad
    low = grad.astype(bf16)
    branch_ref[...] = low
    mixed_grad_ref[...] = nt(low, out_ref[...]).astype(bf16)
    add_rows(
        sums_ref,
        ((0, gain_grad), (1, shift_grad), (3, column_sum(low))),
    )


def middle_back(hidden, grad, query_grad, weights, table, waits=()):
    tokens, width = hidden.shape
    block = by_rows((ROWS, width))
    kernel, in_specs = after(
        waits,
        middle_back_kernel,
        [
            block,
            block,
            block,
            held((width, width), (0, 1)),
            held((width, width), (0, 0)),
            held(table.shape),
        ],
    )
    return pl.pallas_call(
        kernel,
        grid=(tokens // ROWS,),
        in_specs=in_specs,
        out_specs=[block, block, block, pl.BlockSpec((8, width), lambda j: (0, 0))],
        out_shape=[
            out((tokens, width), f32),
            out((tokens, width), bf16),
            out((tokens, width), bf16),
            out((8, width), f32),
        ],
        compiler_params=params(),
        cost_estimate=cost(4 * tokens * width * width, 20 * tokens * width + 4 * width * width),
        name="query_norm_back_self_out_back",
    )(*waits, hidden, grad, query_grad, weights, weights, table)


def entry_back_kernel(x_ref, grad_ref, weight_ref, table_ref, *refs):
    grads, (input_grad_ref, sums_ref) = refs[:-2], refs[-2:]
    incoming, at = 0.0, 0
    for ref in grads:
        columns = ref.shape[1]
        incoming += nt(ref[...], weight_ref[:, at : at + columns])
        at += columns
    part, gain_grad, shift_grad = norm_back(x_ref[...].astype(f32), incoming, row_of(table_ref, GAIN))
    input_grad_ref[...] = grad_ref[...] + part
    add_rows(sums_ref, ((0, gain_grad), (1, shift_grad)))


def entry_back(x, grad, grads, weights, table, waits=()):
    tokens, width = x.shape
    block = by_rows((ROWS, width))
    kernel, in_specs = after(
        waits,
        entry_back_kernel,
        [block, block, held(weights.shape), held(table.shape)]
        + [by_rows((ROWS, part.shape[1])) for part in grads],
    )
    return pl.pallas_call(
        kernel,
        grid=(tokens // ROWS,),
        in_specs=in_specs,
        out_specs=[block, pl.BlockSpec((8, width), lambda j: (0, 0))],
        out_shape=[out((tokens, width), f32), out((8, width), f32)],
        compiler_params=params(),
        cost_estimate=cost(6 * tokens * width * width, 16 * tokens * width + 6 * width * width),
        name="qkv_norm_back",
    )(*waits, x, grad, weights, table, *grads)


def memory_back_kernel(key_grad_ref, value_grad_ref, weight_ref, memory_grad_ref):
    width = key_grad_ref.shape[1]
    made = nt(key_grad_ref[...], weight_ref[:, :width])
    memory_grad_ref[...] = made + nt(value_grad_ref[...], weight_ref[:, width:])


def memory_back(key_grad, value_grad, weights, waits=()):
    tokens, width = key_grad.shape
    block = by_rows((ROWS, width))
    kernel, in_specs = after(
        waits, memory_back_kernel, [block, block, held((width, 2 * width), (0, 1))]
    )
    return pl.pallas_call(
        kernel,
        grid=(tokens // ROWS,),
        in_specs=in_specs,
        out_specs=block,
        out_shape=out((tokens, width), f32),
        compiler_params=params(),
        cost_estimate=cost(4 * tokens * width * width, 8 * tokens * width + 4 * width * width, 0, 64),
        name="memory_back",
    )(*waits, key_grad, value_grad, weights)


def weight_grads_kernel(picks, *refs):
    step = pl.program_id(0)
    grads_ref = refs[-1]
    half, wide = grads_ref.shape[0] // 2, grads_ref.shape[1]
    for at, (left, right, column) in enumerate(picks):

        @pl.when(step == at)
        def _(left=left, right=right, column=column):
            for low in (0, half):
                grads_ref[low : low + half, :] = tn(
                    refs[left][:, low : low + half], refs[right][:, column : column + wide]
                ).astype(bf16)


def spread(made, first_pair, own, dp_size, me_ref, keep_ref, send_ref, columns):
    mine = me_ref[0]
    upper = lax.rem(mine, 2) == 1
    planes = keep_ref.shape[0] // own // dp_size
    mine_plane = lax.rem(lax.shift_right_logical(mine, 1), planes)
    for piece in range(made.shape[0] // (2 * own)):
        pair = first_pair + piece
        away = lax.bitwise_xor(mine_plane, pair % planes)
        place = away * dp_size + pair // planes
        span = pl.ds(pl.multiple_of(place * own, own), own)
        one = made[2 * own * piece : 2 * own * piece + own]
        two = made[2 * own * piece + own : 2 * own * (piece + 1)]
        keep_ref[span, columns] = jnp.where(upper, two, one)
        send_ref[span, columns] = jnp.where(upper, one, two)


def small_grads_kernel(one_ref, two_ref, three_ref, cross_ref, self_ref, hidden_ref, rows_ref):
    rows_ref[...] = jnp.zeros_like(rows_ref)
    places = [(GAIN, one_ref, 0), (GAIN + 1, two_ref, 0), (GAIN + 2, three_ref, 0)]
    places += [(SHIFT, one_ref, 1), (SHIFT + 1, two_ref, 1), (SHIFT + 2, three_ref, 1)]
    places += [(BIAS, self_ref, 0), (BIAS + 1, self_ref, 1), (BIAS + 2, two_ref, 3), (BIAS + 3, cross_ref, 0)]
    places += [(BIAS + 4, cross_ref, 1), (BIAS + 5, three_ref, 3), (BIAS + 6, three_ref, 2)]
    for at, ref, row in places:
        rows_ref[at : at + 1, :] = ref[row : row + 1, :]
    for step in range(hidden_ref.shape[0]):
        rows_ref[HIDDEN_BIAS + step : HIDDEN_BIAS + step + 1, :] = hidden_ref[step, 0:1, :]


def small_grads(*sums):
    width = sums[0].shape[1]
    return pl.pallas_call(
        small_grads_kernel,
        out_shape=out((24, width), f32),
        compiler_params=params(),
        name="small_grads",
    )(*sums)


def split_grads_kernel(picks, dp_size, own, count, me_ref, *refs):
    step = pl.program_id(0)
    keep_ref, send_ref = refs[count : count + 2]
    held_refs, sems = refs[count + 2 : -1], refs[-1]
    half, wide = keep_ref.shape
    copies = [pltpu.make_async_copy(refs[i], held_refs[i], sems.at[i]) for i in range(count)]

    @pl.when(step == 0)
    def _():
        for copy in copies:
            copy.start()

    known = set()
    for at, (left, right, column) in enumerate(picks):
        fresh = sorted({left, right} - known)
        known.update(fresh)

        @pl.when(step == at)
        def _(left=left, right=right, column=column, fresh=fresh):
            for i in fresh:
                copies[i].wait()
            for low in (0, half):
                made = tn(held_refs[left][:, low : low + half], held_refs[right][:, column : column + wide])
                first_pair = low // (2 * own)
                spread(made.astype(bf16), first_pair, own, dp_size, me_ref, keep_ref, send_ref, slice(0, wide))


def weight_grads(pairs, split=None, waits=(), wide=1024):
    arrays, picks = [], []
    for left, right in pairs:
        at = []
        for array in (left, right):
            known = [i for i, other in enumerate(arrays) if other is array]
            if not known:
                arrays.append(array)
            at.append(known[0] if known else len(arrays) - 1)
        picks += [(at[0], at[1], column) for column in range(0, right.shape[1], wide)]
    width = pairs[0][0].shape[1]
    columns = sum(right.shape[1] for _, right in pairs)
    flops = sum(2 * left.shape[0] * width * right.shape[1] for left, right in pairs)
    nbytes = 2 * sum(a.size for a in arrays) + 2 * width * columns
    if split is None:
        return pl.pallas_call(
            functools.partial(weight_grads_kernel, tuple(picks)),
            grid=(len(picks),),
            in_specs=[held(array.shape) for array in arrays],
            out_specs=pl.BlockSpec((width, wide), lambda j: (0, j)),
            out_shape=out((width, columns), bf16),
            compiler_params=params(),
            cost_estimate=cost(flops, nbytes),
            name="weight_grads",
        )(*arrays)
    mine, dp_size, own = split
    half = pl.BlockSpec((width // 2, wide), lambda j: (0, j))
    kernel, in_specs = after(
        waits,
        functools.partial(split_grads_kernel, tuple(picks), dp_size, own, len(arrays)),
        [pl.BlockSpec(memory_space=pltpu.SMEM)] + [pl.BlockSpec(memory_space=pl.ANY)] * len(arrays),
    )
    return pl.pallas_call(
        kernel,
        grid=(len(picks),),
        in_specs=in_specs,
        out_specs=[half, half],
        out_shape=[out((width // 2, columns), bf16)] * 2,
        scratch_shapes=[pltpu.VMEM(array.shape, bf16) for array in arrays]
        + [pltpu.SemaphoreType.DMA((len(arrays),))],
        compiler_params=params(),
        cost_estimate=cost(flops, nbytes),
        name="weight_grads_by_distance",
    )(*waits, mine, *arrays)


def two_rows_kernel(line_x_ref, line_y_ref, got_x_ref, got_y_ref, first_x_ref, first_y_ref):
    rows = line_x_ref.shape[0]
    first_x_ref[:rows] = line_x_ref[...]
    first_x_ref[rows:] = got_x_ref[...]
    first_y_ref[:rows] = line_y_ref[...]
    first_y_ref[rows:] = got_y_ref[...]


def two_rows(line, got_x, got_y, waits=()):
    rows, own, columns = got_x.shape
    lanes = 1280
    steps = columns // lanes
    low = pl.BlockSpec((rows, own, lanes), lambda j: (0, 0, j))
    high = pl.BlockSpec((rows, own, lanes), lambda j: (0, 0, j + steps))
    kernel, in_specs = after(waits, two_rows_kernel, [low, high, low, low])
    return pl.pallas_call(
        kernel,
        grid=(steps,),
        in_specs=in_specs,
        out_specs=[pl.BlockSpec((2 * rows, own, lanes), lambda j: (0, 0, j))] * 2,
        out_shape=[out((2 * rows, own, columns), bf16)] * 2,
        compiler_params=params(),
        cost_estimate=cost(0, 8 * rows * own * columns),
        name="two_rows",
    )(*waits, line, line, got_x, got_y)


def near_kernel(steps, first_x_ref, first_x_got_ref, first_y_ref, first_y_got_ref, whole_ref):
    step = pl.program_id(0)
    rows = first_x_ref.shape[0] // 2

    def put(place, ref, at):
        whole_ref[place * rows : (place + 1) * rows] = ref[at * rows : (at + 1) * rows]

    @pl.when(step < steps)
    def _():
        for place, ref, at in ((0, first_x_ref, 0), (1, first_x_ref, 1), (2, first_x_got_ref, 0), (3, first_x_got_ref, 1)):
            put(place, ref, at)

    @pl.when(step >= steps)
    def _():
        for place, ref, at in ((0, first_y_ref, 0), (2, first_y_ref, 1), (1, first_y_got_ref, 0), (3, first_y_got_ref, 1)):
            put(place, ref, at)


def near_rows(first_x, first_x_got, first_y, first_y_got, waits=()):
    rows, own, columns = first_x.shape
    lanes = 1280
    steps = columns // lanes
    low = pl.BlockSpec((rows, own, lanes), lambda j: (0, 0, jnp.minimum(j, steps - 1)))
    high = pl.BlockSpec((rows, own, lanes), lambda j: (0, 0, jnp.maximum(j - steps, 0)))
    kernel, in_specs = after(waits, functools.partial(near_kernel, steps), [low, low, high, high])
    return pl.pallas_call(
        kernel,
        grid=(2 * steps,),
        in_specs=in_specs,
        out_specs=pl.BlockSpec((2 * rows, own, lanes), lambda j: (0, 0, j)),
        out_shape=out((2 * rows, own, 2 * columns), bf16),
        compiler_params=params(),
        cost_estimate=cost(0, 8 * rows * own * columns),
        name="near_rows",
    )(*waits, first_x, first_x_got, first_y, first_y_got)


def place_kernel(dp_size, me_ref, near_ref, far_ref, whole_ref):
    pairs, own = near_ref.shape[:2]
    planes = pairs // dp_size
    mine = me_ref[0]
    side = lax.rem(mine, 2)
    mine_pair = lax.shift_right_logical(mine, 1)
    for at in range(pairs):
        pair = lax.bitwise_xor(mine_pair, at % dp_size * planes + at // dp_size)
        for ref, core in ((near_ref, side), (far_ref, 1 - side)):
            rows = pl.ds(pl.multiple_of((2 * pair + core) * own, own), own)
            whole_ref[rows, :] = ref[at]


def place(mine, near, far, dp_size):
    pairs, own, columns = near.shape
    lanes = 1024
    block = pl.BlockSpec((pairs, own, lanes), lambda j: (0, 0, j))
    return pl.pallas_call(
        functools.partial(place_kernel, dp_size),
        grid=(columns // lanes,),
        in_specs=[pl.BlockSpec(memory_space=pltpu.SMEM), block, block],
        out_specs=pl.BlockSpec((2 * pairs * own, lanes), lambda j: (0, j)),
        out_shape=out((2 * pairs * own, columns), bf16),
        compiler_params=params(),
        cost_estimate=cost(0, 8 * pairs * own * columns),
        name="place_by_device",
    )(mine, near, far)


def feed_own_kernel(*refs):
    owned, (inner_ref, outer_ref) = refs[:-2], refs[-2:]
    own, width = owned[0].shape[0], outer_ref.shape[1]
    tiles = [
        (ref, at * width) for ref in owned for at in range(0, ref.shape[1] // width, 2)
    ]
    for step, (ref, at) in enumerate(tiles):
        outer_ref[step * own : (step + 1) * own, :] = ref[:, at + width : at + 2 * width].astype(f32)
    for device in range(width // own):
        pieces = [ref[:, at + device * own : at + (device + 1) * own].astype(f32) for ref, at in tiles]
        span = len(tiles) * own
        inner_ref[:, device * span : (device + 1) * span] = jnp.concatenate(pieces, axis=1)


def feed_own_grads(owned, width, waits=()):
    own = owned[0].shape[0]
    steps = sum(part.shape[1] for part in owned) // (2 * width)
    vmem = pl.BlockSpec(memory_space=pltpu.VMEM)
    kernel, in_specs = after(waits, feed_own_kernel, [vmem] * len(owned))
    return pl.pallas_call(
        kernel,
        in_specs=in_specs,
        out_shape=[out((own, steps * width), f32), out((steps * own, width), f32)],
        compiler_params=params(),
        name="feed_own_grads",
    )(*waits, *owned)


def cut_kernel(cuts, whole_ref, *outs):
    for ref, (low, high) in zip(outs, cuts):
        ref[...] = whole_ref[:, low:high].astype(f32)


def cut_columns(whole, ends, waits=()):
    cuts = tuple(zip(ends[:-1], ends[1:]))
    own = whole.shape[0]
    vmem = pl.BlockSpec(memory_space=pltpu.VMEM)
    kernel, in_specs = after(waits, functools.partial(cut_kernel, cuts), [vmem])
    return pl.pallas_call(
        kernel,
        in_specs=in_specs,
        out_shape=[out((own, high - low), f32) for low, high in cuts],
        compiler_params=params(),
        name="own_columns",
    )(*waits, whole)


def plane_pieces_kernel(count, ranges, keep_ref, got_ref, *outs):
    rows = keep_ref.shape[0] // count
    for at, (low, high) in enumerate(ranges):
        for k in range(count):
            span = slice(k * rows, (k + 1) * rows)
            made = keep_ref[span, low:high].astype(f32) + got_ref[span, low:high].astype(f32)
            outs[at * count + k][...] = made.astype(bf16)


def lanes_of(columns):
    return next(n for n in (2048, 1664, 1408, 1280, 1024, 128) if columns % n == 0)


def plane_pieces(keep, got, count, waits, ends):
    rows, columns = keep.shape
    ranges = tuple(zip(ends[:-1], ends[1:]))
    if len(ranges) == 1:
        lanes = lanes_of(columns)
        steps, shapes, ranges = columns // lanes, [(columns, lanes)], ((0, lanes),)
    else:
        lanes, steps, shapes = columns, 1, [(high - low, high - low) for low, high in ranges]
    block = pl.BlockSpec((rows, lanes), lambda j: (0, j))
    kernel, in_specs = after(
        waits, functools.partial(plane_pieces_kernel, count, ranges), [block, block]
    )
    return pl.pallas_call(
        kernel,
        grid=(steps,),
        in_specs=in_specs,
        out_specs=[
            pl.BlockSpec((rows // count, n), lambda j: (0, j)) for _, n in shapes for _ in range(count)
        ],
        out_shape=[out((rows // count, n), bf16) for n, _ in shapes for _ in range(count)],
        compiler_params=params(),
        cost_estimate=cost(0, 6 * rows * columns),
        name="plane_pieces",
    )(*waits, keep, got)


def plane_total_kernel(*refs):
    total = refs[0][...].astype(f32)
    for ref in refs[1:-1]:
        total = total + ref[...].astype(f32)
    refs[-1][...] = total.astype(bf16)


def plane_total(pieces, waits=(), weight=0):
    rows, columns = pieces[0].shape
    lanes = lanes_of(columns)
    block = pl.BlockSpec((rows, lanes), lambda j: (0, j))
    kernel, in_specs = after(waits, plane_total_kernel, [block] * len(pieces))
    return pl.pallas_call(
        kernel,
        grid=(columns // lanes,),
        in_specs=in_specs,
        out_specs=block,
        out_shape=out((rows, columns), bf16),
        compiler_params=params(),
        cost_estimate=cost(weight * rows * columns, 2 * (len(pieces) + 1) * rows * columns),
        name="plane_total",
    )(*waits, *pieces)


def prepare_kernel(
    qkv_ref, out_ref, query_ref, pair_ref, cross_ref, inner_ref, outer_ref, gains_ref, shifts_ref, biases_ref, hidden_ref,
    first_ref, second_ref, third_ref,
):
    own, width = out_ref.shape
    steps = inner_ref.shape[1] // width
    devices = width // own
    rows = [gains_ref[...].astype(f32), shifts_ref[...].astype(f32), biases_ref[...].astype(f32)]
    hidden = hidden_ref[...].astype(f32)
    rows += [hidden[:, step * own : (step + 1) * own] for step in range(steps)]
    rows += [jnp.zeros((SMALL - HIDDEN_BIAS - steps, own), f32)]
    first_ref[:, : 3 * width] = qkv_ref[...]
    first_ref[:, 3 * width :] = jnp.concatenate(rows, axis=0).T.astype(bf16)
    second_ref[:, :width] = out_ref[...]
    second_ref[:, width : 2 * width] = query_ref[...]
    second_ref[:, 2 * width : 4 * width] = pair_ref[...]
    second_ref[:, 4 * width :] = cross_ref[...]
    for step in range(steps):
        pieces = [
            inner_ref[:, (device * steps + step) * own : (device * steps + step + 1) * own].astype(f32)
            for device in range(devices)
        ]
        third_ref[:, 2 * step * width : (2 * step + 1) * width] = jnp.concatenate(pieces, axis=1).astype(bf16)
        third_ref[:, (2 * step + 1) * width : (2 * step + 2) * width] = outer_ref[step * own : (step + 1) * own, :]


def prepare(*shards):
    own, width = shards[1].shape
    steps = shards[5].shape[1] // width
    return pl.pallas_call(
        prepare_kernel,
        out_shape=[
            out((own, 3 * width + SMALL), bf16),
            out((own, 5 * width), bf16),
            out((own, 2 * steps * width), bf16),
        ],
        compiler_params=params(),
        name="shards_to_gather",
    )(*shards)


AXES = ("dp", "fsdp")


def gather(shard):
    return lax.all_gather(shard, AXES, axis=0, tiled=True)


def scatter_sum(whole):
    return lax.psum_scatter(whole, AXES, scatter_dimension=0, tiled=True)


def exchange(array, axis, size, distance):
    return lax.ppermute(array, axis, [(i, i ^ distance) for i in range(size)])


def sum_along(sums, axis, size):
    distance = 1
    while distance < size:
        sums = sums + exchange(sums, axis, size, distance)
        distance *= 2
    return sums


def small_sum(sums, own, dp_size, fsdp_size):
    kept = sum_along(sums, "fsdp", fsdp_size)
    start = (lax.axis_index("dp") * fsdp_size + lax.axis_index("fsdp")) * own
    return lax.dynamic_slice_in_dim(kept, start, own, axis=1)


def add_low(left, right):
    return (left.astype(f32) + right.astype(f32)).astype(bf16)


def scatter_plane(keep, got, fsdp_size, waits=(), cut=()):
    planes = fsdp_size // 2
    made = list(plane_pieces(keep, got, planes, waits, (0, *cut, keep.shape[1])))
    both = [made[at : at + planes] for at in range(0, len(made), planes)]
    return [
        (part[1:], part[:1] + [exchange(part[k], "fsdp", fsdp_size, 2 * k) for k in range(1, planes)])
        for part in both
    ]


def scatter_line(total):
    return lax.psum_scatter(total, "dp", scatter_dimension=0, tiled=True)


def local(
    inputs,
    memory,
    cotangent,
    target_lengths,
    memory_lengths,
    norm_gains,
    norm_biases,
    self_qkv,
    self_out,
    cross_query,
    cross_kv,
    cross_out,
    ffn_in,
    ffn_out,
    proj_biases,
    ffn_in_bias,
):
    width = inputs.shape[2]
    own = self_qkv.shape[0]
    devices = width // own
    steps = ffn_in.shape[1] // width
    dp_size, fsdp_size = lax.axis_size("dp"), lax.axis_size("fsdp")
    by_distance = own % 16 == 0 and fsdp_size == 8
    mine = (lax.axis_index("dp") * fsdp_size + lax.axis_index("fsdp")).astype(jnp.int32).reshape(1)
    split = (mine, dp_size, own) if by_distance else (mine,)

    if by_distance:
        first_shard, second_shard, feed_shard = prepare(
            self_qkv, self_out, cross_query, cross_kv, cross_out, ffn_in, ffn_out,
            norm_gains, norm_biases, proj_biases, ffn_in_bias.reshape(1, -1),
        )
    else:
        small = jnp.concatenate(
            [norm_gains, norm_biases, proj_biases, ffn_in_bias.reshape(steps, own)], axis=0
        )
        small = jnp.pad(small, ((0, SMALL - small.shape[0]), (0, 0))).T
        first_shard = jnp.concatenate([self_qkv, small], axis=1)
        second_shard = jnp.concatenate([self_out, cross_query, cross_kv, cross_out], axis=1)
        inner_shard = ffn_in.reshape(own, devices, steps, own).transpose(0, 2, 1, 3).reshape(own, steps, width)
        outer_shard = ffn_out.reshape(steps, own, width).transpose(1, 0, 2)
        feed_shard = jnp.concatenate([inner_shard, outer_shard], axis=2).reshape(own, 2 * steps * width)

    first = gather(first_shard)
    third = gather(feed_shard)
    x = inputs[0]
    rows = memory[0]
    branch = cotangent[0]
    waits = ()
    if by_distance:
        line = jnp.stack(
            [second_shard] + [exchange(second_shard, "dp", dp_size, k) for k in range(1, dp_size)]
        )
        side = line.shape[2] // 2
        got_x = exchange(line[:, :, :side], "fsdp", fsdp_size, 2)
        got_y = exchange(line[:, :, side:], "fsdp", fsdp_size, 4)
        first_x, first_y = two_rows(line, got_x, got_y, (first,))
        first_x_got = exchange(first_x, "fsdp", fsdp_size, 4)
        first_y_got = exchange(first_y, "fsdp", fsdp_size, 2)
        waits = (first_x, first_y)
    table = first[:, 3 * width :].astype(f32).T[:24]

    normed_one, triple = entry(x, first, table, waits)
    parts = [(triple, at * (width // PAIR), width) for at in range(3)]
    self_mixed, self_stats = attend(target_lengths, *parts, True)
    if by_distance:
        near = near_rows(first_x, first_x_got, first_y, first_y_got, (self_mixed,))
        second = place(mine, near, exchange(near, "fsdp", fsdp_size, 1), dp_size)
    else:
        second = gather(second_shard)
    pair = memory_pair(rows, second, table)
    hidden_one, normed_two, queries = middle(x, self_mixed, second, table)
    cross_parts = [(queries, 0, width), (pair, 0, width), (pair, width // PAIR, width)]
    cross_mixed, cross_stats = attend(memory_lengths, *cross_parts, False)
    hidden_two, normed_three = late(hidden_one, cross_mixed, second, table)
    made, back, hidden_bias_sums, *feed_grads = feed(normed_three, branch, third, table, split)
    grad_two, branch_two, mixed_grad, sums_three = turn(hidden_two, back, branch, second, table)
    waits = ()
    if by_distance:
        feed_got = exchange(feed_grads[1], "fsdp", fsdp_size, 1)
        [(feed_sent, feed_plane)] = scatter_plane(feed_grads[0], feed_got, fsdp_size, (sums_three,))
        waits = tuple(feed_sent)
    else:
        feed_own = scatter_sum(feed_grads[0])
    query_grad, key_grad, value_grad, cross_sums = attend_back(
        memory_lengths, *cross_parts, cross_mixed, mixed_grad, cross_stats, False, waits
    )
    cross_pairs = [
        (cross_mixed, branch_two),
        (normed_two, query_grad),
        (rows, key_grad),
        (rows, value_grad),
    ]
    waits = ()
    if by_distance:
        cross_keep, cross_send = weight_grads(cross_pairs, split)
        cross_got = exchange(cross_send, "fsdp", fsdp_size, 1)
        waits = (cross_send,)
    grad_one, branch_one, mixed_grad, sums_two = middle_back(
        hidden_one, grad_two, query_grad, second, table, waits
    )
    if by_distance:
        [(cross_sent, cross_plane)] = scatter_plane(cross_keep, cross_got, fsdp_size, (grad_one,))
        waits = tuple(cross_sent)
    *self_grads, self_sums = attend_back(
        target_lengths, *parts, self_mixed, mixed_grad, self_stats, True, waits
    )
    self_pairs = [(self_mixed, branch_one)] + [(normed_one, part) for part in self_grads]
    waits = ()
    if by_distance:
        feed_total = plane_total(feed_plane, (self_sums,))
        feed_own = scatter_line(feed_total)
        self_keep, self_send = weight_grads(self_pairs, split, (feed_total,))
        self_got = exchange(self_send, "fsdp", fsdp_size, 1)
        memory_grad = memory_back(key_grad, value_grad, second, (self_send,))
        [(self_sent, self_plane)] = scatter_plane(self_keep, self_got, fsdp_size, (memory_grad,))
        cross_total = plane_total(cross_plane, (self_sent[0],))
        cross_own = scatter_line(cross_total)
        waits = (*self_sent, cross_total)
    input_grad, sums_one = entry_back(x, grad_one, self_grads, first, table, waits)
    sums = small_grads(sums_one, sums_two, sums_three, cross_sums, self_sums, hidden_bias_sums)
    sums = sum_along(sums, "dp", dp_size)
    if by_distance:
        result = layer_result(hidden_two, made, table, (input_grad,))
        inner_own, outer_own = feed_own_grads([feed_own], width, (result,))
        cross_out_own, query_own, pair_own = cut_columns(
            cross_own, (0, width, 2 * width, 4 * width), (inner_own,)
        )
        self_total = plane_total(self_plane, (cross_out_own, sums))
        self_own = scatter_line(self_total)
        self_out_own, triple_own = cut_columns(self_own, (0, width, 4 * width))
    else:
        result = layer_result(hidden_two, made, table)
        memory_grad = memory_back(key_grad, value_grad, second)
        cross_own = scatter_sum(weight_grads(cross_pairs)).astype(f32)
        cross_out_own, query_own = cross_own[:, :width], cross_own[:, width : 2 * width]
        pair_own = cross_own[:, 2 * width :]
        self_own = scatter_sum(weight_grads(self_pairs)).astype(f32)
        self_out_own, triple_own = self_own[:, :width], self_own[:, width:]
        feed_own = feed_own.astype(f32).reshape(own, steps, 2, width)
        inner_own = feed_own[:, :, 0].reshape(own, steps, devices, own).transpose(0, 2, 1, 3)
        inner_own = inner_own.reshape(own, steps * width)
        outer_own = feed_own[:, :, 1].transpose(1, 0, 2).reshape(steps * own, width)
    small_own = small_sum(sums, own, dp_size, fsdp_size)
    return (
        result[None],
        input_grad[None],
        memory_grad[None],
        small_own[GAIN:SHIFT],
        small_own[SHIFT:BIAS],
        triple_own,
        self_out_own,
        query_own,
        pair_own,
        cross_out_own,
        inner_own,
        outer_own,
        small_own[BIAS:HIDDEN_BIAS],
        small_own[HIDDEN_BIAS : HIDDEN_BIAS + steps].reshape(steps * own),
    )


def solution(mesh):
    rows = P(AXES, None, None)
    lengths = P(AXES)
    split = P(AXES, None)
    features = P(None, AXES)
    return jax.shard_map(
        local,
        mesh=mesh,
        in_specs=(rows, rows, rows, lengths, lengths, features, features)
        + (split,) * 7
        + (features, lengths),
        out_specs=(rows, rows, rows, features, features) + (split,) * 7 + (features, lengths),
        check_vma=False,
    )
```

```python
import functools

import jax
import jax.numpy as jnp
from jax import lax
from jax.experimental import pallas as pl
from jax.experimental.pallas import tpu as pltpu
from jax.sharding import PartitionSpec as P

f32 = jnp.float32
bf16 = jnp.bfloat16

HEAD = 64
PAIR = 2 * HEAD
BLOCK = 256
ROWS = 256
SMALL = 128
eps_norm = 1e-05
masked_score = -1e30
gelu_slope = 0.7978845608028654
gelu_cubic = 0.044715
MiB = 1 << 20


def nn(left, right):
    return jnp.dot(left, right, preferred_element_type=f32)


def nt(left, right):
    return lax.dot_general(left, right, (((1,), (1,)), ((), ())), preferred_element_type=f32)


def tn(left, right):
    return lax.dot_general(left, right, (((0,), (0,)), ((), ())), preferred_element_type=f32)


def normalise(hidden):
    centred = hidden - jnp.mean(hidden, axis=-1, keepdims=True)
    spread = lax.rsqrt(jnp.mean(centred * centred, axis=-1, keepdims=True) + eps_norm)
    return centred * spread, spread


def norm_back(hidden, incoming, gain):
    normed, spread = normalise(hidden)
    scaled = incoming * gain
    part = spread * (
        scaled
        - jnp.mean(scaled, axis=-1, keepdims=True)
        - normed * jnp.mean(scaled * normed, axis=-1, keepdims=True)
    )
    gain_grad = jnp.sum(incoming * normed, axis=0, keepdims=True)
    shift_grad = jnp.sum(incoming, axis=0, keepdims=True)
    return part, gain_grad, shift_grad


def column_sum(gradient):
    return jnp.sum(gradient.astype(f32), axis=0, keepdims=True)


def params():
    return pltpu.CompilerParams(vmem_limit_bytes=60 * MiB)


def after(waits, kernel, in_specs):
    count = len(waits)

    def waiting(*refs):
        kernel(*refs[count:])

    return waiting, [pl.BlockSpec(memory_space=pl.ANY)] * count + in_specs


def cost(flops, nbytes, transcendentals=0, high=64):
    return pl.CostEstimate(
        flops=high * flops, bytes_accessed=high * nbytes, transcendentals=high * transcendentals
    )


def held(shape, at=None):
    place = (0,) * len(shape) if at is None else at
    return pl.BlockSpec(shape, lambda j: place, pipeline_mode=pl.Buffered(1))


def by_rows(shape):
    return pl.BlockSpec(shape, lambda j: (j, 0))


def out(shape, dtype):
    return jax.ShapeDtypeStruct(shape, dtype)


GAIN, SHIFT, BIAS, HIDDEN_BIAS = 0, 3, 6, 13


def row_of(table_ref, at):
    return table_ref[at : at + 1, :]


def entry_kernel(x_ref, weight_ref, table_ref, normed_ref, triple_ref):
    width = x_ref.shape[1]
    normed, _ = normalise(x_ref[...].astype(f32))
    low = (normed * row_of(table_ref, GAIN) + row_of(table_ref, SHIFT)).astype(bf16)
    normed_ref[...] = low
    for part in range(3):
        span = slice(part * width, (part + 1) * width)
        made = nn(low, weight_ref[:, span])
        if part == 0:
            made = made + row_of(table_ref, BIAS)
        if part == 2:
            made = made + row_of(table_ref, BIAS + 1)
        triple_ref[:, span] = made.astype(bf16)


def entry(x, weights, table, waits=()):
    tokens, width = x.shape
    kernel, in_specs = after(
        waits, entry_kernel, [by_rows((ROWS, width)), held(weights.shape), held(table.shape)]
    )
    return pl.pallas_call(
        kernel,
        grid=(tokens // ROWS,),
        in_specs=in_specs,
        out_specs=[by_rows((ROWS, width)), by_rows((ROWS, 3 * width))],
        out_shape=[out((tokens, width), bf16), out((tokens, 3 * width), bf16)],
        compiler_params=params(),
        cost_estimate=cost(6 * tokens * width * width, 10 * tokens * width + 6 * width * width, 0, 1),
        name="norm_and_qkv",
    )(*waits, x, weights, table)


def middle_kernel(x_ref, mixed_ref, out_ref, query_ref, table_ref, hidden_ref, normed_ref, made_ref):
    hidden = x_ref[...].astype(f32) + nn(mixed_ref[...], out_ref[...]) + row_of(table_ref, BIAS + 2)
    hidden_ref[...] = hidden
    normed, _ = normalise(hidden)
    low = (normed * row_of(table_ref, GAIN + 1) + row_of(table_ref, SHIFT + 1)).astype(bf16)
    normed_ref[...] = low
    made_ref[...] = (nn(low, query_ref[...]) + row_of(table_ref, BIAS + 3)).astype(bf16)


def middle(x, mixed, weights, table):
    tokens, width = x.shape
    block = by_rows((ROWS, width))
    return pl.pallas_call(
        middle_kernel,
        grid=(tokens // ROWS,),
        in_specs=[
            block,
            block,
            held((width, width), (0, 0)),
            held((width, width), (0, 1)),
            held(table.shape),
        ],
        out_specs=[block, block, block],
        out_shape=[out((tokens, width), f32), out((tokens, width), bf16), out((tokens, width), bf16)],
        compiler_params=params(),
        cost_estimate=cost(4 * tokens * width * width, 12 * tokens * width + 4 * width * width, 0, 1),
        name="self_out_norm_query",
    )(x, mixed, weights, weights, table)


def memory_kernel(memory_ref, weight_ref, table_ref, pair_ref):
    width = memory_ref.shape[1]
    rows = memory_ref[...]
    pair_ref[:, :width] = nn(rows, weight_ref[:, :width]).astype(bf16)
    pair_ref[:, width:] = (nn(rows, weight_ref[:, width:]) + row_of(table_ref, BIAS + 4)).astype(bf16)


def memory_pair(memory, weights, table):
    tokens, width = memory.shape
    return pl.pallas_call(
        memory_kernel,
        grid=(tokens // ROWS,),
        in_specs=[by_rows((ROWS, width)), held((width, 2 * width), (0, 1)), held(table.shape)],
        out_specs=by_rows((ROWS, 2 * width)),
        out_shape=out((tokens, 2 * width), bf16),
        compiler_params=params(),
        cost_estimate=cost(4 * tokens * width * width, 6 * tokens * width + 4 * width * width, 0, 1),
        name="memory_keys_values",
    )(memory, weights, table)


def late_kernel(hidden_ref, mixed_ref, out_ref, table_ref, next_ref, normed_ref):
    hidden = hidden_ref[...] + nn(mixed_ref[...], out_ref[...]) + row_of(table_ref, BIAS + 5)
    next_ref[...] = hidden
    normed, _ = normalise(hidden)
    normed_ref[...] = (normed * row_of(table_ref, GAIN + 2) + row_of(table_ref, SHIFT + 2)).astype(bf16)


def late(hidden, mixed, weights, table):
    tokens, width = hidden.shape
    block = by_rows((ROWS, width))
    return pl.pallas_call(
        late_kernel,
        grid=(tokens // ROWS,),
        in_specs=[block, block, held((width, width), (0, 4)), held(table.shape)],
        out_specs=[block, block],
        out_shape=[out((tokens, width), f32), out((tokens, width), bf16)],
        compiler_params=params(),
        cost_estimate=cost(2 * tokens * width * width, 12 * tokens * width + 2 * width * width, 0, 1),
        name="cross_out_norm",
    )(hidden, mixed, weights, table)


def head_operands(lane, side, query, key, key_bias):
    own = (lane < HEAD) if side == 0 else (lane >= HEAD)
    spare = lane == (HEAD if side == 0 else 0)
    zero = jnp.zeros((), bf16)
    query_own = jnp.where(own, query, zero)
    key_own = jnp.where(own, key, zero)
    query_wide = jnp.where(spare, jnp.ones((), bf16), query_own)
    key_wide = jnp.where(spare, key_bias, key_own)
    return own, query_own, query_wide, key_own, key_wide


def pair_operands(length_ref, query_ref, key_ref):
    lane = lax.broadcasted_iota(jnp.int32, (1, PAIR), 1)
    key_pos = lax.broadcasted_iota(jnp.int32, (key_ref.shape[0], 1), 0)
    key_bias = jnp.where(key_pos < length_ref[0], 0.0, masked_score).astype(bf16)
    query = query_ref[...] * jnp.asarray(HEAD**-0.5, bf16)
    key = key_ref[...]
    return lane, [head_operands(lane, side, query, key, key_bias) for side in (0, 1)]


def scores_by_key(key_wide, query_block, keys, allowed):
    scores = nt(key_wide[:keys], query_block)
    if allowed is None:
        return scores
    last = jnp.where(allowed, scores[keys - BLOCK :], masked_score)
    return last if keys == BLOCK else jnp.concatenate([scores[: keys - BLOCK], last], axis=0)


def causal_block():
    key = lax.broadcasted_iota(jnp.int32, (BLOCK, BLOCK), 0)
    query = lax.broadcasted_iota(jnp.int32, (BLOCK, BLOCK), 1)
    return key <= query


def attend_kernel(causal, length_ref, query_ref, key_ref, value_ref, mixed_ref, stat_ref):
    rows, keys_all = query_ref.shape[0], key_ref.shape[0]
    lane, heads = pair_operands(length_ref, query_ref, key_ref)
    value = value_ref[...]
    allowed = causal_block() if causal else None
    first = lane < HEAD
    value_wide = [jnp.where(heads[side][0], value, jnp.ones((), bf16)) for side in (0, 1)]
    block = BLOCK if causal else rows
    for at in range(0, rows, block):
        keys = at + block if causal else keys_all
        got, tops = [], []
        for side in (0, 1):
            _, _, query_wide, _, key_wide = heads[side]
            scores = scores_by_key(key_wide, query_wide[at : at + block], keys, allowed)
            top = jnp.max(scores, axis=0, keepdims=True)
            exponent = jnp.exp(scores - top)
            got.append(tn(exponent.astype(bf16), value_wide[side][:keys]))
            tops.append(top)
        total = jnp.where(first, got[1], got[0])
        mixed = jnp.where(first, got[0], got[1]) / pltpu.roll(total, HEAD, 1)
        mixed_ref[at : at + block, :] = mixed.astype(bf16)
        logs = jnp.log(total).T
        stat_ref[0, 0:1, at : at + block] = tops[0] + logs[HEAD : HEAD + 1]
        stat_ref[0, 1:2, at : at + block] = tops[1] + logs[0:1]


def pair_block(rows, column=0):
    return pl.BlockSpec((rows, PAIR), lambda j: (0, column + j))


def attend(lengths, query, key, value, causal):
    rows, keys, width = query[0].shape[0], key[0].shape[0], query[2]
    pairs = width // PAIR
    return pl.pallas_call(
        functools.partial(attend_kernel, causal),
        grid=(pairs,),
        in_specs=[
            pl.BlockSpec(memory_space=pltpu.SMEM),
            pair_block(rows, query[1]),
            pair_block(keys, key[1]),
            pair_block(keys, value[1]),
        ],
        out_specs=[pair_block(rows), pl.BlockSpec((1, 2, rows), lambda j: (j, 0, 0))],
        out_shape=[out((rows, width), bf16), out((pairs, 2, rows), f32)],
        compiler_params=params(),
        cost_estimate=cost(16 * rows * keys * width, 4 * (rows + keys) * width, 16 * rows * keys, 1),
        name="attend_causal" if causal else "attend_memory",
    )(lengths, query[0], key[0], value[0])


def attend_back_kernel(
    causal,
    length_ref,
    query_ref,
    key_ref,
    value_ref,
    mixed_ref,
    grad_ref,
    stat_ref,
    query_grad_ref,
    key_grad_ref,
    value_grad_ref,
    sums_ref,
    key_sum,
    value_sum,
):
    rows, keys_all = query_ref.shape[0], key_ref.shape[0]
    scale = HEAD**-0.5
    lane, heads = pair_operands(length_ref, query_ref, key_ref)
    value = value_ref[...]
    grad = grad_ref[...]
    inner = (grad.astype(f32) * mixed_ref[...].astype(f32)).T
    allowed = causal_block() if causal else None
    zero = jnp.zeros((), bf16)
    value_own = [jnp.where(heads[side][0], value, zero) for side in (0, 1)]
    grad_own = [jnp.where(heads[side][0], grad, zero) for side in (0, 1)]
    inner_sum = [
        jnp.sum(inner[side * HEAD : (side + 1) * HEAD], axis=0, keepdims=True) for side in (0, 1)
    ]
    block = BLOCK if causal else rows
    for at in range(rows - block, -1, -block):
        keys = at + block if causal else keys_all
        span = slice(at, at + block)
        sums = None
        for side in (0, 1):
            _, query_own, query_wide, key_own, key_wide = heads[side]
            scores = scores_by_key(key_wide, query_wide[span], keys, allowed)
            probs = jnp.exp(scores - stat_ref[0, side : side + 1, span])
            grad_probs = nt(value_own[side][:keys], grad[span])
            grad_scores = (probs * (grad_probs - inner_sum[side][:, span])).astype(bf16)
            parts = (
                tn(grad_scores, key_own[:keys]),
                nn(grad_scores, query_own[span]),
                nn(probs.astype(bf16), grad_own[side][span]),
            )
            sums = parts if sums is None else tuple(a + b for a, b in zip(sums, parts))
        query_low = (sums[0] * scale).astype(bf16)
        query_grad_ref[span, :] = query_low
        query_total = column_sum(query_low) + (0.0 if at == rows - block else query_total)
        if at == rows - block:
            key_sum[...] = sums[1]
            value_sum[...] = sums[2]
        else:
            key_sum[:keys] += sums[1]
            value_sum[:keys] += sums[2]
    key_grad_ref[...] = key_sum[...].astype(bf16)
    value_low = value_sum[...].astype(bf16)
    value_grad_ref[...] = value_low
    sums_ref[...] = jnp.zeros_like(sums_ref)
    sums_ref[0:1, :] = query_total
    sums_ref[1:2, :] = column_sum(value_low)


def attend_back(lengths, query, key, value, mixed, grad, stats, causal, waits=(), share=(0, 1)):
    rows, keys = query[0].shape[0], key[0].shape[0]
    pairs = query[2] // PAIR // share[1]
    first, width = share[0] * pairs, pairs * PAIR
    kernel, in_specs = after(
        waits,
        functools.partial(attend_back_kernel, causal),
        [
            pl.BlockSpec(memory_space=pltpu.SMEM),
            pair_block(rows, query[1] + first),
            pair_block(keys, key[1] + first),
            pair_block(keys, value[1] + first),
            pair_block(rows, first),
            pair_block(rows, first),
            pl.BlockSpec((1, 2, rows), lambda j: (first + j, 0, 0)),
        ],
    )
    return pl.pallas_call(
        kernel,
        grid=(pairs,),
        in_specs=in_specs,
        out_specs=[pair_block(rows), pair_block(keys), pair_block(keys), pair_block(8)],
        out_shape=[
            out((rows, width), bf16),
            out((keys, width), bf16),
            out((keys, width), bf16),
            out((8, width), f32),
        ],
        scratch_shapes=[pltpu.VMEM((keys, PAIR), f32), pltpu.VMEM((keys, PAIR), f32)],
        compiler_params=params(),
        cost_estimate=cost(24 * rows * keys * width, 8 * (rows + keys) * width, 16 * rows * keys),
        name="attend_causal_back" if causal else "attend_memory_back",
    )(*waits, lengths, query[0], key[0], value[0], mixed, grad, stats)


FEED_ROWS = 512


def feed_kernel(
    split, me_ref, normed_ref, branch_ref, weight_ref, table_ref, made_ref, back_ref, bias_ref, *refs
):
    turned, act, dact = refs[-3:]
    step = pl.program_id(0)
    tokens, width = normed_ref.shape

    @pl.when(step == 0)
    def _():
        made_ref[...] = jnp.zeros_like(made_ref)
        back_ref[...] = jnp.zeros_like(back_ref)
        turned[...] = normed_ref[...].T

    bias = table_ref[pl.ds(HIDDEN_BIAS + step, 1), :]
    bias_sum = jnp.zeros((1, width), f32)
    for at in range(0, tokens, FEED_ROWS):
        span = slice(at, at + FEED_ROWS)
        inner = nn(normed_ref[span, :], weight_ref[:, :width]) + bias
        grad_active = nt(branch_ref[span, :], weight_ref[:, width:])
        square = inner * inner
        bent = jnp.tanh(inner * (gelu_slope + (gelu_slope * gelu_cubic) * square))
        half = 0.5 + 0.5 * bent
        active = (inner * half).astype(bf16)
        slope = half + (0.5 * inner) * (1.0 - bent * bent) * (
            gelu_slope + (3.0 * gelu_slope * gelu_cubic) * square
        )
        grad_inner = (grad_active * slope).astype(bf16)
        act[span, :] = active
        dact[span, :] = grad_inner
        bias_sum += column_sum(grad_inner)
        made_ref[span, :] += nn(active, weight_ref[:, width:])
        back_ref[span, :] += nt(grad_inner, weight_ref[:, :width])
    bias_ref[0] = jnp.broadcast_to(bias_sum, bias_ref.shape[1:])
    for at in range(0, width, FEED_ROWS):
        span = slice(at, at + FEED_ROWS)
        inner_part = nn(turned[span, :], dact[...]).astype(bf16)
        outer_part = tn(act[:, span], branch_ref[...]).astype(bf16)
        for part, columns in ((inner_part, slice(0, width)), (outer_part, slice(width, 2 * width))):
            if split is None:
                refs[0][span, columns] = part
            else:
                dp_size, own = split
                spread(part, at // (2 * own), own, dp_size, me_ref, refs[0], refs[1], columns)


def feed(normed, branch, weights, table, split):
    tokens, width = normed.shape
    steps = weights.shape[1] // (2 * width)
    hidden = steps * width
    whole = pl.BlockSpec((tokens, width), lambda j: (0, 0))
    tile = pl.BlockSpec((width, 2 * width), lambda j: (0, j))
    if split[1:]:
        grad_specs = [pl.BlockSpec((width // 2, 2 * width), lambda j: (0, j))] * 2
        grad_shapes = [out((width // 2, 2 * hidden), bf16)] * 2
    else:
        grad_specs, grad_shapes = [tile], [out((width, 2 * hidden), bf16)]
    return pl.pallas_call(
        functools.partial(feed_kernel, split[1:] or None),
        grid=(steps,),
        in_specs=[
            pl.BlockSpec(memory_space=pltpu.SMEM),
            held((tokens, width)),
            held((tokens, width)),
            tile,
            held(table.shape),
        ],
        out_specs=[whole, whole, pl.BlockSpec((1, 8, width), lambda j: (j, 0, 0))] + grad_specs,
        out_shape=[
            out((tokens, width), f32),
            out((tokens, width), f32),
            out((steps, 8, width), f32),
        ]
        + grad_shapes,
        scratch_shapes=[
            pltpu.VMEM((width, tokens), bf16),
            pltpu.VMEM((tokens, width), bf16),
            pltpu.VMEM((tokens, width), bf16),
        ],
        compiler_params=params(),
        cost_estimate=cost(
            12 * tokens * width * hidden, 8 * width * hidden + 12 * tokens * width, tokens * hidden
        ),
        name="feed_forward_both_ways",
    )(split[0], normed, branch, weights, table)


def add_rows(ref, rows):
    @pl.when(pl.program_id(0) == 0)
    def _():
        ref[...] = jnp.zeros_like(ref)

    for at, row in rows:
        ref[at : at + 1, :] += row


def turn_kernel(
    hidden_ref, back_ref, cotangent_ref, out_ref, table_ref, grad_ref, branch_ref, mixed_grad_ref, sums_ref
):
    low_in = cotangent_ref[...]
    part, gain_grad, shift_grad = norm_back(hidden_ref[...], back_ref[...], row_of(table_ref, GAIN + 2))
    grad = low_in.astype(f32) + part
    grad_ref[...] = grad
    low = grad.astype(bf16)
    branch_ref[...] = low
    mixed_grad_ref[...] = nt(low, out_ref[...]).astype(bf16)
    add_rows(
        sums_ref,
        ((0, gain_grad), (1, shift_grad), (2, column_sum(low_in)), (3, column_sum(low))),
    )


def turn(hidden, back, cotangent, weights, table):
    tokens, width = hidden.shape
    block = by_rows((ROWS, width))
    return pl.pallas_call(
        turn_kernel,
        grid=(tokens // ROWS,),
        in_specs=[block, block, block, held((width, width), (0, 4)), held(table.shape)],
        out_specs=[block, block, block, pl.BlockSpec((8, width), lambda j: (0, 0))],
        out_shape=[
            out((tokens, width), f32),
            out((tokens, width), bf16),
            out((tokens, width), bf16),
            out((8, width), f32),
        ],
        compiler_params=params(),
        cost_estimate=cost(2 * tokens * width * width, 18 * tokens * width + 2 * width * width),
        name="norm_back_cross_out_back",
    )(hidden, back, cotangent, weights, table)


def result_kernel(hidden_ref, made_ref, table_ref, result_ref):
    result_ref[...] = (hidden_ref[...] + made_ref[...] + row_of(table_ref, BIAS + 6)).astype(bf16)


def layer_result(hidden, made, table, waits=()):
    tokens, width = hidden.shape
    block = by_rows((ROWS, width))
    kernel, in_specs = after(waits, result_kernel, [block, block, held(table.shape)])
    return pl.pallas_call(
        kernel,
        grid=(tokens // ROWS,),
        in_specs=in_specs,
        out_specs=block,
        out_shape=out((tokens, width), bf16),
        compiler_params=params(),
        cost_estimate=cost(0, 10 * tokens * width),
        name="layer_result",
    )(*waits, hidden, made, table)


def middle_back_kernel(
    hidden_ref, grad_ref, query_grad_ref, query_ref, out_ref, table_ref,
    next_ref, branch_ref, mixed_grad_ref, sums_ref,
):
    incoming = nt(query_grad_ref[...], query_ref[...])
    part, gain_grad, shift_grad = norm_back(hidden_ref[...], incoming, row_of(table_ref, GAIN + 1))
    grad = grad_ref[...] + part
    next_ref[...] = grad
    low = grad.astype(bf16)
    branch_ref[...] = low
    mixed_grad_ref[...] = nt(low, out_ref[...]).astype(bf16)
    add_rows(
        sums_ref,
        ((0, gain_grad), (1, shift_grad), (3, column_sum(low))),
    )


def middle_back(hidden, grad, query_grad, weights, table, waits=()):
    tokens, width = hidden.shape
    block = by_rows((ROWS, width))
    kernel, in_specs = after(
        waits,
        middle_back_kernel,
        [
            block,
            block,
            block,
            held((width, width), (0, 1)),
            held((width, width), (0, 0)),
            held(table.shape),
        ],
    )
    return pl.pallas_call(
        kernel,
        grid=(tokens // ROWS,),
        in_specs=in_specs,
        out_specs=[block, block, block, pl.BlockSpec((8, width), lambda j: (0, 0))],
        out_shape=[
            out((tokens, width), f32),
            out((tokens, width), bf16),
            out((tokens, width), bf16),
            out((8, width), f32),
        ],
        compiler_params=params(),
        cost_estimate=cost(4 * tokens * width * width, 20 * tokens * width + 4 * width * width),
        name="query_norm_back_self_out_back",
    )(*waits, hidden, grad, query_grad, weights, weights, table)


def entry_back_kernel(x_ref, grad_ref, weight_ref, table_ref, *refs):
    grads, (input_grad_ref, sums_ref) = refs[:-2], refs[-2:]
    incoming, at = 0.0, 0
    for ref in grads:
        columns = ref.shape[1]
        incoming += nt(ref[...], weight_ref[:, at : at + columns])
        at += columns
    part, gain_grad, shift_grad = norm_back(x_ref[...].astype(f32), incoming, row_of(table_ref, GAIN))
    input_grad_ref[...] = grad_ref[...] + part
    add_rows(sums_ref, ((0, gain_grad), (1, shift_grad)))


def entry_back(x, grad, grads, weights, table, waits=()):
    tokens, width = x.shape
    block = by_rows((ROWS, width))
    kernel, in_specs = after(
        waits,
        entry_back_kernel,
        [block, block, held(weights.shape), held(table.shape)]
        + [by_rows((ROWS, part.shape[1])) for part in grads],
    )
    return pl.pallas_call(
        kernel,
        grid=(tokens // ROWS,),
        in_specs=in_specs,
        out_specs=[block, pl.BlockSpec((8, width), lambda j: (0, 0))],
        out_shape=[out((tokens, width), f32), out((8, width), f32)],
        compiler_params=params(),
        cost_estimate=cost(6 * tokens * width * width, 16 * tokens * width + 6 * width * width),
        name="qkv_norm_back",
    )(*waits, x, grad, weights, table, *grads)


def memory_back_kernel(key_grad_ref, value_grad_ref, weight_ref, memory_grad_ref):
    width = key_grad_ref.shape[1]
    made = nt(key_grad_ref[...], weight_ref[:, :width])
    memory_grad_ref[...] = made + nt(value_grad_ref[...], weight_ref[:, width:])


def memory_back(key_grad, value_grad, weights, waits=()):
    tokens, width = key_grad.shape
    block = by_rows((ROWS, width))
    kernel, in_specs = after(
        waits, memory_back_kernel, [block, block, held((width, 2 * width), (0, 1))]
    )
    return pl.pallas_call(
        kernel,
        grid=(tokens // ROWS,),
        in_specs=in_specs,
        out_specs=block,
        out_shape=out((tokens, width), f32),
        compiler_params=params(),
        cost_estimate=cost(4 * tokens * width * width, 8 * tokens * width + 4 * width * width, 0, 64),
        name="memory_back",
    )(*waits, key_grad, value_grad, weights)


def weight_grads_kernel(picks, *refs):
    step = pl.program_id(0)
    grads_ref = refs[-1]
    half, wide = grads_ref.shape[0] // 2, grads_ref.shape[1]
    for at, (left, right, column) in enumerate(picks):

        @pl.when(step == at)
        def _(left=left, right=right, column=column):
            for low in (0, half):
                grads_ref[low : low + half, :] = tn(
                    refs[left][:, low : low + half], refs[right][:, column : column + wide]
                ).astype(bf16)


def spread(made, first_pair, own, dp_size, me_ref, keep_ref, send_ref, columns):
    mine = me_ref[0]
    upper = lax.rem(mine, 2) == 1
    planes = keep_ref.shape[0] // own // dp_size
    mine_plane = lax.rem(lax.shift_right_logical(mine, 1), planes)
    for piece in range(made.shape[0] // (2 * own)):
        pair = first_pair + piece
        away = lax.bitwise_xor(mine_plane, pair % planes)
        place = away * dp_size + pair // planes
        span = pl.ds(pl.multiple_of(place * own, own), own)
        one = made[2 * own * piece : 2 * own * piece + own]
        two = made[2 * own * piece + own : 2 * own * (piece + 1)]
        keep_ref[span, columns] = jnp.where(upper, two, one)
        send_ref[span, columns] = jnp.where(upper, one, two)


def small_grads_kernel(one_ref, two_ref, three_ref, cross_ref, self_ref, hidden_ref, rows_ref):
    rows_ref[...] = jnp.zeros_like(rows_ref)
    places = [(GAIN, one_ref, 0), (GAIN + 1, two_ref, 0), (GAIN + 2, three_ref, 0)]
    places += [(SHIFT, one_ref, 1), (SHIFT + 1, two_ref, 1), (SHIFT + 2, three_ref, 1)]
    places += [(BIAS, self_ref, 0), (BIAS + 1, self_ref, 1), (BIAS + 2, two_ref, 3), (BIAS + 3, cross_ref, 0)]
    places += [(BIAS + 4, cross_ref, 1), (BIAS + 5, three_ref, 3), (BIAS + 6, three_ref, 2)]
    for at, ref, row in places:
        rows_ref[at : at + 1, :] = ref[row : row + 1, :]
    for step in range(hidden_ref.shape[0]):
        rows_ref[HIDDEN_BIAS + step : HIDDEN_BIAS + step + 1, :] = hidden_ref[step, 0:1, :]


def small_grads(*sums):
    width = sums[0].shape[1]
    return pl.pallas_call(
        small_grads_kernel,
        out_shape=out((24, width), f32),
        compiler_params=params(),
        name="small_grads",
    )(*sums)


def split_grads_kernel(picks, dp_size, own, count, me_ref, *refs):
    step = pl.program_id(0)
    keep_ref, send_ref = refs[count : count + 2]
    held_refs, sems = refs[count + 2 : -1], refs[-1]
    half, wide = keep_ref.shape
    copies = [pltpu.make_async_copy(refs[i], held_refs[i], sems.at[i]) for i in range(count)]

    @pl.when(step == 0)
    def _():
        for copy in copies:
            copy.start()

    known = set()
    for at, (left, right, column) in enumerate(picks):
        fresh = sorted({left, right} - known)
        known.update(fresh)

        @pl.when(step == at)
        def _(left=left, right=right, column=column, fresh=fresh):
            for i in fresh:
                copies[i].wait()
            for low in (0, half):
                made = tn(held_refs[left][:, low : low + half], held_refs[right][:, column : column + wide])
                first_pair = low // (2 * own)
                spread(made.astype(bf16), first_pair, own, dp_size, me_ref, keep_ref, send_ref, slice(0, wide))


def weight_grads(pairs, split=None, waits=(), wide=1024):
    arrays, picks = [], []
    for left, right in pairs:
        at = []
        for array in (left, right):
            known = [i for i, other in enumerate(arrays) if other is array]
            if not known:
                arrays.append(array)
            at.append(known[0] if known else len(arrays) - 1)
        picks += [(at[0], at[1], column) for column in range(0, right.shape[1], wide)]
    width = pairs[0][0].shape[1]
    columns = sum(right.shape[1] for _, right in pairs)
    flops = sum(2 * left.shape[0] * width * right.shape[1] for left, right in pairs)
    nbytes = 2 * sum(a.size for a in arrays) + 2 * width * columns
    if split is None:
        return pl.pallas_call(
            functools.partial(weight_grads_kernel, tuple(picks)),
            grid=(len(picks),),
            in_specs=[held(array.shape) for array in arrays],
            out_specs=pl.BlockSpec((width, wide), lambda j: (0, j)),
            out_shape=out((width, columns), bf16),
            compiler_params=params(),
            cost_estimate=cost(flops, nbytes),
            name="weight_grads",
        )(*arrays)
    mine, dp_size, own = split
    half = pl.BlockSpec((width // 2, wide), lambda j: (0, j))
    kernel, in_specs = after(
        waits,
        functools.partial(split_grads_kernel, tuple(picks), dp_size, own, len(arrays)),
        [pl.BlockSpec(memory_space=pltpu.SMEM)] + [pl.BlockSpec(memory_space=pl.ANY)] * len(arrays),
    )
    return pl.pallas_call(
        kernel,
        grid=(len(picks),),
        in_specs=in_specs,
        out_specs=[half, half],
        out_shape=[out((width // 2, columns), bf16)] * 2,
        scratch_shapes=[pltpu.VMEM(array.shape, bf16) for array in arrays]
        + [pltpu.SemaphoreType.DMA((len(arrays),))],
        compiler_params=params(),
        cost_estimate=cost(flops, nbytes),
        name="weight_grads_by_distance",
    )(*waits, mine, *arrays)


def two_rows_kernel(line_x_ref, line_y_ref, got_x_ref, got_y_ref, first_x_ref, first_y_ref):
    rows = line_x_ref.shape[0]
    first_x_ref[:rows] = line_x_ref[...]
    first_x_ref[rows:] = got_x_ref[...]
    first_y_ref[:rows] = line_y_ref[...]
    first_y_ref[rows:] = got_y_ref[...]


def two_rows(line, got_x, got_y, waits=()):
    rows, own, columns = got_x.shape
    lanes = 1280
    steps = columns // lanes
    low = pl.BlockSpec((rows, own, lanes), lambda j: (0, 0, j))
    high = pl.BlockSpec((rows, own, lanes), lambda j: (0, 0, j + steps))
    kernel, in_specs = after(waits, two_rows_kernel, [low, high, low, low])
    return pl.pallas_call(
        kernel,
        grid=(steps,),
        in_specs=in_specs,
        out_specs=[pl.BlockSpec((2 * rows, own, lanes), lambda j: (0, 0, j))] * 2,
        out_shape=[out((2 * rows, own, columns), bf16)] * 2,
        compiler_params=params(),
        cost_estimate=cost(0, 8 * rows * own * columns),
        name="two_rows",
    )(*waits, line, line, got_x, got_y)


def near_kernel(steps, first_x_ref, first_x_got_ref, first_y_ref, first_y_got_ref, whole_ref):
    step = pl.program_id(0)
    rows = first_x_ref.shape[0] // 2

    def put(place, ref, at):
        whole_ref[place * rows : (place + 1) * rows] = ref[at * rows : (at + 1) * rows]

    @pl.when(step < steps)
    def _():
        for place, ref, at in ((0, first_x_ref, 0), (1, first_x_ref, 1), (2, first_x_got_ref, 0), (3, first_x_got_ref, 1)):
            put(place, ref, at)

    @pl.when(step >= steps)
    def _():
        for place, ref, at in ((0, first_y_ref, 0), (2, first_y_ref, 1), (1, first_y_got_ref, 0), (3, first_y_got_ref, 1)):
            put(place, ref, at)


def near_rows(first_x, first_x_got, first_y, first_y_got, waits=()):
    rows, own, columns = first_x.shape
    lanes = 1280
    steps = columns // lanes
    low = pl.BlockSpec((rows, own, lanes), lambda j: (0, 0, jnp.minimum(j, steps - 1)))
    high = pl.BlockSpec((rows, own, lanes), lambda j: (0, 0, jnp.maximum(j - steps, 0)))
    kernel, in_specs = after(waits, functools.partial(near_kernel, steps), [low, low, high, high])
    return pl.pallas_call(
        kernel,
        grid=(2 * steps,),
        in_specs=in_specs,
        out_specs=pl.BlockSpec((2 * rows, own, lanes), lambda j: (0, 0, j)),
        out_shape=out((2 * rows, own, 2 * columns), bf16),
        compiler_params=params(),
        cost_estimate=cost(0, 8 * rows * own * columns),
        name="near_rows",
    )(*waits, first_x, first_x_got, first_y, first_y_got)


def place_kernel(dp_size, me_ref, near_ref, far_ref, whole_ref):
    pairs, own = near_ref.shape[:2]
    planes = pairs // dp_size
    mine = me_ref[0]
    side = lax.rem(mine, 2)
    mine_pair = lax.shift_right_logical(mine, 1)
    for at in range(pairs):
        pair = lax.bitwise_xor(mine_pair, at % dp_size * planes + at // dp_size)
        for ref, core in ((near_ref, side), (far_ref, 1 - side)):
            rows = pl.ds(pl.multiple_of((2 * pair + core) * own, own), own)
            whole_ref[rows, :] = ref[at]


def place(mine, near, far, dp_size):
    pairs, own, columns = near.shape
    lanes = 1024
    block = pl.BlockSpec((pairs, own, lanes), lambda j: (0, 0, j))
    return pl.pallas_call(
        functools.partial(place_kernel, dp_size),
        grid=(columns // lanes,),
        in_specs=[pl.BlockSpec(memory_space=pltpu.SMEM), block, block],
        out_specs=pl.BlockSpec((2 * pairs * own, lanes), lambda j: (0, j)),
        out_shape=out((2 * pairs * own, columns), bf16),
        compiler_params=params(),
        cost_estimate=cost(0, 8 * pairs * own * columns),
        name="place_by_device",
    )(mine, near, far)


def feed_own_kernel(*refs):
    owned, (inner_ref, outer_ref) = refs[:-2], refs[-2:]
    own, width = owned[0].shape[0], outer_ref.shape[1]
    tiles = [
        (ref, at * width) for ref in owned for at in range(0, ref.shape[1] // width, 2)
    ]
    for step, (ref, at) in enumerate(tiles):
        outer_ref[step * own : (step + 1) * own, :] = ref[:, at + width : at + 2 * width].astype(f32)
    for device in range(width // own):
        pieces = [ref[:, at + device * own : at + (device + 1) * own].astype(f32) for ref, at in tiles]
        span = len(tiles) * own
        inner_ref[:, device * span : (device + 1) * span] = jnp.concatenate(pieces, axis=1)


def feed_own_grads(owned, width, waits=()):
    own = owned[0].shape[0]
    steps = sum(part.shape[1] for part in owned) // (2 * width)
    vmem = pl.BlockSpec(memory_space=pltpu.VMEM)
    kernel, in_specs = after(waits, feed_own_kernel, [vmem] * len(owned))
    return pl.pallas_call(
        kernel,
        in_specs=in_specs,
        out_shape=[out((own, steps * width), f32), out((steps * own, width), f32)],
        compiler_params=params(),
        name="feed_own_grads",
    )(*waits, *owned)


def cut_kernel(cuts, whole_ref, *outs):
    for ref, (low, high) in zip(outs, cuts):
        ref[...] = whole_ref[:, low:high].astype(f32)


def cut_columns(whole, ends, waits=()):
    cuts = tuple(zip(ends[:-1], ends[1:]))
    own = whole.shape[0]
    vmem = pl.BlockSpec(memory_space=pltpu.VMEM)
    kernel, in_specs = after(waits, functools.partial(cut_kernel, cuts), [vmem])
    return pl.pallas_call(
        kernel,
        in_specs=in_specs,
        out_shape=[out((own, high - low), f32) for low, high in cuts],
        compiler_params=params(),
        name="own_columns",
    )(*waits, whole)


def plane_pieces_kernel(count, ranges, keep_ref, got_ref, *outs):
    rows = keep_ref.shape[0] // count
    for at, (low, high) in enumerate(ranges):
        for k in range(count):
            span = slice(k * rows, (k + 1) * rows)
            made = keep_ref[span, low:high].astype(f32) + got_ref[span, low:high].astype(f32)
            outs[at * count + k][...] = made.astype(bf16)


def lanes_of(columns):
    return next(n for n in (2048, 1664, 1408, 1280, 1024, 128) if columns % n == 0)


def plane_pieces(keep, got, count, waits, ends):
    rows, columns = keep.shape
    ranges = tuple(zip(ends[:-1], ends[1:]))
    if len(ranges) == 1:
        lanes = lanes_of(columns)
        steps, shapes, ranges = columns // lanes, [(columns, lanes)], ((0, lanes),)
    else:
        lanes, steps, shapes = columns, 1, [(high - low, high - low) for low, high in ranges]
    block = pl.BlockSpec((rows, lanes), lambda j: (0, j))
    kernel, in_specs = after(
        waits, functools.partial(plane_pieces_kernel, count, ranges), [block, block]
    )
    return pl.pallas_call(
        kernel,
        grid=(steps,),
        in_specs=in_specs,
        out_specs=[
            pl.BlockSpec((rows // count, n), lambda j: (0, j)) for _, n in shapes for _ in range(count)
        ],
        out_shape=[out((rows // count, n), bf16) for n, _ in shapes for _ in range(count)],
        compiler_params=params(),
        cost_estimate=cost(0, 6 * rows * columns),
        name="plane_pieces",
    )(*waits, keep, got)


def plane_total_kernel(*refs):
    total = refs[0][...].astype(f32)
    for ref in refs[1:-1]:
        total = total + ref[...].astype(f32)
    refs[-1][...] = total.astype(bf16)


def plane_total(pieces, waits=(), weight=0):
    rows, columns = pieces[0].shape
    lanes = lanes_of(columns)
    block = pl.BlockSpec((rows, lanes), lambda j: (0, j))
    kernel, in_specs = after(waits, plane_total_kernel, [block] * len(pieces))
    return pl.pallas_call(
        kernel,
        grid=(columns // lanes,),
        in_specs=in_specs,
        out_specs=block,
        out_shape=out((rows, columns), bf16),
        compiler_params=params(),
        cost_estimate=cost(weight * rows * columns, 2 * (len(pieces) + 1) * rows * columns),
        name="plane_total",
    )(*waits, *pieces)


def prepare_kernel(
    qkv_ref, out_ref, query_ref, pair_ref, cross_ref, inner_ref, outer_ref, gains_ref, shifts_ref, biases_ref, hidden_ref,
    first_ref, second_ref, third_ref,
):
    own, width = out_ref.shape
    steps = inner_ref.shape[1] // width
    devices = width // own
    rows = [gains_ref[...].astype(f32), shifts_ref[...].astype(f32), biases_ref[...].astype(f32)]
    hidden = hidden_ref[...].astype(f32)
    rows += [hidden[:, step * own : (step + 1) * own] for step in range(steps)]
    rows += [jnp.zeros((SMALL - HIDDEN_BIAS - steps, own), f32)]
    first_ref[:, : 3 * width] = qkv_ref[...]
    first_ref[:, 3 * width :] = jnp.concatenate(rows, axis=0).T.astype(bf16)
    second_ref[:, :width] = out_ref[...]
    second_ref[:, width : 2 * width] = query_ref[...]
    second_ref[:, 2 * width : 4 * width] = pair_ref[...]
    second_ref[:, 4 * width :] = cross_ref[...]
    for step in range(steps):
        pieces = [
            inner_ref[:, (device * steps + step) * own : (device * steps + step + 1) * own].astype(f32)
            for device in range(devices)
        ]
        third_ref[:, 2 * step * width : (2 * step + 1) * width] = jnp.concatenate(pieces, axis=1).astype(bf16)
        third_ref[:, (2 * step + 1) * width : (2 * step + 2) * width] = outer_ref[step * own : (step + 1) * own, :]


def prepare(*shards):
    own, width = shards[1].shape
    steps = shards[5].shape[1] // width
    return pl.pallas_call(
        prepare_kernel,
        out_shape=[
            out((own, 3 * width + SMALL), bf16),
            out((own, 5 * width), bf16),
            out((own, 2 * steps * width), bf16),
        ],
        compiler_params=params(),
        name="shards_to_gather",
    )(*shards)


AXES = ("dp", "fsdp")


def gather(shard):
    return lax.all_gather(shard, AXES, axis=0, tiled=True)


def scatter_sum(whole):
    return lax.psum_scatter(whole, AXES, scatter_dimension=0, tiled=True)


def exchange(array, axis, size, distance):
    return lax.ppermute(array, axis, [(i, i ^ distance) for i in range(size)])


def sum_along(sums, axis, size):
    distance = 1
    while distance < size:
        sums = sums + exchange(sums, axis, size, distance)
        distance *= 2
    return sums


def small_sum(sums, own, dp_size, fsdp_size):
    kept = sum_along(sums, "fsdp", fsdp_size)
    start = (lax.axis_index("dp") * fsdp_size + lax.axis_index("fsdp")) * own
    return lax.dynamic_slice_in_dim(kept, start, own, axis=1)


def add_low(left, right):
    return (left.astype(f32) + right.astype(f32)).astype(bf16)


def scatter_plane(keep, got, fsdp_size, waits=(), cut=()):
    planes = fsdp_size // 2
    made = list(plane_pieces(keep, got, planes, waits, (0, *cut, keep.shape[1])))
    both = [made[at : at + planes] for at in range(0, len(made), planes)]
    return [
        (part[1:], part[:1] + [exchange(part[k], "fsdp", fsdp_size, 2 * k) for k in range(1, planes)])
        for part in both
    ]


def scatter_line(total):
    return lax.psum_scatter(total, "dp", scatter_dimension=0, tiled=True)


def local(
    inputs,
    memory,
    cotangent,
    target_lengths,
    memory_lengths,
    norm_gains,
    norm_biases,
    self_qkv,
    self_out,
    cross_query,
    cross_kv,
    cross_out,
    ffn_in,
    ffn_out,
    proj_biases,
    ffn_in_bias,
):
    width = inputs.shape[2]
    own = self_qkv.shape[0]
    devices = width // own
    steps = ffn_in.shape[1] // width
    dp_size, fsdp_size = lax.axis_size("dp"), lax.axis_size("fsdp")
    by_distance = own % 16 == 0 and fsdp_size == 8
    mine = (lax.axis_index("dp") * fsdp_size + lax.axis_index("fsdp")).astype(jnp.int32).reshape(1)
    split = (mine, dp_size, own) if by_distance else (mine,)

    if by_distance:
        first_shard, second_shard, feed_shard = prepare(
            self_qkv, self_out, cross_query, cross_kv, cross_out, ffn_in, ffn_out,
            norm_gains, norm_biases, proj_biases, ffn_in_bias.reshape(1, -1),
        )
    else:
        small = jnp.concatenate(
            [norm_gains, norm_biases, proj_biases, ffn_in_bias.reshape(steps, own)], axis=0
        )
        small = jnp.pad(small, ((0, SMALL - small.shape[0]), (0, 0))).T
        first_shard = jnp.concatenate([self_qkv, small], axis=1)
        second_shard = jnp.concatenate([self_out, cross_query, cross_kv, cross_out], axis=1)
        inner_shard = ffn_in.reshape(own, devices, steps, own).transpose(0, 2, 1, 3).reshape(own, steps, width)
        outer_shard = ffn_out.reshape(steps, own, width).transpose(1, 0, 2)
        feed_shard = jnp.concatenate([inner_shard, outer_shard], axis=2).reshape(own, 2 * steps * width)

    first = gather(first_shard)
    third = gather(feed_shard)
    x = inputs[0]
    rows = memory[0]
    branch = cotangent[0]
    waits = ()
    if by_distance:
        line = jnp.stack(
            [second_shard] + [exchange(second_shard, "dp", dp_size, k) for k in range(1, dp_size)]
        )
        side = line.shape[2] // 2
        got_x = exchange(line[:, :, :side], "fsdp", fsdp_size, 2)
        got_y = exchange(line[:, :, side:], "fsdp", fsdp_size, 4)
        first_x, first_y = two_rows(line, got_x, got_y, (first,))
        first_x_got = exchange(first_x, "fsdp", fsdp_size, 4)
        first_y_got = exchange(first_y, "fsdp", fsdp_size, 2)
        waits = (first_x, first_y)
    table = first[:, 3 * width :].astype(f32).T[:24]

    normed_one, triple = entry(x, first, table, waits)
    parts = [(triple, at * (width // PAIR), width) for at in range(3)]
    self_mixed, self_stats = attend(target_lengths, *parts, True)
    if by_distance:
        near = near_rows(first_x, first_x_got, first_y, first_y_got, (self_mixed,))
        second = place(mine, near, exchange(near, "fsdp", fsdp_size, 1), dp_size)
    else:
        second = gather(second_shard)
    pair = memory_pair(rows, second, table)
    hidden_one, normed_two, queries = middle(x, self_mixed, second, table)
    cross_parts = [(queries, 0, width), (pair, 0, width), (pair, width // PAIR, width)]
    cross_mixed, cross_stats = attend(memory_lengths, *cross_parts, False)
    hidden_two, normed_three = late(hidden_one, cross_mixed, second, table)
    made, back, hidden_bias_sums, *feed_grads = feed(normed_three, branch, third, table, split)
    grad_two, branch_two, mixed_grad, sums_three = turn(hidden_two, back, branch, second, table)
    waits = ()
    if by_distance:
        feed_got = exchange(feed_grads[1], "fsdp", fsdp_size, 1)
        [(feed_sent, feed_plane)] = scatter_plane(feed_grads[0], feed_got, fsdp_size, (sums_three,))
        waits = tuple(feed_sent)
    else:
        feed_own = scatter_sum(feed_grads[0])
    query_grad, key_grad, value_grad, cross_sums = attend_back(
        memory_lengths, *cross_parts, cross_mixed, mixed_grad, cross_stats, False, waits
    )
    cross_pairs = [
        (cross_mixed, branch_two),
        (normed_two, query_grad),
        (rows, key_grad),
        (rows, value_grad),
    ]
    waits = ()
    if by_distance:
        cross_keep, cross_send = weight_grads(cross_pairs, split)
        cross_got = exchange(cross_send, "fsdp", fsdp_size, 1)
        waits = (cross_send,)
    grad_one, branch_one, mixed_grad, sums_two = middle_back(
        hidden_one, grad_two, query_grad, second, table, waits
    )
    if by_distance:
        [(cross_sent, cross_plane)] = scatter_plane(cross_keep, cross_got, fsdp_size, (grad_one,))
        waits = tuple(cross_sent)
    *self_grads, self_sums = attend_back(
        target_lengths, *parts, self_mixed, mixed_grad, self_stats, True, waits
    )
    self_pairs = [(self_mixed, branch_one)] + [(normed_one, part) for part in self_grads]
    waits = ()
    if by_distance:
        feed_total = plane_total(feed_plane, (self_sums,))
        feed_own = scatter_line(feed_total)
        self_keep, self_send = weight_grads(self_pairs, split, (feed_total,))
        self_got = exchange(self_send, "fsdp", fsdp_size, 1)
        memory_grad = memory_back(key_grad, value_grad, second, (self_send,))
        [(self_sent, self_plane)] = scatter_plane(self_keep, self_got, fsdp_size, (memory_grad,))
        cross_total = plane_total(cross_plane, (self_sent[0],))
        cross_own = scatter_line(cross_total)
        waits = (*self_sent, cross_total)
    input_grad, sums_one = entry_back(x, grad_one, self_grads, first, table, waits)
    sums = small_grads(sums_one, sums_two, sums_three, cross_sums, self_sums, hidden_bias_sums)
    sums = sum_along(sums, "dp", dp_size)
    if by_distance:
        result = layer_result(hidden_two, made, table, (input_grad,))
        inner_own, outer_own = feed_own_grads([feed_own], width, (result,))
        cross_out_own, query_own, pair_own = cut_columns(
            cross_own, (0, width, 2 * width, 4 * width), (inner_own,)
        )
        self_total = plane_total(self_plane, (cross_out_own, sums))
        self_own = scatter_line(self_total)
        self_out_own, triple_own = cut_columns(self_own, (0, width, 4 * width))
    else:
        result = layer_result(hidden_two, made, table)
        memory_grad = memory_back(key_grad, value_grad, second)
        cross_own = scatter_sum(weight_grads(cross_pairs)).astype(f32)
        cross_out_own, query_own = cross_own[:, :width], cross_own[:, width : 2 * width]
        pair_own = cross_own[:, 2 * width :]
        self_own = scatter_sum(weight_grads(self_pairs)).astype(f32)
        self_out_own, triple_own = self_own[:, :width], self_own[:, width:]
        feed_own = feed_own.astype(f32).reshape(own, steps, 2, width)
        inner_own = feed_own[:, :, 0].reshape(own, steps, devices, own).transpose(0, 2, 1, 3)
        inner_own = inner_own.reshape(own, steps * width)
        outer_own = feed_own[:, :, 1].transpose(1, 0, 2).reshape(steps * own, width)
    small_own = small_sum(sums, own, dp_size, fsdp_size)
    return (
        result[None],
        input_grad[None],
        memory_grad[None],
        small_own[GAIN:SHIFT],
        small_own[SHIFT:BIAS],
        triple_own,
        self_out_own,
        query_own,
        pair_own,
        cross_out_own,
        inner_own,
        outer_own,
        small_own[BIAS:HIDDEN_BIAS],
        small_own[HIDDEN_BIAS : HIDDEN_BIAS + steps].reshape(steps * own),
    )


def solution(mesh):
    rows = P(AXES, None, None)
    lengths = P(AXES)
    split = P(AXES, None)
    features = P(None, AXES)
    return jax.shard_map(
        local,
        mesh=mesh,
        in_specs=(rows, rows, rows, lengths, lengths, features, features)
        + (split,) * 7
        + (features, lengths),
        out_specs=(rows, rows, rows, features, features) + (split,) * 7 + (features, lengths),
        check_vma=False,
    )
```
